128 devices in a mesh: ctx: 8 (over y_lo, x), dp: 2 (over core), fsdp: 8 (over z, y_hi).
Axes of the slice: x: 4, y: 4 (y_hi: 2, y_lo: 2; y = y_hi * 2 + y_lo), z: 4, core: 2. Of those that a mesh axis runs over, the one named last changes fastest.
Arguments:
- inputs: float32 [16, 1024, 768], P(('dp', 'fsdp'), 'ctx'), may hold values from -6 to 6
- positions: int32 [16, 1024], P(('dp', 'fsdp'), 'ctx'), may hold values from 0 to 1023, as said below
- cotangent: float32 [16, 1024, 768], P(('dp', 'fsdp'), 'ctx'), may hold values from -6 to 6
- w_qkv: bfloat16 [2, 768, 2304], P(None, 'fsdp'), may hold values from -0.21875 to 0.21875
- b_qkv: bfloat16 [2, 2304], P(None, 'fsdp'), may hold values from -3 to 3
- w_out: bfloat16 [2, 768, 768], P(None, 'fsdp'), may hold values from -0.875 to 0.875
- b_out: bfloat16 [2, 768], P(None, 'fsdp'), may hold values from -1.75 to 1.75
- w_up: bfloat16 [2, 768, 3072], P(None, 'fsdp'), may hold values from -0.21875 to 0.21875
- b_up: bfloat16 [2, 3072], P(None, 'fsdp'), may hold values from -3 to 3
- w_down: bfloat16 [2, 3072, 768], P(None, 'fsdp'), may hold values from -0.109375 to 0.109375
- b_down: bfloat16 [2, 768], P(None, 'fsdp'), may hold values from -1.75 to 1.75
- ln_gain: bfloat16 [2, 768], P(None, 'fsdp'), may hold values from 0.5 to 1.5
- ln_bias: bfloat16 [2, 768], P(None, 'fsdp'), may hold values from -1.75 to 1.75
Outputs:
- outputs: float32 [16, 1024, 768], P(('dp', 'fsdp'), 'ctx')
- grad_inputs: float32 [16, 1024, 768], P(('dp', 'fsdp'), 'ctx')
- grad_w_qkv: float32 [2, 768, 2304], P(None, 'fsdp')
- grad_b_qkv: float32 [2, 2304], P(None, 'fsdp')
- grad_w_out: float32 [2, 768, 768], P(None, 'fsdp')
- grad_b_out: float32 [2, 768], P(None, 'fsdp')
- grad_w_up: float32 [2, 768, 3072], P(None, 'fsdp')
- grad_b_up: float32 [2, 3072], P(None, 'fsdp')
- grad_w_down: float32 [2, 3072, 768], P(None, 'fsdp')
- grad_b_down: float32 [2, 768], P(None, 'fsdp')
- grad_gain: float32 [2, 768], P(None, 'fsdp')
- grad_shift: float32 [2, 768], P(None, 'fsdp')
The draws below stay inside these ranges and needn't reach their ends.
Inputs may be any that keep to these rules, and one draw needn't show every extreme that they name: Each row is one sequence's positions in stored order, made of 16 blocks of 64 consecutive positions. The row's stored tokens come in consecutive pairs of blocks; the blocks of a pair are position blocks b and 15 - b, in either order; which b goes to which pair is drawn afresh for each row. Every position appears once in a row.
All inputs are finite; a program needn't handle non-finite values.
Results may differ from the reference program's by a relative error of at most 0.02.
Values may be sent and summed in bfloat16 or wider, within the bound.
A program may use at most 192 MiB of HBM per device.

```python
import jax
import jax.numpy as jnp
from jax import lax

D = 768
HEADS = 12
HEAD_DIM = 64
ROT = 16
FF = 3072
LAYERS = 2
SEQ_LEN = 1024
SEQS_ALL = 16
HALF_BLK = 64


def draw_positions(key, part):
    key = jax.random.fold_in(key, 11)
    count = SEQ_LEN // HALF_BLK
    pairs = count // 2
    perm_key, flip_key = jax.random.split(key)
    subkeys = jax.random.split(perm_key, SEQS_ALL)
    order = jax.vmap(lambda single: jax.random.permutation(single, pairs))(subkeys).astype(jnp.int32)
    flips = jax.random.randint(flip_key, (SEQS_ALL, pairs), 0, 2).astype(jnp.int32)
    first_block = jnp.where(flips == 1, count - 1 - order, order).astype(jnp.int32)
    second_block = (count - 1 - first_block).astype(jnp.int32)
    blocks = jnp.stack([first_block, second_block], axis=-1).reshape(SEQS_ALL, count)
    offsets = jnp.arange(HALF_BLK, dtype=jnp.int32)
    places = blocks[:, :, None] * HALF_BLK + offsets[None, None, :]
    return places.reshape(SEQS_ALL, SEQ_LEN).astype(jnp.int32)


def level_of(own_key, extent, shards, low, largest):
    def one(axis_at, shards_of):
        draws = jax.random.uniform(jax.random.fold_in(jax.random.fold_in(own_key, 6), axis_at), (shards_of,), jnp.float32, low / len(shards), largest / len(shards))
        return jnp.repeat(jnp.exp(draws), extent[axis_at] // shards_of).reshape((-1,) + (1,) * (len(extent) - axis_at - 1))

    factor_of = one(*shards[0])
    for cut in shards[1:]:
        factor_of = factor_of * one(*cut)
    return factor_of


def scatter_about(stream_key, dims, scale, limit, pieces=(), kind=jnp.bfloat16):
    entries = scale * jax.random.normal(stream_key, dims, jnp.float32)
    if pieces:
        entries = entries * level_of(stream_key, dims, pieces, -0.22, 0.18)
    return jnp.clip(entries, -limit, limit).astype(kind)


def setup_inputs(seed: int = 0) -> dict:
    streams_of = jax.random.split(jax.random.key(seed), 14)
    inputs = scatter_about(streams_of[0], (SEQS_ALL, SEQ_LEN, D), 1.0, 6.0, ((0, 16), (1, 8)), jnp.float32)
    positions = draw_positions(jax.random.fold_in(streams_of[13], 71), 0)
    cotangent = scatter_about(streams_of[2], (SEQS_ALL, SEQ_LEN, D), 1.0, 6.0, ((0, 16), (1, 8)), jnp.float32)
    w_qkv = scatter_about(streams_of[3], (LAYERS, D, 3 * D), D ** -0.5, 0.21875, ((1, 8),))
    b_qkv = scatter_about(streams_of[4], (LAYERS, 3 * D), 0.5, 3.0, ((1, 8),))
    w_out = scatter_about(streams_of[5], (LAYERS, D, D), (D // 16) ** -0.5, 0.875, ((1, 8),))
    b_out = scatter_about(streams_of[6], (LAYERS, D), 0.3, 1.75, ((1, 8),))
    w_up = scatter_about(streams_of[7], (LAYERS, D, FF), D ** -0.5, 0.21875, ((1, 8),))
    b_up = scatter_about(streams_of[8], (LAYERS, FF), 0.5, 3.0, ((1, 8),))
    w_down = scatter_about(streams_of[9], (LAYERS, FF, D), FF ** -0.5, 0.109375, ((1, 8),))
    b_down = scatter_about(streams_of[10], (LAYERS, D), 0.3, 1.75, ((1, 8),))
    ln_gain = jnp.clip(1.0 + 0.1 * jax.random.normal(streams_of[11], (LAYERS, D), jnp.float32), 0.5, 1.5).astype(jnp.bfloat16)
    ln_bias = scatter_about(streams_of[12], (LAYERS, D), 0.3, 1.75, ((1, 8),))
    return {"inputs": inputs, "positions": positions, "cotangent": cotangent, "w_qkv": w_qkv, "b_qkv": b_qkv, "w_out": w_out, "b_out": b_out, "w_up": w_up, "b_up": b_up, "w_down": w_down, "b_down": b_down, "ln_gain": ln_gain, "ln_bias": ln_bias}


@jax.custom_vjp
def low(v):
    return lax.optimization_barrier(v.astype(jnp.bfloat16)).astype(jnp.float32)

@jax.custom_vjp
def low_back(v):
    return v

def low_keep(v):
    return (low(v), None)

def low_pass(kept, grad):
    return (grad,)

def back_keep(v):
    return (v, None)

def back_low(kept, grad):
    return (low(grad),)
low.defvjp(low_keep, low_pass)
low_back.defvjp(back_keep, back_low)
epsilon = 1e-05
highest = lax.Precision.HIGHEST

def rotary(values, places):
    half_rot = ROT // 2
    frequency = 10000.0 ** (-2.0 * jnp.arange(half_rot, dtype=jnp.float32) / ROT)
    angles = places.astype(jnp.float32)[..., None] * frequency
    cosine = jnp.cos(angles)[..., None, :]
    sine_part = jnp.sin(angles)[..., None, :]
    first_half = values[..., :half_rot]
    second = values[..., half_rot:ROT]
    return jnp.concatenate([first_half * cosine - second * sine_part, second * cosine + first_half * sine_part, values[..., ROT:]], axis=-1)

def one_layer(stream, places, weights):
    w_qkv, b_qkv, w_out, b_out, w_up, b_up, w_down, b_down, gain_vec, shift_vec = weights
    length = stream.shape[0]
    row_mean = lax.optimization_barrier(jnp.mean(stream, axis=-1, keepdims=True))
    centred = stream - row_mean
    row_var = lax.optimization_barrier(jnp.mean(centred * centred, axis=-1, keepdims=True))
    normed = low(centred * lax.rsqrt(row_var + epsilon) * gain_vec + shift_vec)
    qkv_proj = low_back(jnp.dot(normed, w_qkv, precision=highest) + b_qkv)
    grouped = qkv_proj.reshape(length, HEADS, 3, HEAD_DIM)
    query = grouped[:, :, 0, :]
    key_part = grouped[:, :, 1, :]
    value_part = grouped[:, :, 2, :]
    query_rot = low(rotary(query, places) * HEAD_DIM ** (-0.5))
    key_rot = low(rotary(key_part, places))
    value_low = low(value_part)
    scores = low_back(jnp.einsum('qhd,khd->hqk', query_rot, key_rot, precision=highest))
    causal_mask = places[:, None] >= places[None, :]
    scores = jnp.where(causal_mask[None], scores, -jnp.inf)
    row_max = lax.optimization_barrier(jnp.max(scores, axis=-1, keepdims=True))
    expos = jnp.exp(scores - row_max)
    probs = low(expos / lax.optimization_barrier(jnp.sum(expos, axis=-1, keepdims=True)))
    attended = jnp.einsum('hqk,khd->qhd', probs, value_low, precision=highest).reshape(length, D)
    attended = low_back(low(attended))
    hidden_pre = low_back(jnp.dot(normed, w_up, precision=highest) + b_up)
    hidden_act = low(jax.nn.gelu(hidden_pre, approximate=False))
    branch = jnp.dot(attended, w_out, precision=highest) + jnp.dot(hidden_act, w_down, precision=highest)
    branch = low_back(branch + b_out + b_down)
    return stream + branch

def reference(inputs, positions, cotangent, w_qkv, b_qkv, w_out, b_out, w_up, b_up, w_down, b_down, ln_gain, ln_bias):
    params = (w_qkv.astype(jnp.float32), b_qkv.astype(jnp.float32), w_out.astype(jnp.float32), b_out.astype(jnp.float32), w_up.astype(jnp.float32), b_up.astype(jnp.float32), w_down.astype(jnp.float32), b_down.astype(jnp.float32), ln_gain.astype(jnp.float32), ln_bias.astype(jnp.float32))

    def network(stream_all, weights_all):

        def per_sequence(pair):
            stream, places = pair
            for index_layer in range(LAYERS):
                stream = one_layer(stream, places, tuple((w[index_layer] for w in weights_all)))
            return stream
        return lax.map(jax.checkpoint(per_sequence), (stream_all, positions))
    outputs, pullback = jax.vjp(network, inputs, params)
    grad_inputs, grads = pullback(cotangent)
    return (outputs, grad_inputs, grads[0], grads[1], grads[2], grads[3], grads[4], grads[5], grads[6], grads[7], grads[8], grads[9])
```

```python
import functools

import jax
import jax.numpy as jnp
from jax import lax
from jax.experimental import pallas as pl
from jax.experimental.pallas import tpu as pltpu
from jax.sharding import PartitionSpec as P

MESH = pl.DeviceIdType.MESH
HEAD_DIM = 64
ROT = 16
LAYERS = 2
D = 768
FF = 3072
N = 8
TOK = 128
SEQ = 1024
HALF = 384
epsilon = 1e-05
BF = jnp.bfloat16
F32 = jnp.float32
ANY = pl.BlockSpec(memory_space=pl.ANY)


def dot(a, b, dims):
    return lax.dot_general(a, b, (dims, ((), ())), preferred_element_type=F32)


def meet(devices):
    barrier = pltpu.get_barrier_semaphore()
    for device in devices:
        pl.semaphore_signal(barrier, inc=1, device_id=device, device_id_type=MESH)
    pl.semaphore_wait(barrier, len(devices))


def push(src, dst, send, recv, device):
    copy = pltpu.make_async_remote_copy(
        src_ref=src, dst_ref=dst, send_sem=send, recv_sem=recv, device_id=device, device_id_type=MESH
    )
    copy.start()
    return copy


def others(axis, index):
    return [{axis: lax.rem(index + d, N)} for d in range(1, N)]


class Group:
    def __init__(self, axis):
        self.axis = axis
        index = lax.axis_index(axis)
        self.r, self.h = (index % 4, index // 4) if axis == "ctx" else (index // 2, index % 2)
        self.right = {axis: self.slot(1, 0)}
        self.left = {axis: self.slot(3, 0)}
        self.pair = {axis: self.slot(0, 1)}

    def slot(self, dr, dh):
        r, h = lax.rem(self.r + dr, 4), lax.rem(self.h + dh, 2)
        return h * 4 + r if self.axis == "ctx" else r * 2 + h

    def neighbours(self):
        return [self.right, self.left, self.pair]


GATHERS = 9


def gather_steps(group, own, at, cut, rows, send, recv):
    head, tail = pl.ds(0, cut), pl.ds(cut, rows - cut)

    def go(i, src, dst, device):
        return push(src, dst, send.at[i], recv.at[i], device)

    me, twin = group.slot(0, 0), group.slot(0, 1)
    c0 = go(0, own, at(me), group.right)
    c1 = go(1, own, at(me), group.left)
    c2 = go(2, own, at(me), group.pair)
    c0.wait_recv()
    behind = at(group.slot(3, 0)).at[head]
    c3 = go(3, behind, behind, group.right)
    c1.wait_recv()
    ahead = at(group.slot(1, 0)).at[tail]
    c4 = go(4, ahead, ahead, group.left)
    c2.wait_recv()
    c5 = go(5, at(twin), at(twin), group.right)
    c6 = go(6, at(twin), at(twin), group.left)
    c5.wait_recv()
    behind = at(group.slot(3, 1)).at[head]
    c7 = go(7, behind, behind, group.right)
    c6.wait_recv()
    ahead = at(group.slot(1, 1)).at[tail]
    c8 = go(8, ahead, ahead, group.left)
    for copy in (c3, c4, c7, c8):
        copy.wait_recv()
    for copy in (c0, c1, c2, c3, c4, c5, c6, c7, c8):
        copy.wait_send()


SCATTERS = 13


def scatter_scratch(rows, cut, width):
    return [
        pltpu.VMEM((2, cut, width), BF),
        pltpu.VMEM((2, rows - cut, width), BF),
        pltpu.VMEM((2, cut, width), BF),
        pltpu.VMEM((2, rows - cut, width), BF),
        pltpu.VMEM((2, rows, width), BF),
        pltpu.VMEM((2, rows, width), BF),
        pltpu.VMEM((rows, width), BF),
        pltpu.VMEM((rows, width), BF),
    ]


def scatter_steps(group, src, cut, rows, buffers, send, recv):
    in_right, in_left, st_left, st_right, from_right, from_left, st_pair, from_pair = buffers
    head, tail = pl.ds(0, cut), pl.ds(cut, rows - cut)
    copies = []

    def go(a, b, device):
        i = len(copies)
        copy = push(a, b, send.at[i], recv.at[i], device)
        copies.append(copy)
        return copy

    hs = (1, 0)
    far = []
    for n, h in enumerate(hs):
        block = src.at[group.slot(2, h)]
        far.append(
            (
                go(block.at[head], in_right.at[n], group.left),
                go(block.at[tail], in_left.at[n], group.right),
            )
        )
    near = []
    for n, h in enumerate(hs):
        near.append(
            [
                go(src.at[group.slot(3, h)].at[tail], from_right.at[n].at[tail], group.left),
                go(src.at[group.slot(1, h)].at[head], from_left.at[n].at[head], group.right),
            ]
        )
    for n, h in enumerate(hs):
        far[n][0].wait_recv()
        st_left[n] = (src[group.slot(3, h), head].astype(F32) + in_right[n].astype(F32)).astype(BF)
        near[n].append(go(st_left.at[n], from_right.at[n].at[head], group.left))
        far[n][1].wait_recv()
        st_right[n] = (src[group.slot(1, h), tail].astype(F32) + in_left[n].astype(F32)).astype(BF)
        near[n].append(go(st_right.at[n], from_left.at[n].at[tail], group.right))
    total = None
    for n, h in enumerate(hs):
        for copy in near[n]:
            copy.wait_recv()
        total = src[group.slot(0, h)].astype(F32) + from_right[n].astype(F32) + from_left[n].astype(F32)
        if n == 0:
            st_pair[...] = total.astype(BF)
            last = go(st_pair, from_pair, group.pair)
    last.wait_recv()
    total = total + from_pair[...].astype(F32)
    for copy in copies:
        copy.wait_send()
    return total


def sems(count):
    return [pltpu.SemaphoreType.DMA((count,)), pltpu.SemaphoreType.DMA((count,))]


def params(collective_id):
    return pltpu.CompilerParams(
        collective_id=collective_id, has_side_effects=True, vmem_limit_bytes=32 * 1024 * 1024
    )


def gather_kernel(src, dst, send, recv, own):
    group = Group("ctx")
    local = pltpu.make_async_copy(src, dst.at[group.slot(0, 0)], own)
    local.start()
    meet(group.neighbours())
    gather_steps(group, src, lambda slot: dst.at[slot], TOK // 2, TOK, send, recv)
    local.wait()


def gather_ctx(block, collective_id):
    return pl.pallas_call(
        gather_kernel,
        out_shape=jax.ShapeDtypeStruct((N,) + block.shape, block.dtype),
        in_specs=[ANY],
        out_specs=ANY,
        scratch_shapes=sems(GATHERS) + [pltpu.SemaphoreType.DMA],
        compiler_params=params(collective_id),
    )(block)


def scatter_kernel(src, dst, *rest):
    *buffers, send, recv = rest
    group = Group("ctx")
    meet(group.neighbours())
    dst[...] = scatter_steps(group, src, TOK // 2, TOK, buffers, send, recv)


def scatter_ctx(parts, collective_id):
    vmem = pl.BlockSpec(memory_space=pltpu.VMEM)
    return pl.pallas_call(
        scatter_kernel,
        out_shape=jax.ShapeDtypeStruct(parts.shape[1:], F32),
        in_specs=[vmem],
        out_specs=vmem,
        scratch_shapes=scatter_scratch(TOK, TOK // 2, D) + sems(SCATTERS),
        compiler_params=params(collective_id),
    )(parts)


PIECE = 64
W_LAYER = 96 + PIECE
W_ROWS = LAYERS * W_LAYER + 16


def weights_kernel(
    src, places, cols_all, pieces_all, places_all, held, mixed, got, send, recv, send_z, recv_z, own
):
    c, f, k = lax.axis_index("ctx"), lax.axis_index("fsdp"), lax.axis_index("dp")
    group = Group("fsdp")
    cs = others("ctx", c)
    core = {"dp": 1 - k}
    first = pltpu.make_async_copy(src.at[k], held.at[f], own.at[0])
    first.start()
    mark = pltpu.make_async_copy(places, places_all.at[c], own.at[1])
    mark.start()
    meet(group.neighbours() + cs + [core])
    copies = []

    def go(a, b, device):
        i = len(copies)
        copies.append(push(a, b, send.at[i], recv.at[i], device))
        return copies[-1]

    for peer in cs:
        go(places, places_all.at[c], peer)
    gather_steps(group, src.at[k], lambda slot: held.at[slot], 176, W_ROWS, send_z, recv_z)
    first.wait()
    low = lax.broadcasted_iota(jnp.int32, (16, HALF), 0) < 8
    for i in range(N):
        for layer in range(LAYERS):
            at, to = layer * W_LAYER + 96, layer * PIECE
            own_rows = held[i, pl.ds(at, 16)].astype(F32)
            shared = held[i // 2 * 2 + c // 4, pl.ds(at, 16)].astype(F32)
            mixed[i, pl.ds(to, 16)] = jnp.where(low, own_rows, shared).astype(BF)
            mixed[i, pl.ds(to + 16, 48)] = held[i, pl.ds(at + 16, 48)]
    turn = [go(mixed.at[peer["ctx"]], got.at[c], peer) for peer in cs]
    got[c] = mixed[c]
    cross = go(held, cols_all.at[k], core)
    keep = [pltpu.make_async_copy(held, cols_all.at[k], own.at[2])]
    keep[0].start()
    for copy in turn:
        copy.wait_recv()
    keep.append(pltpu.make_async_copy(got, pieces_all.at[k], own.at[3]))
    keep[1].start()
    last = go(got, pieces_all.at[k], core)
    for copy in copies[: N - 1] + [cross, last]:
        copy.wait_recv()
    for copy in copies:
        copy.wait_send()
    for copy in keep + [mark]:
        copy.wait()


def gather_weights(src, places, collective_id):
    return pl.pallas_call(
        weights_kernel,
        out_shape=(
            jax.ShapeDtypeStruct((2, N, W_ROWS, HALF), BF),
            jax.ShapeDtypeStruct((2, N, LAYERS * PIECE, HALF), BF),
            jax.ShapeDtypeStruct((N,) + places.shape, places.dtype),
        ),
        in_specs=[ANY] * 2,
        out_specs=[ANY] * 3,
        scratch_shapes=[
            pltpu.VMEM((N, W_ROWS, HALF), BF),
            pltpu.VMEM((N, LAYERS * PIECE, HALF), BF),
            pltpu.VMEM((N, LAYERS * PIECE, HALF), BF),
        ]
        + sems(2 * (N - 1) + 2)
        + sems(GATHERS)
        + [pltpu.SemaphoreType.DMA((4,))],
        compiler_params=params(collective_id),
    )(src, places)


ROWS_A = 112
ROWS = ROWS_A + PIECE
CUT = 96


def grads_kernel(src_a, src_b, out, mine_a, mine_b, their_a, their_b, got, blocks, total, *rest):
    *buffers, send, recv, send_z, recv_z, send_x, recv_x, own = rest
    c, k = lax.axis_index("ctx"), lax.axis_index("dp")
    core = {"dp": 1 - k}
    fsdp, ctx = Group("fsdp"), Group("ctx")
    cs = others("ctx", c)
    loads = [
        pltpu.make_async_copy(src_b.at[k], mine_b, own.at[0]),
        pltpu.make_async_copy(src_a.at[k], mine_a, own.at[1]),
    ]
    for copy in loads:
        copy.start()
    meet([core] + fsdp.neighbours() + cs)
    copies = []

    def go(a, b, device):
        i = len(copies)
        copies.append(push(a, b, send.at[i], recv.at[i], device))
        return copies[-1]

    first_b = go(src_b.at[1 - k], their_b, core)
    first_a = go(src_a.at[1 - k], their_a, core)
    loads[0].wait()
    first_b.wait_recv()
    for i in range(N):
        mine_b[i] = (mine_b[i].astype(F32) + their_b[i].astype(F32)).astype(BF)
    turn = [go(mine_b.at[peer["ctx"]], got.at[c], peer) for peer in cs]
    got[c] = mine_b[c]
    loads[1].wait()
    first_a.wait_recv()
    for i in range(N):
        blocks[i, pl.ds(0, ROWS_A)] = (mine_a[i].astype(F32) + their_a[i].astype(F32)).astype(BF)
    for copy in turn:
        copy.wait_recv()
    low = lax.broadcasted_iota(jnp.int32, (16, HALF), 0) < 8
    for i in range(N):
        rows = got[i, pl.ds(0, 16)].astype(F32)
        pair = got[i + 1 - 2 * (i % 2), pl.ds(0, 16)].astype(F32)
        blocks[i, pl.ds(ROWS_A, 16)] = jnp.where(low, rows, rows + pair).astype(BF)
        blocks[i, pl.ds(ROWS_A + 16, 48)] = got[i, pl.ds(16, 48)]
    total[...] = scatter_steps(fsdp, blocks, CUT, ROWS, buffers, send_z, recv_z).astype(BF)
    keep = pltpu.make_async_copy(total, out.at[k, c], own.at[2])
    keep.start()
    gather_steps(ctx, total, lambda slot: out.at[k, slot], CUT, ROWS, send_x, recv_x)
    keep.wait()
    go(out.at[k], out.at[k], core).wait_recv()
    for copy in copies:
        copy.wait_send()


def reduce_grads(src_a, src_b, collective_id):
    return pl.pallas_call(
        grads_kernel,
        out_shape=jax.ShapeDtypeStruct((2, N, ROWS, HALF), BF),
        in_specs=[ANY] * 2,
        out_specs=ANY,
        scratch_shapes=[
            pltpu.VMEM((N, ROWS_A, HALF), BF),
            pltpu.VMEM((N, PIECE, HALF), BF),
            pltpu.VMEM((N, ROWS_A, HALF), BF),
            pltpu.VMEM((N, PIECE, HALF), BF),
            pltpu.VMEM((N, PIECE, HALF), BF),
            pltpu.VMEM((N, ROWS, HALF), BF),
            pltpu.VMEM((ROWS, HALF), BF),
        ]
        + scatter_scratch(ROWS, CUT, HALF)
        + sems(2 + N - 1 + 1)
        + sems(SCATTERS)
        + sems(GATHERS)
        + [pltpu.SemaphoreType.DMA((3,))],
        compiler_params=params(collective_id),
    )(src_a, src_b)


def rotary_tables(places):
    half_rot = ROT // 2
    frequency = 10000.0 ** (-2.0 * jnp.arange(half_rot, dtype=F32) / ROT)
    angles = places.astype(F32)[:, None] * frequency
    cosine, sine = jnp.cos(angles), jnp.sin(angles)
    count = places.shape[0]
    rest = HEAD_DIM - ROT
    own = jnp.concatenate([cosine, cosine, jnp.ones((count, rest), F32)], axis=1)
    left = jnp.concatenate([jnp.zeros_like(sine), sine, jnp.zeros((count, rest), F32)], axis=1)
    right = jnp.concatenate([-sine, jnp.zeros_like(sine), jnp.zeros((count, rest), F32)], axis=1)
    return tuple(jnp.concatenate([t, t], axis=1) for t in (own, left, right))


def rotate(values, tables):
    own, left, right = tables
    return values * own + jnp.roll(values, 8, axis=1) * left + jnp.roll(values, -8, axis=1) * right


def rotate_back(grads, tables):
    own, left, right = tables
    return grads * own + jnp.roll(grads * left, -8, axis=1) + jnp.roll(grads * right, 8, axis=1)


def norm_part(stream, gain_vec, shift_vec):
    row_mean = jnp.mean(stream, axis=-1, keepdims=True)
    centred = stream - row_mean
    row_var = jnp.mean(centred * centred, axis=-1, keepdims=True)
    return centred * lax.rsqrt(row_var + epsilon) * gain_vec + shift_vec


def gelu_exact(values):
    return jax.nn.gelu(values, approximate=False)


def units_of(pair, s):
    first, second = pair[:, :HEAD_DIM], pair[:, HEAD_DIM:]
    shared = lax.dynamic_slice_in_dim(second, s * (SEQ // 2), SEQ // 2, axis=0)
    return jnp.stack([first[: SEQ // 2], first[SEQ // 2 :], shared])


def pair_of(units, s):
    first = jnp.concatenate([units[0], units[1]], axis=0)
    second = jnp.zeros_like(first)
    second = lax.dynamic_update_slice_in_dim(second, units[2], s * (SEQ // 2), axis=0)
    return jnp.concatenate([first, second], axis=1)


def wide_of(pair):
    first, second = pair[:, :HEAD_DIM], pair[:, HEAD_DIM:]
    return jnp.stack([first, first, second])


def body(
    inputs, positions, cotangent, w_qkv, b_qkv, w_out, b_out, w_up, b_up, w_down, b_down, ln_gain, ln_bias
):
    c = lax.axis_index("ctx")
    p, s = c // 2, lax.rem(c, 2)
    head_a, head_b = 3 * p + 2 * s, 3 * p + 1

    def heads_cols(w):
        grouped = w.reshape(w.shape[:-1] + (12, 3, HEAD_DIM))
        axis = grouped.ndim - 3
        both = jnp.concatenate(
            [
                lax.dynamic_slice_in_dim(grouped, head_a, 1, axis=axis),
                lax.dynamic_slice_in_dim(grouped, head_b, 1, axis=axis),
            ],
            axis=axis,
        )
        return jnp.swapaxes(both, axis, axis + 1).reshape(w.shape[:-1] + (HALF,))

    def hidden_cols(w):
        return lax.dynamic_slice_in_dim(w, c * HALF, HALF, axis=w.ndim - 1)

    f = lax.axis_index("fsdp")
    f_s = lax.rem(f, 2)

    def piece(w, start, count):
        return lax.dynamic_slice_in_dim(w, start, count, axis=1)

    cols = jnp.concatenate([heads_cols(w_qkv), hidden_cols(w_up)], axis=-1)
    first_rows = piece(w_out, jnp.where(f_s == 0, 0, 32) + 8 * c, 8)
    shared_rows = piece(w_out, jnp.where(f_s == 0, 64, -32) + 8 * jnp.where(f_s == 0, c % 4, c), 8)
    down_rows = piece(w_down, 48 * c, 48)
    by_layer = jnp.concatenate([cols, first_rows, shared_rows, down_rows], axis=1)
    vec = jnp.concatenate([b_qkv, b_out, b_up, b_down, ln_gain, ln_bias], axis=1).reshape(-1)
    vec = jnp.pad(vec, (0, 16 * D - vec.shape[0])).reshape(16, D)
    src = jnp.concatenate([by_layer.reshape(LAYERS * W_LAYER, D), vec], axis=0)
    src = jnp.stack([src[:, :HALF], src[:, HALF:]])
    places = jnp.broadcast_to(positions, (8, TOK))
    cols_all, pieces_all, places_all = gather_weights(src, places, 1)
    cols_all = jnp.concatenate([cols_all[0], cols_all[1]], axis=-1)
    pieces_all = jnp.concatenate([pieces_all[0], pieces_all[1]], axis=-1)
    w_cat = [cols_all[:, i * W_LAYER : i * W_LAYER + 96].reshape(D, D) for i in range(LAYERS)]
    w_mix = []
    for i in range(LAYERS):
        one = pieces_all[:, i * PIECE : (i + 1) * PIECE]
        w_mix.append(
            jnp.concatenate(
                [one[:, :8].reshape(64, D), one[:, 8:16].reshape(64, D), one[:, 16:].reshape(HALF, D)], axis=0
            )
        )
    vec_all = cols_all[:, LAYERS * W_LAYER :]
    vec_all = vec_all.reshape(N, -1)[:, : LAYERS * 1056].reshape(N, LAYERS, 1056)
    vec_all = jnp.swapaxes(vec_all, 0, 1).astype(F32)
    starts = (0, 288, 384, 768, 864, 960, 1056)
    b_qkv_all, b_out_all, b_up_all, b_down_all, gain_all, shift_all = (
        vec_all[:, :, starts[i] : starts[i + 1]].reshape(LAYERS, -1) for i in range(6)
    )
    b_cat = jnp.concatenate([heads_cols(b_qkv_all), hidden_cols(b_up_all)], axis=-1)
    b_sum = b_out_all + b_down_all
    places_row = places_all[:, 0, :].reshape(SEQ)
    tables = rotary_tables(places_row)
    causal = places_row[:, None] >= places_row[None, :]
    causal_shared = lax.dynamic_slice_in_dim(causal, s * (SEQ // 2), SEQ // 2, axis=0)
    causal_units = jnp.stack([causal[: SEQ // 2], causal[SEQ // 2 :], causal_shared])

    kept = []
    stream = inputs[0]
    for layer in range(LAYERS):
        normed = norm_part(stream, gain_all[layer], shift_all[layer]).astype(BF)
        normed = gather_ctx(normed, 2 + layer).reshape(SEQ, D)
        pre = dot(normed, w_cat[layer], ((1,), (0,))) + b_cat[layer]
        query = (rotate(pre[:, :128], tables) * HEAD_DIM ** (-0.5)).astype(BF)
        key = rotate(pre[:, 128:256], tables).astype(BF)
        value = pre[:, 256:384].astype(BF)
        hidden_pre = pre[:, HALF:]
        q_units, k_units, v_units = units_of(query, s), wide_of(key), wide_of(value)
        scores = jnp.einsum("uqd,ukd->uqk", q_units, k_units, preferred_element_type=F32)
        scores = jnp.where(causal_units, scores, -jnp.inf)
        row_max = jnp.max(scores, axis=-1, keepdims=True)
        expos = jnp.exp(scores - row_max)
        probs = expos / jnp.sum(expos, axis=-1, keepdims=True)
        probs_low = probs.astype(BF)
        attended = jnp.einsum("uqk,ukd->uqd", probs_low, v_units, preferred_element_type=F32).astype(BF)
        mixed = jnp.concatenate([pair_of(attended, s), gelu_exact(hidden_pre).astype(BF)], axis=1)
        branch = dot(mixed, w_mix[layer], ((1,), (0,))).astype(BF)
        kept.append((stream, normed, q_units, k_units, v_units, probs, probs_low, hidden_pre, mixed))
        stream = stream + (scatter_ctx(branch.reshape(N, TOK, D), 4 + layer) + b_sum[layer])

    grad = cotangent[0]
    done = [None] * LAYERS
    for layer in reversed(range(LAYERS)):
        stream_in, normed, q_units, k_units, v_units, probs, probs_low, hidden_pre, mixed = kept[layer]
        own_low = grad.astype(BF)
        grad_low = gather_ctx(own_low, 6 + layer).reshape(SEQ, D)
        grad_mix = dot(mixed, grad_low, ((0,), (0,)))
        grad_cat = dot(grad_low, w_mix[layer], ((1,), (1,)))
        grad_att = units_of(grad_cat[:, :128].astype(BF), s)
        grad_hidden = jax.vjp(gelu_exact, hidden_pre)[1](grad_cat[:, 128:])[0].astype(BF)
        grad_probs = jnp.einsum("uqd,ukd->uqk", grad_att, v_units, preferred_element_type=F32)
        grad_scores = (
            probs * (grad_probs - jnp.sum(grad_probs * probs, axis=-1, keepdims=True))
        ).astype(BF)
        grad_q = jnp.einsum("uqk,ukd->uqd", grad_scores, k_units, preferred_element_type=F32)
        grad_k = jnp.einsum("uqk,uqd->ukd", grad_scores, q_units, preferred_element_type=F32)
        grad_v = jnp.einsum("uqk,uqd->ukd", probs_low, grad_att, preferred_element_type=F32)
        grad_q = rotate_back(pair_of(grad_q, s) * HEAD_DIM ** (-0.5), tables)
        grad_k = rotate_back(jnp.concatenate([grad_k[0] + grad_k[1], grad_k[2]], axis=1), tables)
        grad_v = jnp.concatenate([grad_v[0] + grad_v[1], grad_v[2]], axis=1)
        grad_pre = jnp.concatenate(
            [grad_q.astype(BF), grad_k.astype(BF), grad_v.astype(BF), grad_hidden], axis=1
        )
        grad_normed = dot(grad_pre, w_cat[layer], ((1,), (1,))).astype(BF)
        grad_normed = scatter_ctx(grad_normed.reshape(N, TOK, D), 8 + layer)
        grad_w = dot(normed, grad_pre, ((0,), (0,)))
        grad_b = jnp.sum(grad_pre.astype(F32), axis=0)
        _, norm_back = jax.vjp(norm_part, stream_in, gain_all[layer], shift_all[layer])
        grad_stream, grad_gain, grad_shift = norm_back(grad_normed)
        grad_branch = jnp.sum(own_low.astype(F32), axis=0)
        grad = grad + grad_stream

        by_head = jnp.swapaxes(grad_b[:HALF].reshape(3, 2, HEAD_DIM), 0, 1)
        all_heads = jnp.zeros((12, 3, HEAD_DIM), F32)
        all_heads = lax.dynamic_update_slice_in_dim(all_heads, by_head[:1], head_a, axis=0)
        all_heads = lax.dynamic_update_slice_in_dim(all_heads, by_head[1:], head_b, axis=0)
        hidden_rows = jnp.where(jnp.arange(N)[:, None] == c, grad_b[HALF:][None], 0.0)
        vectors = jnp.concatenate(
            [
                all_heads.reshape(N, 288),
                grad_branch.reshape(N, 96),
                hidden_rows,
                grad_gain.reshape(N, 96),
                grad_shift.reshape(N, 96),
            ],
            axis=1,
        )
        vectors = jnp.pad(vectors, ((0, 0), (0, 16 * D - 960))).reshape(N, 16, D)
        part_a = jnp.concatenate([grad_w.reshape(N, 96, D).astype(BF), vectors.astype(BF)], axis=1)
        part_b = jnp.concatenate(
            [
                grad_mix[:64].reshape(N, 8, D),
                grad_mix[64:128].reshape(N, 8, D),
                grad_mix[128:].reshape(N, 48, D),
            ],
            axis=1,
        ).astype(BF)
        part_a, part_b = (jnp.stack([t[..., :HALF], t[..., HALF:]]) for t in (part_a, part_b))
        done[layer] = reduce_grads(part_a, part_b, 10 + layer)

    outs = []
    for layer in range(LAYERS):
        got = jnp.concatenate([done[layer][0], done[layer][1]], axis=-1).astype(F32)
        qkv = got[:, :96, :HALF].reshape(4, 2, 96, 3, 2, HEAD_DIM)
        shared = qkv[:, 0, :, :, 1] + qkv[:, 1, :, :, 1]
        qkv = jnp.stack([qkv[:, 0, :, :, 0], shared, qkv[:, 1, :, :, 0]], axis=1)
        g_qkv = jnp.transpose(qkv, (2, 0, 1, 3, 4)).reshape(96, 3 * D)
        g_up = jnp.transpose(got[:, :96, HALF:], (1, 0, 2)).reshape(96, FF)
        vectors = jnp.sum(got[:, 96:98], axis=0).reshape(-1)
        b_cut = (0, 288, 384, 768, 864, 960)
        g_b_qkv, g_branch, g_b_up, g_gain, g_shift = (vectors[b_cut[i] : b_cut[i + 1]] for i in range(5))
        g_down = got[:, ROWS_A + 16 :].reshape(HALF, D)
        first = got[:, ROWS_A : ROWS_A + 8].reshape(64, D)
        shared = got[:, ROWS_A + 8 : ROWS_A + 16].reshape(64, D)
        g_out = jnp.where(
            f_s == 0,
            jnp.concatenate([first, shared[:32]], axis=0),
            jnp.concatenate([shared[32:], first], axis=0),
        )
        outs.append((g_qkv, g_b_qkv, g_out, g_branch, g_up, g_b_up, g_down, g_branch, g_gain, g_shift))
    stacked = tuple(jnp.stack([outs[i][j] for i in range(LAYERS)]) for j in range(10))
    return (stream[None], grad[None]) + stacked


def solution(mesh):
    seqs = ("dp", "fsdp")
    whole = P(None, "fsdp", None)
    row = P(None, "fsdp")
    in_specs = (
        P(seqs, "ctx", None), P(seqs, "ctx"), P(seqs, "ctx", None),
        whole, row, whole, row, whole, row, whole, row, row, row,
    )
    out_specs = (
        P(seqs, "ctx", None), P(seqs, "ctx", None),
        whole, row, whole, row, whole, row, whole, row, row, row,
    )
    return jax.shard_map(body, mesh=mesh, in_specs=in_specs, out_specs=out_specs, check_vma=False)
```

```python
import functools

import jax
import jax.numpy as jnp
from jax import lax
from jax.experimental import pallas as pl
from jax.experimental.pallas import tpu as pltpu
from jax.sharding import PartitionSpec as P

MESH = pl.DeviceIdType.MESH
HEAD_DIM = 64
ROT = 16
LAYERS = 2
D = 768
FF = 3072
N = 8
TOK = 128
SEQ = 1024
HALF = 384
epsilon = 1e-05
BF = jnp.bfloat16
F32 = jnp.float32
ANY = pl.BlockSpec(memory_space=pl.ANY)


def dot(a, b, dims):
    return lax.dot_general(a, b, (dims, ((), ())), preferred_element_type=F32)


def meet(devices):
    barrier = pltpu.get_barrier_semaphore()
    for device in devices:
        pl.semaphore_signal(barrier, inc=1, device_id=device, device_id_type=MESH)
    pl.semaphore_wait(barrier, len(devices))


def push(src, dst, send, recv, device):
    copy = pltpu.make_async_remote_copy(
        src_ref=src, dst_ref=dst, send_sem=send, recv_sem=recv, device_id=device, device_id_type=MESH
    )
    copy.start()
    return copy


def others(axis, index):
    return [{axis: lax.rem(index + d, N)} for d in range(1, N)]


class Group:
    def __init__(self, axis):
        self.axis = axis
        index = lax.axis_index(axis)
        self.r, self.h = (index % 4, index // 4) if axis == "ctx" else (index // 2, index % 2)
        self.right = {axis: self.slot(1, 0)}
        self.left = {axis: self.slot(3, 0)}
        self.pair = {axis: self.slot(0, 1)}

    def slot(self, dr, dh):
        r, h = lax.rem(self.r + dr, 4), lax.rem(self.h + dh, 2)
        return h * 4 + r if self.axis == "ctx" else r * 2 + h

    def neighbours(self):
        return [self.right, self.left, self.pair]


class Lane:
    def __init__(self, sems):
        self.send, self.recv = sems
        self.copies = []

    def go(self, src, dst, device):
        i = len(self.copies)
        self.copies.append(push(src, dst, self.send.at[i], self.recv.at[i], device))
        return self.copies[-1]

    def finish(self):
        for copy in self.copies:
            copy.wait_send()


def run(*steps):
    live = list(steps)
    while live:
        for one in list(live):
            try:
                next(one)
            except StopIteration:
                live.remove(one)


GATHERS = 8


def gather_steps(lane, group, own, at, cut, rows):
    head, tail = pl.ds(0, cut), pl.ds(cut, rows - cut)
    go = lane.go
    me, twin, far = group.slot(0, 0), group.slot(0, 1), group.slot(2, 0)
    c0 = go(own, at(me), group.right)
    c1 = go(own, at(me), group.left)
    c2 = go(own, at(me), group.pair)
    yield
    c0.wait_recv()
    behind = at(group.slot(3, 0)).at[head]
    c3 = go(behind, behind, group.right)
    yield
    c1.wait_recv()
    ahead = at(group.slot(1, 0)).at[tail]
    c4 = go(ahead, ahead, group.left)
    yield
    c2.wait_recv()
    c5 = go(at(twin), at(twin), group.right)
    c6 = go(at(twin), at(twin), group.left)
    yield
    c3.wait_recv()
    yield
    c4.wait_recv()
    c7 = go(at(far), at(far), group.pair)
    for copy in (c5, c6, c7):
        yield
        copy.wait_recv()


SCATTERS = 11


def scatter_scratch(rows, cut, width):
    return [
        pltpu.VMEM((rows, width), BF),
        pltpu.VMEM((rows, width), BF),
        pltpu.VMEM((cut, width), BF),
        pltpu.VMEM((rows - cut, width), BF),
        pltpu.VMEM((cut, width), BF),
        pltpu.VMEM((rows - cut, width), BF),
        pltpu.VMEM((2, rows, width), BF),
        pltpu.VMEM((2, rows, width), BF),
        pltpu.VMEM((rows, width), BF),
        pltpu.VMEM((rows, width), BF),
    ]


SCRATCHES = 10


def scatter_steps(lane, group, src, cut, rows, buffers, take):
    in_far, st_far, in_right, in_left, st_left, st_right, from_right, from_left, st_pair, from_pair = buffers
    head, tail = pl.ds(0, cut), pl.ds(cut, rows - cut)
    go = lane.go
    opposite = go(src.at[group.slot(2, 1)], in_far, group.pair)
    beside = [
        go(src.at[group.slot(3, 1)], from_right.at[0], group.left),
        go(src.at[group.slot(1, 1)], from_left.at[0], group.right),
    ]
    near = [
        go(src.at[group.slot(3, 0)].at[tail], from_right.at[1].at[tail], group.left),
        go(src.at[group.slot(1, 0)].at[head], from_left.at[1].at[head], group.right),
    ]
    yield
    opposite.wait_recv()
    st_far[...] = (src[group.slot(2, 0)].astype(F32) + in_far[...].astype(F32)).astype(BF)
    far_left = go(st_far.at[head], in_right, group.left)
    far_right = go(st_far.at[tail], in_left, group.right)
    for copy in beside:
        yield
        copy.wait_recv()
    total = src[group.slot(0, 1)].astype(F32) + from_right[0].astype(F32) + from_left[0].astype(F32)
    st_pair[...] = total.astype(BF)
    last = go(st_pair, from_pair, group.pair)
    yield
    far_left.wait_recv()
    st_left[...] = (src[group.slot(3, 0), head].astype(F32) + in_right[...].astype(F32)).astype(BF)
    near.append(go(st_left, from_right.at[1].at[head], group.left))
    yield
    far_right.wait_recv()
    st_right[...] = (src[group.slot(1, 0), tail].astype(F32) + in_left[...].astype(F32)).astype(BF)
    near.append(go(st_right, from_left.at[1].at[tail], group.right))
    for copy in near + [last]:
        yield
        copy.wait_recv()
    total = src[group.slot(0, 0)].astype(F32) + from_right[1].astype(F32) + from_left[1].astype(F32)
    take(total + from_pair[...].astype(F32))


def sems(count):
    return [pltpu.SemaphoreType.DMA((count,)), pltpu.SemaphoreType.DMA((count,))]


def params(collective_id):
    return pltpu.CompilerParams(
        collective_id=collective_id, has_side_effects=True, vmem_limit_bytes=32 * 1024 * 1024
    )


def normalize(stream):
    mean = jnp.mean(stream, axis=-1, keepdims=True)
    centred = stream - mean
    scale = lax.rsqrt(jnp.mean(centred * centred, axis=-1, keepdims=True) + epsilon)
    return centred * scale, scale


def norm_back(stream, grad_normed, gain):
    unit, scale = normalize(stream)
    grad_unit = grad_normed * gain
    first = jnp.mean(grad_unit, axis=-1, keepdims=True)
    second = jnp.mean(grad_unit * unit, axis=-1, keepdims=True)
    grad_gain = jnp.sum(grad_normed * unit, axis=0, keepdims=True)
    grad_shift = jnp.sum(grad_normed, axis=0, keepdims=True)
    return scale * (grad_unit - first - unit * second), grad_gain, grad_shift


PIECE = 64
ROWS = 96 + PIECE
CUT = 80
W_FIRST = ROWS + 16
W_CUT = 96
VMEM = pl.BlockSpec(memory_space=pltpu.VMEM)


def shard_scratch(rows):
    return [
        pltpu.VMEM((N, rows, HALF), BF),
        pltpu.VMEM((N, PIECE, HALF), BF),
        pltpu.VMEM((N, PIECE, HALF), BF),
    ]


SHARD_LANE = N - 1 + 3


def shard_steps(lane, lane_z, fsdp, cs, core, src, cut, rows, scratch, outs, own, kept):
    held, mixed, got = scratch
    c, k = lax.axis_index("ctx"), lax.axis_index("dp")
    first = pltpu.make_async_copy(src.at[k], held.at[fsdp.slot(0, 0)], own.at[0])
    first.start()
    yield from gather_steps(lane_z, fsdp, src.at[k], lambda slot: held.at[slot], cut, rows)
    first.wait()
    low = lax.broadcasted_iota(jnp.int32, (16, HALF), 0) < 8
    for i in range(N):
        own_rows = held[i, pl.ds(96, 16)].astype(F32)
        shared = held[i // 2 * 2 + c // 4, pl.ds(96, 16)].astype(F32)
        mixed[i, pl.ds(0, 16)] = jnp.where(low, own_rows, shared).astype(BF)
        mixed[i, pl.ds(16, 48)] = held[i, pl.ds(112, 48)]
    turn = [lane.go(mixed.at[peer["ctx"]], got.at[c], peer) for peer in cs]
    got[c] = mixed[c]
    cross = []

    def share(part, out, sem):
        cross.append(lane.go(part, out.at[k], core))
        keep = pltpu.make_async_copy(part, out.at[k], sem)
        keep.start()
        kept.append(keep)

    share(held.at[:, pl.ds(0, 96)], outs[0], own.at[1])
    if len(outs) > 2:
        share(held.at[:, pl.ds(ROWS, 16)], outs[2], own.at[2])
    for copy in turn:
        yield
        copy.wait_recv()
    share(got, outs[1], own.at[3])
    for copy in cross:
        yield
        copy.wait_recv()


COLS_SHAPE = jax.ShapeDtypeStruct((2, N, 96, HALF), BF)
PIECES_SHAPE = jax.ShapeDtypeStruct((2, N, PIECE, HALF), BF)


def weights_kernel(
    src, places, x, cot, cols_all, pieces_all, vec_all, places_all, unit_all, low_all, *rest
):
    scratch, unit, low_g, rest = rest[:3], rest[3], rest[4], rest[5:]
    lane, lane_z, lane_m, lane_u, lane_g = (Lane(rest[2 * i : 2 * i + 2]) for i in range(5))
    own, keeps = rest[10], rest[11]
    c = lax.axis_index("ctx")
    fsdp, ctx = Group("fsdp"), Group("ctx")
    cs = others("ctx", c)
    core = {"dp": 1 - lax.axis_index("dp")}
    mark = pltpu.make_async_copy(places, places_all.at[c], keeps.at[0])
    mark.start()
    meet(fsdp.neighbours() + cs + [core])
    kept = [mark]
    marks = [lane_m.go(places, places_all.at[c], peer) for peer in cs]

    def tokens():
        unit[...] = normalize(x[...])[0].astype(BF)
        low_g[...] = cot[...].astype(BF)
        keep = pltpu.make_async_copy(unit, unit_all.at[c], keeps.at[1])
        keep.start()
        kept.append(keep)
        yield from gather_steps(lane_u, ctx, unit, lambda slot: unit_all.at[slot], TOK // 2, TOK)
        keep = pltpu.make_async_copy(low_g, low_all.at[c], keeps.at[2])
        keep.start()
        kept.append(keep)
        yield from gather_steps(lane_g, ctx, low_g, lambda slot: low_all.at[slot], TOK // 2, TOK)

    outs = (cols_all, pieces_all, vec_all)
    run(
        shard_steps(lane, lane_z, fsdp, cs, core, src, W_CUT, W_FIRST, scratch, outs, own, kept),
        tokens(),
    )
    for copy in marks:
        copy.wait_recv()
    for each in (lane, lane_z, lane_m, lane_u, lane_g):
        each.finish()
    for copy in kept:
        copy.wait()


def gather_weights(src, places, x, cot, collective_id):
    tokens = jax.ShapeDtypeStruct((N, TOK, D), BF)
    return pl.pallas_call(
        weights_kernel,
        out_shape=(
            COLS_SHAPE,
            PIECES_SHAPE,
            jax.ShapeDtypeStruct((2, N, 16, HALF), BF),
            jax.ShapeDtypeStruct((N,) + places.shape, places.dtype),
            tokens,
            tokens,
        ),
        in_specs=[ANY] * 2 + [VMEM] * 2,
        out_specs=[ANY] * 6,
        scratch_shapes=shard_scratch(W_FIRST)
        + [pltpu.VMEM((TOK, D), BF), pltpu.VMEM((TOK, D), BF)]
        + sems(SHARD_LANE)
        + sems(GATHERS)
        + sems(N - 1)
        + sems(GATHERS)
        + sems(GATHERS)
        + [pltpu.SemaphoreType.DMA((4,)), pltpu.SemaphoreType.DMA((3,))],
        compiler_params=params(collective_id),
    )(src, places, x, cot)


def between_kernel(parts, x, bias, src, x_next, unit_all, cols_all, pieces_all, *rest):
    scratch, unit, rest = rest[:3], rest[3], rest[4:]
    buffers, rest = rest[:SCRATCHES], rest[SCRATCHES:]
    lane, lane_u, lane_w, lane_z = (Lane(rest[2 * i : 2 * i + 2]) for i in range(4))
    own, keeps = rest[8], rest[9]
    ctx, fsdp = Group("ctx"), Group("fsdp")
    cs = others("ctx", lax.axis_index("ctx"))
    core = {"dp": 1 - lax.axis_index("dp")}
    meet(fsdp.neighbours() + cs + [core])
    kept = []

    def tokens():
        def take(total):
            x_next[...] = x[...] + (total + bias[...])

        yield from scatter_steps(lane, ctx, parts, TOK // 2, TOK, buffers, take)
        unit[...] = normalize(x_next[...])[0].astype(BF)
        keep = pltpu.make_async_copy(unit, unit_all.at[ctx.slot(0, 0)], keeps)
        keep.start()
        kept.append(keep)
        yield from gather_steps(lane_u, ctx, unit, lambda slot: unit_all.at[slot], TOK // 2, TOK)

    outs = (cols_all, pieces_all)
    run(
        tokens(),
        shard_steps(lane_w, lane_z, fsdp, cs, core, src, CUT, ROWS, scratch, outs, own, kept),
    )
    for each in (lane, lane_u, lane_w, lane_z):
        each.finish()
    for copy in kept:
        copy.wait()


def between(parts, x, bias, src, collective_id):
    return pl.pallas_call(
        between_kernel,
        out_shape=(
            jax.ShapeDtypeStruct((TOK, D), F32),
            jax.ShapeDtypeStruct((N, TOK, D), BF),
            COLS_SHAPE,
            PIECES_SHAPE,
        ),
        in_specs=[VMEM] * 3 + [ANY],
        out_specs=(VMEM, ANY, ANY, ANY),
        scratch_shapes=shard_scratch(ROWS)
        + [pltpu.VMEM((TOK, D), BF)]
        + scatter_scratch(TOK, TOK // 2, D)
        + sems(SCATTERS)
        + sems(GATHERS)
        + sems(SHARD_LANE)
        + sems(GATHERS)
        + [pltpu.SemaphoreType.DMA((4,)), pltpu.SemaphoreType.DMA],
        compiler_params=params(collective_id),
    )(parts, x, bias, src)


def grads_scratch():
    return [
        pltpu.VMEM((N, 96, HALF), BF),
        pltpu.VMEM((N, PIECE, HALF), BF),
        pltpu.VMEM((N, 96, HALF), BF),
        pltpu.VMEM((N, PIECE, HALF), BF),
        pltpu.VMEM((N, PIECE, HALF), BF),
        pltpu.VMEM((N, ROWS, HALF), BF),
    ] + scatter_scratch(ROWS, CUT, HALF)


GRADS = 6 + SCRATCHES


def grads_steps(lane, lane_z, fsdp, cs, core, src_a, src_b, scratch, own, take):
    mine_a, mine_b, their_a, their_b, got, blocks = scratch[:6]
    c, k = lax.axis_index("ctx"), lax.axis_index("dp")
    loads = [
        pltpu.make_async_copy(src_b.at[k], mine_b, own.at[0]),
        pltpu.make_async_copy(src_a.at[k], mine_a, own.at[1]),
    ]
    for copy in loads:
        copy.start()
    first_b = lane.go(src_b.at[1 - k], their_b, core)
    first_a = lane.go(src_a.at[1 - k], their_a, core)
    yield
    loads[0].wait()
    first_b.wait_recv()
    for i in range(N):
        mine_b[i] = (mine_b[i].astype(F32) + their_b[i].astype(F32)).astype(BF)
    turn = [lane.go(mine_b.at[peer["ctx"]], got.at[c], peer) for peer in cs]
    got[c] = mine_b[c]
    yield
    loads[1].wait()
    first_a.wait_recv()
    for i in range(N):
        blocks[i, pl.ds(0, 96)] = (mine_a[i].astype(F32) + their_a[i].astype(F32)).astype(BF)
    for copy in turn:
        yield
        copy.wait_recv()
    low = lax.broadcasted_iota(jnp.int32, (16, HALF), 0) < 8
    for i in range(N):
        rows = got[i, pl.ds(0, 16)].astype(F32)
        pair = got[i + 1 - 2 * (i % 2), pl.ds(0, 16)].astype(F32)
        blocks[i, pl.ds(96, 16)] = jnp.where(low, rows, rows + pair).astype(BF)
        blocks[i, pl.ds(112, 48)] = got[i, pl.ds(16, 48)]
    yield from scatter_steps(lane_z, fsdp, blocks, CUT, ROWS, scratch[6:], take)


def turn_kernel(
    parts, x, grad, gain, src_a, src_b, grad_next, low_all, vecs, share, low_g, *rest
):
    buffers, rest = rest[:SCRATCHES], rest[SCRATCHES:]
    scratch, rest = rest[:GRADS], rest[GRADS:]
    lane, lane_g, lane_w, lane_z = (Lane(rest[2 * i : 2 * i + 2]) for i in range(4))
    own, keep_sem = rest[8], rest[9]
    ctx, fsdp = Group("ctx"), Group("fsdp")
    cs = others("ctx", lax.axis_index("ctx"))
    core = {"dp": 1 - lax.axis_index("dp")}
    meet(cs + fsdp.neighbours() + [core])
    kept = []

    def tokens():
        def take(total):
            back, grad_gain, grad_shift = norm_back(x[...], total, gain[...])
            grad_next[...] = grad[...] + back
            rounded = grad[...].astype(BF).astype(F32)
            vecs[pl.ds(0, 1)] = jnp.sum(rounded, axis=0, keepdims=True)
            vecs[pl.ds(1, 1)] = grad_gain
            vecs[pl.ds(2, 1)] = grad_shift
            vecs[pl.ds(3, 5)] = jnp.zeros((5, D), F32)

        yield from scatter_steps(lane, ctx, parts, TOK // 2, TOK, buffers, take)
        low_g[...] = grad_next[...].astype(BF)
        keep = pltpu.make_async_copy(low_g, low_all.at[ctx.slot(0, 0)], keep_sem)
        keep.start()
        kept.append(keep)
        yield from gather_steps(lane_g, ctx, low_g, lambda slot: low_all.at[slot], TOK // 2, TOK)

    def weights():
        def take(total):
            share[...] = total.astype(BF)

        yield from grads_steps(lane_w, lane_z, fsdp, cs, core, src_a, src_b, scratch, own, take)

    run(tokens(), weights())
    for each in (lane, lane_g, lane_w, lane_z):
        each.finish()
    for copy in kept:
        copy.wait()


def turn(parts, x, grad, gain, src_a, src_b, collective_id):
    return pl.pallas_call(
        turn_kernel,
        out_shape=(
            jax.ShapeDtypeStruct((TOK, D), F32),
            jax.ShapeDtypeStruct((N, TOK, D), BF),
            jax.ShapeDtypeStruct((8, D), F32),
            jax.ShapeDtypeStruct((ROWS, HALF), BF),
        ),
        in_specs=[VMEM] * 4 + [ANY] * 2,
        out_specs=(VMEM, ANY, VMEM, VMEM),
        scratch_shapes=[pltpu.VMEM((TOK, D), BF)]
        + scatter_scratch(TOK, TOK // 2, D)
        + grads_scratch()
        + sems(SCATTERS)
        + sems(GATHERS)
        + sems(2 + N - 1)
        + sems(SCATTERS)
        + [pltpu.SemaphoreType.DMA((2,)), pltpu.SemaphoreType.DMA],
        compiler_params=params(collective_id),
    )(parts, x, grad, gain, src_a, src_b)


ALL_ROWS = LAYERS * ROWS + 16


def last_kernel(
    parts, x, grad, gain, out_parts, x_last, bias, src_a, src_b, vecs, share,
    grad_next, outputs, out, both, v_mine, v_their, v_all, *rest,
):
    buffers, rest = rest[:SCRATCHES], rest[SCRATCHES:]
    buffers_o, rest = rest[:SCRATCHES], rest[SCRATCHES:]
    scratch, rest = rest[:GRADS], rest[GRADS:]
    lane, lane_o, lane_w, lane_z, lane_v, lane_x = (Lane(rest[2 * i : 2 * i + 2]) for i in range(6))
    own, keep_sem = rest[12], rest[13]
    c, f, k = lax.axis_index("ctx"), lax.axis_index("fsdp"), lax.axis_index("dp")
    ctx, fsdp = Group("ctx"), Group("fsdp")
    cs, fs = others("ctx", c), others("fsdp", f)
    core = {"dp": 1 - k}
    meet(cs + fs + [core])
    kept = []

    def tokens():
        def take(total):
            back, grad_gain, grad_shift = norm_back(x[...], total, gain[...])
            grad_next[...] = grad[...] + back
            rounded = grad[...].astype(BF).astype(F32)
            branch = jnp.sum(rounded, axis=0, keepdims=True)
            mine = jnp.concatenate([vecs[...], branch, grad_gain, grad_shift, jnp.zeros((5, D), F32)], axis=0)
            v_mine[0] = mine[:, :HALF].astype(BF)
            v_mine[1] = mine[:, HALF:].astype(BF)

        yield from scatter_steps(lane, ctx, parts, TOK // 2, TOK, buffers, take)
        cross = lane_v.go(v_mine.at[1 - k], v_their, core)
        yield
        cross.wait_recv()
        v_all[f] = (v_mine[k].astype(F32) + v_their[...].astype(F32)).astype(BF)
        copies = [lane_v.go(v_all.at[f], v_all.at[f], peer) for peer in fs]
        for copy in copies:
            yield
            copy.wait_recv()
        total = v_all[0].astype(F32)
        for i in range(1, N):
            total = total + v_all[i].astype(F32)
        both[pl.ds(LAYERS * ROWS, 16)] = total.astype(BF)

    def weights():
        def take(total):
            both[pl.ds(0, ROWS)] = total.astype(BF)

        both[pl.ds(ROWS, ROWS)] = share[...]
        yield from grads_steps(lane_w, lane_z, fsdp, cs, core, src_a, src_b, scratch, own, take)

    def ends():
        def take(total):
            outputs[...] = x_last[...] + (total + bias[...])

        yield from scatter_steps(lane_o, ctx, out_parts, TOK // 2, TOK, buffers_o, take)

    run(tokens(), weights(), ends())
    keep = pltpu.make_async_copy(both, out.at[k, c], keep_sem)
    keep.start()
    run(gather_steps(lane_x, ctx, both, lambda slot: out.at[k, slot], 176, ALL_ROWS))
    keep.wait()
    lane_x.go(out.at[k], out.at[k], core).wait_recv()
    for each in (lane, lane_o, lane_w, lane_z, lane_v, lane_x):
        each.finish()


def last(parts, x, grad, gain, out_parts, x_last, bias, src_a, src_b, vecs, share, collective_id):
    tokens = jax.ShapeDtypeStruct((TOK, D), F32)
    return pl.pallas_call(
        last_kernel,
        out_shape=(tokens, tokens, jax.ShapeDtypeStruct((2, N, ALL_ROWS, HALF), BF)),
        in_specs=[VMEM] * 7 + [ANY] * 2 + [VMEM] * 2,
        out_specs=(VMEM, VMEM, ANY),
        scratch_shapes=[
            pltpu.VMEM((ALL_ROWS, HALF), BF),
            pltpu.VMEM((2, 16, HALF), BF),
            pltpu.VMEM((16, HALF), BF),
            pltpu.VMEM((N, 16, HALF), BF),
        ]
        + scatter_scratch(TOK, TOK // 2, D)
        + scatter_scratch(TOK, TOK // 2, D)
        + grads_scratch()
        + sems(SCATTERS)
        + sems(SCATTERS)
        + sems(2 + N - 1)
        + sems(SCATTERS)
        + sems(N)
        + sems(GATHERS + 1)
        + [pltpu.SemaphoreType.DMA((2,)), pltpu.SemaphoreType.DMA],
        compiler_params=params(collective_id),
    )(parts, x, grad, gain, out_parts, x_last, bias, src_a, src_b, vecs, share)


def marks_of(places):
    frequency = 10000.0 ** (-2.0 * jnp.arange(ROT // 2, dtype=F32) / ROT)
    where = places.astype(F32).reshape(1, -1)
    angles = frequency[:, None] * where
    return jnp.concatenate([jnp.cos(angles), jnp.sin(angles), jnp.broadcast_to(where, angles.shape)], axis=0)


def tables_kernel(marks, tables, col):
    zero = jnp.zeros((8, TOK), F32)
    one = zero + 1.0
    for i in range(N):
        cosine, sine, where = marks[i, 0:8], marks[i, 8:16], marks[i, 16:24]
        rows = pl.ds(i * TOK, TOK)
        own = [cosine, cosine] + [one] * 6
        left = [zero, sine] + [zero] * 6
        right = [-sine, zero] + [zero] * 6
        for t, tiles in enumerate((own, left, right)):
            tables[t, rows] = jnp.concatenate(tiles + tiles, axis=0).T
        col[rows] = jnp.concatenate([where] * 16, axis=0).T


def rotary_tables(marks):
    return pl.pallas_call(
        tables_kernel,
        out_shape=(jax.ShapeDtypeStruct((3, SEQ, 128), F32), jax.ShapeDtypeStruct((SEQ, 128), F32)),
        in_specs=[VMEM],
        out_specs=[VMEM] * 2,
        compiler_params=pltpu.CompilerParams(vmem_limit_bytes=48 * 1024 * 1024),
    )(marks)


BLOCK = 256
BLOCKS = SEQ // BLOCK


def unit_rows(b):
    s = lax.axis_index("ctx") % 2
    start = jnp.where(b < BLOCKS, b * BLOCK, s * (SEQ // 2) + (b - BLOCKS) * BLOCK)
    start = pl.multiple_of(start, BLOCK)
    lanes = lax.broadcasted_iota(jnp.int32, (BLOCK, 2 * HEAD_DIM), 1) // HEAD_DIM
    return start, lanes == jnp.where(b < BLOCKS, 0, 1)


def forward_kernel(
    unit, gain, shift, w_cat, w_mix, b_cat, col, row, tables,
    branch, normed, query, key, value, slope, mixed, lse, turned,
):
    @pl.loop(0, BLOCKS)
    def _(i):
        rows = pl.ds(pl.multiple_of(i * BLOCK, BLOCK), BLOCK)
        low = (unit[rows].astype(F32) * gain[...] + shift[...]).astype(BF)
        normed[rows] = low
        heads = dot(low, w_cat[0], ((1,), (0,))) + b_cat[:, :HALF]

        def rotate(values):
            return (
                values * tables[0, rows]
                + pltpu.roll(values, 8, axis=1) * tables[1, rows]
                + pltpu.roll(values, 120, axis=1) * tables[2, rows]
            )

        query[rows] = (rotate(heads[:, :128]) * HEAD_DIM ** (-0.5)).astype(BF)
        key[rows] = rotate(heads[:, 128:256]).astype(BF)
        value[rows] = heads[:, 256:].astype(BF)
        pre = dot(low, w_cat[1], ((1,), (0,))) + b_cat[:, HALF:]
        cdf = 0.5 * (1.0 + lax.erf(pre * 0.5**0.5))
        mixed[rows, pl.ds(128, HALF)] = (pre * cdf).astype(BF)
        mixed[rows, pl.ds(0, 128)] = jnp.zeros((BLOCK, 128), BF)
        slope[rows] = cdf + pre * (jnp.exp(-0.5 * pre * pre) * 0.3989422804014327)

    turned[...] = value[...].astype(F32).T.astype(BF)

    @pl.loop(0, BLOCKS + 2)
    def _(b):
        start, mask = unit_rows(b)
        rows = pl.ds(start, BLOCK)
        q = jnp.where(mask, query[rows].astype(F32), 0.0).astype(BF)
        scores = dot(key[...], q, ((1,), (1,)))
        seen = jnp.concatenate([col[...], col[...]], axis=1) <= row[pl.ds(start // BLOCK, 1)]
        scores = jnp.where(seen, scores, -jnp.inf)
        top = jnp.max(scores, axis=0, keepdims=True)
        expos = jnp.exp(scores - top)
        total = jnp.sum(expos, axis=0, keepdims=True)
        lse[pl.ds(b, 1)] = top + jnp.log(total)
        probs = (expos * (1.0 / total)).astype(BF)
        out = dot(turned[...], probs, ((1,), (0,))).T
        mixed[rows, pl.ds(0, 128)] = jnp.where(mask, out, mixed[rows, pl.ds(0, 128)].astype(F32)).astype(BF)

    @pl.loop(0, BLOCKS)
    def _(i):
        rows = pl.ds(pl.multiple_of(i * BLOCK, BLOCK), BLOCK)
        branch[rows] = dot(mixed[rows], w_mix[...], ((1,), (0,))).astype(BF)


def local_params():
    return pltpu.CompilerParams(vmem_limit_bytes=48 * 1024 * 1024)


def forward(unit, gain, shift, w_cat, w_mix, b_cat, col, row, tables):
    shape = jax.ShapeDtypeStruct
    return pl.pallas_call(
        forward_kernel,
        out_shape=(
            shape((SEQ, D), BF),
            shape((SEQ, D), BF),
            shape((SEQ, 128), BF),
            shape((SEQ, 128), BF),
            shape((SEQ, 128), BF),
            shape((SEQ, HALF), F32),
            shape((SEQ, 512), BF),
            shape((8, BLOCK), F32),
        ),
        in_specs=[VMEM] * 9,
        out_specs=[VMEM] * 8,
        scratch_shapes=[pltpu.VMEM((128, SEQ), BF)],
        compiler_params=local_params(),
    )(unit, gain, shift, w_cat, w_mix, b_cat, col, row, tables)


def backward_kernel(
    low, w_mix, w_cat, normed, query, key, value, slope, mixed, lse, col, row, tables,
    grad_normed, part_a, part_b, grad_b,
    grad_att, grad_pre, dq, dk, dv, turned, big,
):
    @pl.loop(0, BLOCKS)
    def _(i):
        rows = pl.ds(pl.multiple_of(i * BLOCK, BLOCK), BLOCK)
        back = dot(low[rows], w_mix[...], ((1,), (1,)))
        grad_att[rows] = back[:, :128].astype(BF)
        grad_pre[rows, pl.ds(HALF, HALF)] = (back[:, 128:] * slope[rows]).astype(BF)

    turned[...] = key[...].astype(F32).T.astype(BF)
    dq[...] = jnp.zeros((SEQ, 128), F32)
    dk[...] = jnp.zeros((SEQ, 128), F32)
    dv[...] = jnp.zeros((SEQ, 128), F32)

    @pl.loop(0, BLOCKS + 2)
    def _(b):
        start, mask = unit_rows(b)
        rows = pl.ds(start, BLOCK)
        q = jnp.where(mask, query[rows].astype(F32), 0.0).astype(BF)
        g = jnp.where(mask, grad_att[rows].astype(F32), 0.0).astype(BF)
        scores = dot(key[...], q, ((1,), (1,)))
        seen = jnp.concatenate([col[...], col[...]], axis=1) <= row[pl.ds(start // BLOCK, 1)]
        probs = jnp.exp(jnp.where(seen, scores, -jnp.inf) - lse[pl.ds(b, 1)])
        grad_probs = dot(value[...], g, ((1,), (1,)))
        mean = jnp.sum(probs * grad_probs, axis=0, keepdims=True)
        grad_scores = (probs * (grad_probs - mean)).astype(BF)
        dq[rows] = jnp.where(mask, dot(turned[...], grad_scores, ((1,), (0,))).T, dq[rows])
        dk[...] += dot(grad_scores, q, ((1,), (0,)))
        dv[...] += dot(probs.astype(BF), g, ((1,), (0,)))

    grad_b[...] = jnp.zeros((1, D), F32)

    @pl.loop(0, BLOCKS)
    def _(i):
        rows = pl.ds(pl.multiple_of(i * BLOCK, BLOCK), BLOCK)

        def rotate_back(grads):
            return (
                grads * tables[0, rows]
                + pltpu.roll(grads * tables[1, rows], 120, axis=1)
                + pltpu.roll(grads * tables[2, rows], 8, axis=1)
            )

        grad_pre[rows, pl.ds(0, 128)] = rotate_back(dq[rows] * HEAD_DIM ** (-0.5)).astype(BF)
        grad_pre[rows, pl.ds(128, 128)] = rotate_back(dk[rows]).astype(BF)
        grad_pre[rows, pl.ds(256, 128)] = dv[rows].astype(BF)
        block = grad_pre[rows]
        grad_b[...] += jnp.sum(block.astype(F32), axis=0, keepdims=True)
        grad_normed[rows] = (
            dot(block[:, :HALF], w_cat[0], ((1,), (1,))) + dot(block[:, HALF:], w_cat[1], ((1,), (1,)))
        ).astype(BF)

    @pl.loop(0, D // BLOCK)
    def _(i):
        cols = pl.ds(pl.multiple_of(i * BLOCK, BLOCK), BLOCK)
        big[cols] = dot(normed[:, cols], grad_pre[...], ((0,), (0,)))

    for f in range(N):
        for h in range(2):
            part_a[h, f] = big[96 * f : 96 * f + 96, HALF * h : HALF * h + HALF].astype(BF)

    @pl.loop(0, 2)
    def _(i):
        cols = pl.ds(pl.multiple_of(i * BLOCK, BLOCK), BLOCK)
        big[cols] = dot(mixed[:, cols], low[...], ((0,), (0,)))

    for j in range(N):
        for h in range(2):
            at = slice(HALF * h, HALF * h + HALF)
            first = big[8 * j : 8 * j + 8, at]
            second = big[64 + 8 * j : 64 + 8 * j + 8, at]
            part_b[h, j, pl.ds(0, 16)] = jnp.concatenate([first, second], axis=0).astype(BF)
            part_b[h, j, pl.ds(16, 48)] = big[128 + 48 * j : 176 + 48 * j, at].astype(BF)


def backward(low, w_mix, w_cat, normed, query, key, value, slope, mixed, lse, col, row, tables):
    shape = jax.ShapeDtypeStruct
    return pl.pallas_call(
        backward_kernel,
        out_shape=(
            shape((SEQ, D), BF),
            shape((2, N, 96, HALF), BF),
            shape((2, N, PIECE, HALF), BF),
            shape((1, D), F32),
        ),
        in_specs=[VMEM] * 13,
        out_specs=[VMEM] * 4,
        scratch_shapes=[
            pltpu.VMEM((SEQ, 128), BF),
            pltpu.VMEM((SEQ, D), BF),
            pltpu.VMEM((SEQ, 128), F32),
            pltpu.VMEM((SEQ, 128), F32),
            pltpu.VMEM((SEQ, 128), F32),
            pltpu.VMEM((128, SEQ), BF),
            pltpu.VMEM((D, D), F32),
        ],
        compiler_params=local_params(),
    )(low, w_mix, w_cat, normed, query, key, value, slope, mixed, lse, col, row, tables)


def spread_kernel(got, g_qkv, g_out, g_up, g_down):
    odd = lax.axis_index("fsdp") % 2
    for layer in range(LAYERS):
        base = layer * ROWS

        def heads(i):
            return got[0, i, pl.ds(base, 96)].astype(F32)

        chunks = []
        for p in range(4):
            one, two = heads(2 * p), heads(2 * p + 1)
            both = one + two
            for values, lane in ((one, 0), (both, HEAD_DIM), (two, 0)):
                chunks += [values[:, 128 * i + lane : 128 * i + lane + HEAD_DIM] for i in range(3)]
        for i in range(len(chunks) // 2):
            g_qkv[layer, :, pl.ds(128 * i, 128)] = jnp.concatenate(chunks[2 * i : 2 * i + 2], axis=1)
        for i in range(N):
            g_up[layer, :, pl.ds(HALF * i, HALF)] = got[1, i, pl.ds(base, 96)].astype(F32)
            for h in range(2):
                cols = pl.ds(HALF * h, HALF)
                g_down[layer, pl.ds(48 * i, 48), cols] = got[h, i, pl.ds(base + 112, 48)].astype(F32)
        for h in range(2):
            cols = pl.ds(HALF * h, HALF)
            rows = [got[h, i, pl.ds(base + 96, 16)].astype(F32) for i in range(N)]
            first = [r[:8] for r in rows]
            even = jnp.concatenate(first + [r[8:] for r in rows[:4]], axis=0)
            uneven = jnp.concatenate([r[8:] for r in rows[4:]] + first, axis=0)
            g_out[layer, :, cols] = jnp.where(odd == 0, even, uneven)


def spread(got):
    shape = jax.ShapeDtypeStruct
    return pl.pallas_call(
        spread_kernel,
        out_shape=(
            shape((LAYERS, 96, 3 * D), F32),
            shape((LAYERS, 96, D), F32),
            shape((LAYERS, 96, FF), F32),
            shape((LAYERS, HALF, D), F32),
        ),
        in_specs=[VMEM],
        out_specs=[VMEM] * 4,
        compiler_params=local_params(),
    )(got)


def body(
    inputs, positions, cotangent, w_qkv, b_qkv, w_out, b_out, w_up, b_up, w_down, b_down, ln_gain, ln_bias
):
    c = lax.axis_index("ctx")
    p, s = c // 2, lax.rem(c, 2)
    head_a, head_b = 3 * p + 2 * s, 3 * p + 1

    def heads_cols(w):
        grouped = w.reshape(w.shape[:-1] + (12, 3, HEAD_DIM))
        axis = grouped.ndim - 3
        both = jnp.concatenate(
            [
                lax.dynamic_slice_in_dim(grouped, head_a, 1, axis=axis),
                lax.dynamic_slice_in_dim(grouped, head_b, 1, axis=axis),
            ],
            axis=axis,
        )
        return jnp.swapaxes(both, axis, axis + 1).reshape(w.shape[:-1] + (HALF,))

    def hidden_cols(w):
        return lax.dynamic_slice_in_dim(w, c * HALF, HALF, axis=w.ndim - 1)

    f = lax.axis_index("fsdp")
    f_s = lax.rem(f, 2)

    def piece(w, start, count):
        return lax.dynamic_slice_in_dim(w, start, count, axis=1)

    cols = jnp.concatenate([heads_cols(w_qkv), hidden_cols(w_up)], axis=-1)
    first_rows = piece(w_out, jnp.where(f_s == 0, 0, 32) + 8 * c, 8)
    shared_rows = piece(w_out, jnp.where(f_s == 0, 64, -32) + 8 * jnp.where(f_s == 0, c % 4, c), 8)
    down_rows = piece(w_down, 48 * c, 48)
    by_layer = jnp.concatenate([cols, first_rows, shared_rows, down_rows], axis=1)
    vec = jnp.concatenate([b_qkv, b_out, b_up, b_down, ln_gain, ln_bias], axis=1).reshape(-1)
    vec = jnp.pad(vec, (0, 16 * D - vec.shape[0])).reshape(16, D)
    stream, cot = inputs[0], cotangent[0]
    src = [jnp.concatenate([by_layer[0], vec], axis=0), by_layer[1]]
    src = [jnp.stack([one[:, :HALF], one[:, HALF:]]) for one in src]
    cols, pieces, vec_all, marks, unit, low_last = gather_weights(
        src[0], marks_of(positions), stream, cot, 1
    )

    def mix_of(pieces):
        one = jnp.concatenate([pieces[0], pieces[1]], axis=-1)
        return jnp.concatenate(
            [one[:, :8].reshape(64, D), one[:, 8:16].reshape(64, D), one[:, 16:].reshape(HALF, D)], axis=0
        )

    w_cat, w_mix = [cols.reshape(2, D, HALF)], [mix_of(pieces)]
    vec_all = jnp.concatenate([vec_all[0], vec_all[1]], axis=-1)
    vec_all = vec_all.reshape(N, -1)[:, : LAYERS * 1056].reshape(N, LAYERS, 1056)
    vec_all = jnp.swapaxes(vec_all, 0, 1).astype(F32)
    starts = (0, 288, 384, 768, 864, 960, 1056)
    b_qkv_all, b_out_all, b_up_all, b_down_all, gain_all, shift_all = (
        vec_all[:, :, starts[i] : starts[i + 1]].reshape(LAYERS, -1) for i in range(6)
    )
    b_cat = jnp.concatenate([heads_cols(b_qkv_all), hidden_cols(b_up_all)], axis=-1)
    b_sum = b_out_all + b_down_all
    tables, col = rotary_tables(marks)
    row = marks[:, 16].reshape(BLOCKS, BLOCK)

    def ahead(layer, unit):
        return forward(
            unit.reshape(SEQ, D), gain_all[layer][None], shift_all[layer][None], w_cat[layer], w_mix[layer],
            b_cat[layer][None], col, row, tables,
        )

    def back(layer, low, kept):
        return backward(low.reshape(SEQ, D), w_mix[layer], w_cat[layer], *kept, col, row, tables)

    branch, *kept_first = ahead(0, unit)
    x_last, unit, cols, pieces = between(branch.reshape(N, TOK, D), stream, b_sum[0][None], src[1], 2)
    w_cat.append(cols.reshape(2, D, HALF))
    w_mix.append(mix_of(pieces))
    branch, *kept_last = ahead(1, unit)
    grad_normed, part_a, part_b, grad_b_last = back(1, low_last, kept_last)
    grad, low, vecs, share = turn(
        grad_normed.reshape(N, TOK, D), x_last, cot, gain_all[1][None], part_a, part_b, 3
    )
    grad_normed, part_a, part_b, grad_b_first = back(0, low, kept_first)
    vecs = jnp.concatenate([vecs[:3], grad_b_last, grad_b_first, jnp.zeros((3, D), F32)], axis=0)
    grad, outputs, got = last(
        grad_normed.reshape(N, TOK, D), stream, grad, gain_all[0][None], branch.reshape(N, TOK, D), x_last,
        b_sum[1][None], part_a, part_b, vecs, share, 4,
    )
    g_qkv, g_out, g_up, g_down = spread(got)

    rows = jnp.concatenate([got[0, :, LAYERS * ROWS :], got[1, :, LAYERS * ROWS :]], axis=-1).astype(F32)
    summed = jnp.sum(rows, axis=0)

    def cut(vector, width):
        return lax.dynamic_slice_in_dim(vector, f * width, width, axis=vector.ndim - 1)

    def own_vectors(biases):
        qkv = biases[:, :HALF].reshape(4, 2, 3, 2, HEAD_DIM)
        shared = qkv[:, 0, :, 1] + qkv[:, 1, :, 1]
        qkv = jnp.stack([qkv[:, 0, :, 0], shared, qkv[:, 1, :, 0]], axis=1).reshape(3 * D)
        up = lax.dynamic_index_in_dim(biases[:, HALF:], f, axis=0, keepdims=False)
        return cut(qkv, 288), up

    pairs = [own_vectors(rows[:, 4]), own_vectors(rows[:, 3])]
    g_b_qkv = jnp.stack([pair[0] for pair in pairs])
    g_b_up = jnp.stack([pair[1] for pair in pairs])
    g_branch, g_gain, g_shift = (cut(jnp.stack([summed[8 + i], summed[i]]), 96) for i in range(3))
    return (
        outputs[None], grad[None], g_qkv, g_b_qkv, g_out, g_branch, g_up, g_b_up, g_down, g_branch, g_gain, g_shift,
    )


def solution(mesh):
    seqs = ("dp", "fsdp")
    whole = P(None, "fsdp", None)
    row = P(None, "fsdp")
    in_specs = (
        P(seqs, "ctx", None), P(seqs, "ctx"), P(seqs, "ctx", None),
        whole, row, whole, row, whole, row, whole, row, row, row,
    )
    out_specs = (
        P(seqs, "ctx", None), P(seqs, "ctx", None),
        whole, row, whole, row, whole, row, whole, row, row, row,
    )
    return jax.shard_map(body, mesh=mesh, in_specs=in_specs, out_specs=out_specs, check_vma=False)
```

```python
import functools

import jax
import jax.numpy as jnp
from jax import lax
from jax.experimental import pallas as pl
from jax.experimental.pallas import tpu as pltpu
from jax.sharding import PartitionSpec as P

MESH = pl.DeviceIdType.MESH
HEAD_DIM = 64
ROT = 16
LAYERS = 2
D = 768
FF = 3072
N = 8
TOK = 128
SEQ = 1024
HALF = 384
epsilon = 1e-05
BF = jnp.bfloat16
F32 = jnp.float32
ANY = pl.BlockSpec(memory_space=pl.ANY)


def dot(a, b, dims):
    return lax.dot_general(a, b, (dims, ((), ())), preferred_element_type=F32)


def meet(devices):
    barrier = pltpu.get_barrier_semaphore()
    for device in devices:
        pl.semaphore_signal(barrier, inc=1, device_id=device, device_id_type=MESH)
    pl.semaphore_wait(barrier, len(devices))


def push(src, dst, send, recv, device):
    copy = pltpu.make_async_remote_copy(
        src_ref=src, dst_ref=dst, send_sem=send, recv_sem=recv, device_id=device, device_id_type=MESH
    )
    copy.start()
    return copy


def others(axis, index):
    return [{axis: lax.rem(index + d, N)} for d in range(1, N)]


class Group:
    def __init__(self, axis):
        self.axis = axis
        index = lax.axis_index(axis)
        self.r, self.h = (index % 4, index // 4) if axis == "ctx" else (index // 2, index % 2)
        self.right = {axis: self.slot(1, 0)}
        self.left = {axis: self.slot(3, 0)}
        self.pair = {axis: self.slot(0, 1)}

    def slot(self, dr, dh):
        r, h = lax.rem(self.r + dr, 4), lax.rem(self.h + dh, 2)
        return h * 4 + r if self.axis == "ctx" else r * 2 + h

    def neighbours(self):
        return [self.right, self.left, self.pair]


class Lane:
    def __init__(self, sems):
        self.send, self.recv = sems
        self.copies = []

    def go(self, src, dst, device):
        i = len(self.copies)
        self.copies.append(push(src, dst, self.send.at[i], self.recv.at[i], device))
        return self.copies[-1]

    def finish(self):
        for copy in self.copies:
            copy.wait_send()


def run(*steps):
    live = list(steps)
    while live:
        for one in list(live):
            try:
                next(one)
            except StopIteration:
                live.remove(one)


GATHERS = 8


def gather_steps(lane, group, own, at, cut, rows):
    head, tail = pl.ds(0, cut), pl.ds(cut, rows - cut)
    go = lane.go
    me, twin, far = group.slot(0, 0), group.slot(0, 1), group.slot(2, 0)
    c0 = go(own, at(me), group.right)
    c1 = go(own, at(me), group.left)
    c2 = go(own, at(me), group.pair)
    yield
    c0.wait_recv()
    behind = at(group.slot(3, 0)).at[head]
    c3 = go(behind, behind, group.right)
    yield
    c1.wait_recv()
    ahead = at(group.slot(1, 0)).at[tail]
    c4 = go(ahead, ahead, group.left)
    yield
    c2.wait_recv()
    c5 = go(at(twin), at(twin), group.right)
    c6 = go(at(twin), at(twin), group.left)
    yield
    c3.wait_recv()
    yield
    c4.wait_recv()
    c7 = go(at(far), at(far), group.pair)
    for copy in (c5, c6, c7):
        yield
        copy.wait_recv()


SCATTERS = 11


def scatter_scratch(rows, cut, width):
    return [
        pltpu.VMEM((rows, width), BF),
        pltpu.VMEM((rows, width), BF),
        pltpu.VMEM((cut, width), BF),
        pltpu.VMEM((rows - cut, width), BF),
        pltpu.VMEM((cut, width), BF),
        pltpu.VMEM((rows - cut, width), BF),
        pltpu.VMEM((2, rows, width), BF),
        pltpu.VMEM((2, rows, width), BF),
        pltpu.VMEM((rows, width), BF),
        pltpu.VMEM((rows, width), BF),
    ]


SCRATCHES = 10


def scatter_steps(lane, group, src, cut, rows, buffers, take):
    in_far, st_far, in_right, in_left, st_left, st_right, from_right, from_left, st_pair, from_pair = buffers
    head, tail = pl.ds(0, cut), pl.ds(cut, rows - cut)
    go = lane.go
    opposite = go(src.at[group.slot(2, 1)], in_far, group.pair)
    beside = [
        go(src.at[group.slot(3, 1)], from_right.at[0], group.left),
        go(src.at[group.slot(1, 1)], from_left.at[0], group.right),
    ]
    near = [
        go(src.at[group.slot(3, 0)].at[tail], from_right.at[1].at[tail], group.left),
        go(src.at[group.slot(1, 0)].at[head], from_left.at[1].at[head], group.right),
    ]
    yield
    opposite.wait_recv()
    st_far[...] = (src[group.slot(2, 0)].astype(F32) + in_far[...].astype(F32)).astype(BF)
    far_left = go(st_far.at[head], in_right, group.left)
    far_right = go(st_far.at[tail], in_left, group.right)
    for copy in beside:
        yield
        copy.wait_recv()
    total = src[group.slot(0, 1)].astype(F32) + from_right[0].astype(F32) + from_left[0].astype(F32)
    st_pair[...] = total.astype(BF)
    last = go(st_pair, from_pair, group.pair)
    yield
    far_left.wait_recv()
    st_left[...] = (src[group.slot(3, 0), head].astype(F32) + in_right[...].astype(F32)).astype(BF)
    near.append(go(st_left, from_right.at[1].at[head], group.left))
    yield
    far_right.wait_recv()
    st_right[...] = (src[group.slot(1, 0), tail].astype(F32) + in_left[...].astype(F32)).astype(BF)
    near.append(go(st_right, from_left.at[1].at[tail], group.right))
    for copy in near + [last]:
        yield
        copy.wait_recv()
    total = src[group.slot(0, 0)].astype(F32) + from_right[1].astype(F32) + from_left[1].astype(F32)
    take(total + from_pair[...].astype(F32))


def sems(count):
    return [pltpu.SemaphoreType.DMA((count,)), pltpu.SemaphoreType.DMA((count,))]


def params(collective_id):
    return pltpu.CompilerParams(
        collective_id=collective_id, has_side_effects=True, vmem_limit_bytes=56 * 1024 * 1024
    )


def normalize(stream):
    mean = jnp.mean(stream, axis=-1, keepdims=True)
    centred = stream - mean
    scale = lax.rsqrt(jnp.mean(centred * centred, axis=-1, keepdims=True) + epsilon)
    return centred * scale, scale


def norm_back(stream, grad_normed, gain):
    unit, scale = normalize(stream)
    grad_unit = grad_normed * gain
    first = jnp.mean(grad_unit, axis=-1, keepdims=True)
    second = jnp.mean(grad_unit * unit, axis=-1, keepdims=True)
    grad_gain = jnp.sum(grad_normed * unit, axis=0, keepdims=True)
    grad_shift = jnp.sum(grad_normed, axis=0, keepdims=True)
    return scale * (grad_unit - first - unit * second), grad_gain, grad_shift


PIECE = 64
ROWS = 96 + PIECE
CUT = 80
W_FIRST = ROWS + 16
W_CUT = 96
VMEM = pl.BlockSpec(memory_space=pltpu.VMEM)


def shard_scratch(rows):
    return [
        pltpu.VMEM((N, rows, HALF), BF),
        pltpu.VMEM((N, PIECE, HALF), BF),
        pltpu.VMEM((N, PIECE, HALF), BF),
    ]


SHARD_LANE = N - 1 + 3


def shard_steps(lane, lane_z, fsdp, cs, core, src, cut, rows, scratch, outs, own, kept):
    held, mixed, got = scratch
    c, k = lax.axis_index("ctx"), lax.axis_index("dp")
    first = pltpu.make_async_copy(src.at[k], held.at[fsdp.slot(0, 0)], own.at[0])
    first.start()
    yield from gather_steps(lane_z, fsdp, src.at[k], lambda slot: held.at[slot], cut, rows)
    first.wait()
    low = lax.broadcasted_iota(jnp.int32, (16, HALF), 0) < 8
    for i in range(N):
        own_rows = held[i, pl.ds(96, 16)].astype(F32)
        shared = held[i // 2 * 2 + c // 4, pl.ds(96, 16)].astype(F32)
        mixed[i, pl.ds(0, 16)] = jnp.where(low, own_rows, shared).astype(BF)
        mixed[i, pl.ds(16, 48)] = held[i, pl.ds(112, 48)]
    turn = [lane.go(mixed.at[peer["ctx"]], got.at[c], peer) for peer in cs]
    got[c] = mixed[c]
    cross = []

    def share(part, out, sem):
        cross.append(lane.go(part, out.at[k], core))
        keep = pltpu.make_async_copy(part, out.at[k], sem)
        keep.start()
        kept.append(keep)

    share(held.at[:, pl.ds(0, 96)], outs[0], own.at[1])
    if len(outs) > 2:
        share(held.at[:, pl.ds(ROWS, 16)], outs[2], own.at[2])
    for copy in turn:
        yield
        copy.wait_recv()
    share(got, outs[1], own.at[3])
    for copy in cross:
        yield
        copy.wait_recv()


COLS_SHAPE = jax.ShapeDtypeStruct((2, N, 96, HALF), BF)
PIECES_SHAPE = jax.ShapeDtypeStruct((2, N, PIECE, HALF), BF)


def weights_kernel(
    src, places, x, cols_all, pieces_all, vec_all, places_all, unit_all, *rest
):
    scratch, unit, rest = rest[:3], rest[3], rest[4:]
    lane, lane_z, lane_m, lane_u = (Lane(rest[2 * i : 2 * i + 2]) for i in range(4))
    own, keeps = rest[8], rest[9]
    c = lax.axis_index("ctx")
    fsdp, ctx = Group("fsdp"), Group("ctx")
    cs = others("ctx", c)
    core = {"dp": 1 - lax.axis_index("dp")}
    mark = pltpu.make_async_copy(places, places_all.at[c], keeps.at[0])
    mark.start()
    meet(fsdp.neighbours() + cs + [core])
    kept = [mark]
    marks = [lane_m.go(places, places_all.at[c], peer) for peer in cs]

    def tokens():
        unit[...] = normalize(x[...])[0].astype(BF)
        keep = pltpu.make_async_copy(unit, unit_all.at[c], keeps.at[1])
        keep.start()
        kept.append(keep)
        yield from gather_steps(lane_u, ctx, unit, lambda slot: unit_all.at[slot], TOK // 2, TOK)

    outs = (cols_all, pieces_all, vec_all)
    run(
        shard_steps(lane, lane_z, fsdp, cs, core, src, W_CUT, W_FIRST, scratch, outs, own, kept),
        tokens(),
    )
    for copy in marks:
        copy.wait_recv()
    for each in (lane, lane_z, lane_m, lane_u):
        each.finish()
    for copy in kept:
        copy.wait()


def gather_weights(src, places, x, collective_id):
    tokens = jax.ShapeDtypeStruct((N, TOK, D), BF)
    return pl.pallas_call(
        weights_kernel,
        out_shape=(
            COLS_SHAPE,
            PIECES_SHAPE,
            jax.ShapeDtypeStruct((2, N, 16, HALF), BF),
            jax.ShapeDtypeStruct((N,) + places.shape, places.dtype),
            tokens,
        ),
        in_specs=[ANY] * 2 + [VMEM],
        out_specs=[ANY] * 5,
        scratch_shapes=shard_scratch(W_FIRST)
        + [pltpu.VMEM((TOK, D), BF)]
        + sems(SHARD_LANE)
        + sems(GATHERS)
        + sems(N - 1)
        + sems(GATHERS)
        + [pltpu.SemaphoreType.DMA((4,)), pltpu.SemaphoreType.DMA((2,))],
        compiler_params=params(collective_id),
    )(src, places, x)


def marks_of(places):
    frequency = 10000.0 ** (-2.0 * jnp.arange(ROT // 2, dtype=F32) / ROT)
    where = places.astype(F32).reshape(1, -1)
    angles = frequency[:, None] * where
    return jnp.concatenate([jnp.cos(angles), jnp.sin(angles), jnp.broadcast_to(where, angles.shape)], axis=0)


def prepare_kernel(marks, vectors, tables, col, rows_out):
    zero = jnp.zeros((8, TOK), F32)
    one = zero + 1.0
    for i in range(N):
        cosine, sine, where = marks[i, 0:8], marks[i, 8:16], marks[i, 16:24]
        rows = pl.ds(i * TOK, TOK)
        own = [cosine, cosine] + [one] * 6
        left = [zero, sine] + [zero] * 6
        right = [-sine, zero] + [zero] * 6
        for t, tiles in enumerate((own, left, right)):
            tables[t, rows] = jnp.concatenate(tiles + tiles, axis=0).T
        col[rows] = jnp.concatenate([where] * 16, axis=0).T

    c = lax.axis_index("ctx")
    head_a, head_b = 3 * (c // 2) + 2 * (c % 2), 3 * (c // 2) + 1

    def place(values, column, width, cut):
        shard = jnp.zeros((1, width), jnp.int32)
        for t in range(1, N):
            shard = shard + jnp.where(column >= cut * t, 1, 0)
        inner = column - cut * shard
        pick = lax.broadcasted_iota(jnp.int32, (HALF, width), 0) == inner
        spread_ = dot(values.astype(BF), jnp.where(pick, 1.0, 0.0).astype(BF), ((1,), (0,)))
        mine = lax.broadcasted_iota(jnp.int32, (N, width), 0) == shard
        return jnp.sum(jnp.where(mine, spread_, 0.0), axis=0, keepdims=True)

    lanes = lax.broadcasted_iota(jnp.int32, (1, D), 1)
    lane = lax.broadcasted_iota(jnp.int32, (1, HALF), 1)
    third = jnp.where(lane >= 128, 1, 0) + jnp.where(lane >= 256, 1, 0)
    within = lane - 128 * third
    second = jnp.where(within >= HEAD_DIM, 1, 0)
    head = jnp.where(second == 1, head_b, head_a)
    column = 192 * head + HEAD_DIM * third + (within - HEAD_DIM * second)
    for layer in range(LAYERS):
        shards = [vectors[layer, i].astype(F32) for i in range(N)]

        def row(r):
            return jnp.concatenate([one_shard[r : r + 1] for one_shard in shards], axis=0)

        rows_out[layer, 0:1] = place(row(2), lanes, D, 96)
        rows_out[layer, 1:2] = place(row(3), lanes, D, 96)
        rows_out[layer, 2:3] = place(row(4), lanes, D, 96) + place(row(5), lanes, D, 96)
        rows_out[layer, 3:4, pl.ds(0, HALF)] = place(row(0), column, HALF, 288)
        rows_out[layer, 3:4, pl.ds(HALF, HALF)] = vectors[layer, c].astype(F32)[1:2]
        rows_out[layer, 4:8] = jnp.zeros((4, D), F32)


def prepare(marks, vectors):
    return pl.pallas_call(
        prepare_kernel,
        out_shape=(
            jax.ShapeDtypeStruct((3, SEQ, 128), F32),
            jax.ShapeDtypeStruct((SEQ, 128), F32),
            jax.ShapeDtypeStruct((LAYERS, 8, D), F32),
        ),
        in_specs=[VMEM] * 2,
        out_specs=[VMEM] * 3,
        compiler_params=pltpu.CompilerParams(vmem_limit_bytes=48 * 1024 * 1024),
    )(marks, vectors)


BLOCK = 256
BLOCKS = SEQ // BLOCK


def unit_rows(b):
    s = lax.axis_index("ctx") % 2
    start = jnp.where(b < BLOCKS, b * BLOCK, s * (SEQ // 2) + (b - BLOCKS) * BLOCK)
    start = pl.multiple_of(start, BLOCK)
    lanes = lax.broadcasted_iota(jnp.int32, (BLOCK, 2 * HEAD_DIM), 1) // HEAD_DIM
    return start, lanes == jnp.where(b < BLOCKS, 0, 1)


def mix_rows(pieces, w_mix):
    for h in range(2):
        cols = pl.ds(HALF * h, HALF)
        rows = [pieces[h, j, pl.ds(0, 16)].astype(F32) for j in range(N)]
        heads = [r[:8] for r in rows] + [r[8:] for r in rows]
        w_mix[pl.ds(0, 128), cols] = jnp.concatenate(heads, axis=0).astype(BF)
        for j in range(N):
            w_mix[pl.ds(128 + 48 * j, 48), cols] = pieces[h, j, pl.ds(16, 48)]


def forward_steps(
    unit, vectors, w_cat, pieces, col, row, tables,
    branch, normed, query, key, value, slope, mixed, lse, w_mix, turned,
):
    mix_rows(pieces, w_mix)

    @pl.loop(0, BLOCKS)
    def _(i):
        rows = pl.ds(pl.multiple_of(i * BLOCK, BLOCK), BLOCK)
        low = (unit[rows].astype(F32) * vectors[0:1] + vectors[1:2]).astype(BF)
        normed[rows] = low
        heads = dot(low, w_cat[0], ((1,), (0,))) + vectors[3:4, :HALF]

        def rotate(values):
            return (
                values * tables[0, rows]
                + pltpu.roll(values, 8, axis=1) * tables[1, rows]
                + pltpu.roll(values, 120, axis=1) * tables[2, rows]
            )

        query[rows] = (rotate(heads[:, :128]) * HEAD_DIM ** (-0.5)).astype(BF)
        key[rows] = rotate(heads[:, 128:256]).astype(BF)
        value[rows] = heads[:, 256:].astype(BF)
        pre = dot(low, w_cat[1], ((1,), (0,))) + vectors[3:4, HALF:]
        cdf = 0.5 * (1.0 + lax.erf(pre * 0.5**0.5))
        mixed[rows, pl.ds(128, HALF)] = (pre * cdf).astype(BF)
        mixed[rows, pl.ds(0, 128)] = jnp.zeros((BLOCK, 128), BF)
        slope[rows] = cdf + pre * (jnp.exp(-0.5 * pre * pre) * 0.3989422804014327)

    turned[...] = value[...].astype(F32).T.astype(BF)
    yield
    for n in range(3):

        @pl.loop(2 * n, 2 * n + 2)
        def _(b):
            start, mask = unit_rows(b)
            rows = pl.ds(start, BLOCK)
            q = jnp.where(mask, query[rows].astype(F32), 0.0).astype(BF)
            scores = dot(key[...], q, ((1,), (1,)))
            seen = jnp.concatenate([col[...], col[...]], axis=1) <= row[pl.ds(start // BLOCK, 1)]
            scores = jnp.where(seen, scores, -jnp.inf)
            top = jnp.max(scores, axis=0, keepdims=True)
            expos = jnp.exp(scores - top)
            total = jnp.sum(expos, axis=0, keepdims=True)
            lse[pl.ds(b, 1)] = top + jnp.log(total)
            probs = (expos * (1.0 / total)).astype(BF)
            out = dot(turned[...], probs, ((1,), (0,))).T
            mixed[rows, pl.ds(0, 128)] = jnp.where(mask, out, mixed[rows, pl.ds(0, 128)].astype(F32)).astype(BF)

        yield
    for i in range(N):
        rows = pl.ds(i * TOK, TOK)
        branch[i] = dot(mixed[rows], w_mix[...], ((1,), (0,))).astype(BF)


def forward_shapes():
    shape = jax.ShapeDtypeStruct
    return (
        shape((N, TOK, D), BF),
        shape((SEQ, D), BF),
        shape((SEQ, 128), BF),
        shape((SEQ, 128), BF),
        shape((SEQ, 128), BF),
        shape((SEQ, HALF), F32),
        shape((SEQ, 512), BF),
        shape((8, BLOCK), F32),
        shape((512, D), BF),
    )


FORWARDS = 9


def local_params():
    return pltpu.CompilerParams(vmem_limit_bytes=56 * 1024 * 1024)


def forward_kernel(*refs):
    run(forward_steps(*refs))


def forward(*args):
    return pl.pallas_call(
        forward_kernel,
        out_shape=forward_shapes(),
        in_specs=[VMEM] * len(args),
        out_specs=[VMEM] * FORWARDS,
        scratch_shapes=[pltpu.VMEM((128, SEQ), BF)],
        compiler_params=local_params(),
    )(*args)


def forward_between_kernel(*refs):
    args, (x, cot, src), refs = refs[:7], refs[7:10], refs[10:]
    outs, refs = refs[:FORWARDS], refs[FORWARDS:]
    (x_next, unit_all, low_all, cols_all, pieces_all), refs = refs[:5], refs[5:]
    turned, unit, low_g, scratch, rest = refs[0], refs[1], refs[2], refs[3:6], refs[6:]
    buffers, rest = rest[:SCRATCHES], rest[SCRATCHES:]
    lane, lane_u, lane_g, lane_w, lane_z = (Lane(rest[2 * i : 2 * i + 2]) for i in range(5))
    own, keeps = rest[10], rest[11]
    ctx, fsdp = Group("ctx"), Group("fsdp")
    cs = others("ctx", lax.axis_index("ctx"))
    core = {"dp": 1 - lax.axis_index("dp")}
    meet(fsdp.neighbours() + cs + [core])
    kept = []
    branch, vectors = outs[0], args[1]

    def tokens():
        yield from forward_steps(*args, *outs, turned)

        def take(total):
            x_next[...] = x[...] + (total + vectors[2:3])

        yield from scatter_steps(lane, ctx, branch, TOK // 2, TOK, buffers, take)
        unit[...] = normalize(x_next[...])[0].astype(BF)
        keep = pltpu.make_async_copy(unit, unit_all.at[ctx.slot(0, 0)], keeps.at[0])
        keep.start()
        kept.append(keep)
        yield from gather_steps(lane_u, ctx, unit, lambda slot: unit_all.at[slot], TOK // 2, TOK)

    def later():
        low_g[...] = cot[...].astype(BF)
        keep = pltpu.make_async_copy(low_g, low_all.at[ctx.slot(0, 0)], keeps.at[1])
        keep.start()
        kept.append(keep)
        yield from gather_steps(lane_g, ctx, low_g, lambda slot: low_all.at[slot], TOK // 2, TOK)

    outs_w = (cols_all, pieces_all)
    run(
        shard_steps(lane_w, lane_z, fsdp, cs, core, src, CUT, ROWS, scratch, outs_w, own, kept),
        later(),
        tokens(),
    )
    for each in (lane, lane_u, lane_g, lane_w, lane_z):
        each.finish()
    for copy in kept:
        copy.wait()


def forward_between(args, x, cot, src, collective_id):
    tokens = jax.ShapeDtypeStruct((N, TOK, D), BF)
    return pl.pallas_call(
        forward_between_kernel,
        out_shape=forward_shapes()
        + (jax.ShapeDtypeStruct((TOK, D), F32), tokens, tokens, COLS_SHAPE, PIECES_SHAPE),
        in_specs=[VMEM] * 9 + [ANY],
        out_specs=[VMEM] * (FORWARDS + 1) + [ANY] * 4,
        scratch_shapes=[
            pltpu.VMEM((128, SEQ), BF),
            pltpu.VMEM((TOK, D), BF),
            pltpu.VMEM((TOK, D), BF),
        ]
        + shard_scratch(ROWS)
        + scatter_scratch(TOK, TOK // 2, D)
        + sems(SCATTERS)
        + sems(GATHERS)
        + sems(GATHERS)
        + sems(SHARD_LANE)
        + sems(GATHERS)
        + [pltpu.SemaphoreType.DMA((4,)), pltpu.SemaphoreType.DMA((2,))],
        compiler_params=params(collective_id),
    )(*args, x, cot, src)


BACK_ARGS = 12


def backward_scratch():
    return [
        pltpu.VMEM((SEQ, 128), BF),
        pltpu.VMEM((SEQ, D), BF),
        pltpu.VMEM((SEQ, 128), F32),
        pltpu.VMEM((SEQ, 128), F32),
        pltpu.VMEM((SEQ, 128), F32),
        pltpu.VMEM((128, SEQ), BF),
        pltpu.VMEM((D, D), F32),
        pltpu.VMEM((N, TOK, D), BF),
        pltpu.VMEM((2, N, 96, HALF), BF),
        pltpu.VMEM((2, N, PIECE, HALF), BF),
    ]


BACKS = 10


def backward_steps(
    ready, low, w_cat, normed, query, key, value, slope, mixed, lse, w_mix, col, row, tables, grad_b,
    grad_att, grad_pre, dq, dk, dv, turned, big, grad_normed, part_a, part_b,
):
    @pl.loop(0, 2)
    def _(i):
        cols = pl.ds(pl.multiple_of(i * BLOCK, BLOCK), BLOCK)
        big[cols] = dot(mixed[:, cols], low[...], ((0,), (0,)))

    for j in range(N):
        for h in range(2):
            at = slice(HALF * h, HALF * h + HALF)
            first = big[8 * j : 8 * j + 8, at]
            second = big[64 + 8 * j : 64 + 8 * j + 8, at]
            part_b[h, j, pl.ds(0, 16)] = jnp.concatenate([first, second], axis=0).astype(BF)
            part_b[h, j, pl.ds(16, 48)] = big[128 + 48 * j : 176 + 48 * j, at].astype(BF)
    ready.add("b")
    yield

    @pl.loop(0, BLOCKS)
    def _(i):
        rows = pl.ds(pl.multiple_of(i * BLOCK, BLOCK), BLOCK)
        back = dot(low[rows], w_mix[...], ((1,), (1,)))
        grad_att[rows] = back[:, :128].astype(BF)
        grad_pre[rows, pl.ds(HALF, HALF)] = (back[:, 128:] * slope[rows]).astype(BF)

    turned[...] = key[...].astype(F32).T.astype(BF)
    dq[...] = jnp.zeros((SEQ, 128), F32)
    dk[...] = jnp.zeros((SEQ, 128), F32)
    dv[...] = jnp.zeros((SEQ, 128), F32)
    yield
    for n in range(3):

        @pl.loop(2 * n, 2 * n + 2)
        def _(b):
            start, mask = unit_rows(b)
            rows = pl.ds(start, BLOCK)
            q = jnp.where(mask, query[rows].astype(F32), 0.0).astype(BF)
            g = jnp.where(mask, grad_att[rows].astype(F32), 0.0).astype(BF)
            scores = dot(key[...], q, ((1,), (1,)))
            seen = jnp.concatenate([col[...], col[...]], axis=1) <= row[pl.ds(start // BLOCK, 1)]
            probs = jnp.exp(jnp.where(seen, scores, -jnp.inf) - lse[pl.ds(b, 1)])
            grad_probs = dot(value[...], g, ((1,), (1,)))
            mean = jnp.sum(probs * grad_probs, axis=0, keepdims=True)
            grad_scores = (probs * (grad_probs - mean)).astype(BF)
            dq[rows] = jnp.where(mask, dot(turned[...], grad_scores, ((1,), (0,))).T, dq[rows])
            dk[...] += dot(grad_scores, q, ((1,), (0,)))
            dv[...] += dot(probs.astype(BF), g, ((1,), (0,)))

        yield
    grad_b[...] = jnp.zeros((1, D), F32)

    @pl.loop(0, N)
    def _(i):
        rows = pl.ds(pl.multiple_of(i * TOK, TOK), TOK)

        def rotate_back(grads):
            return (
                grads * tables[0, rows]
                + pltpu.roll(grads * tables[1, rows], 120, axis=1)
                + pltpu.roll(grads * tables[2, rows], 8, axis=1)
            )

        grad_pre[rows, pl.ds(0, 128)] = rotate_back(dq[rows] * HEAD_DIM ** (-0.5)).astype(BF)
        grad_pre[rows, pl.ds(128, 128)] = rotate_back(dk[rows]).astype(BF)
        grad_pre[rows, pl.ds(256, 128)] = dv[rows].astype(BF)
        block = grad_pre[rows]
        grad_b[...] += jnp.sum(block.astype(F32), axis=0, keepdims=True)
        grad_normed[i] = (
            dot(block[:, :HALF], w_cat[0], ((1,), (1,))) + dot(block[:, HALF:], w_cat[1], ((1,), (1,)))
        ).astype(BF)

    ready.add("normed")
    yield

    @pl.loop(0, D // BLOCK)
    def _(i):
        cols = pl.ds(pl.multiple_of(i * BLOCK, BLOCK), BLOCK)
        big[cols] = dot(normed[:, cols], grad_pre[...], ((0,), (0,)))

    for f in range(N):
        for h in range(2):
            part_a[h, f] = big[96 * f : 96 * f + 96, HALF * h : HALF * h + HALF].astype(BF)
    ready.add("a")


def grads_scratch():
    return [
        pltpu.VMEM((N, 96, HALF), BF),
        pltpu.VMEM((N, PIECE, HALF), BF),
        pltpu.VMEM((N, PIECE, HALF), BF),
        pltpu.VMEM((N, ROWS, HALF), BF),
    ] + scatter_scratch(ROWS, CUT, HALF)


GRADS = 4 + SCRATCHES


def grads_steps(ready, lane, lane_z, fsdp, cs, core, part_a, part_b, scratch, take):
    their_a, their_b, got, blocks = scratch[:4]
    c, k = lax.axis_index("ctx"), lax.axis_index("dp")
    while "b" not in ready:
        yield
    first_b = lane.go(part_b.at[1 - k], their_b, core)
    yield
    first_b.wait_recv()
    for i in range(N):
        their_b[i] = (part_b[k, i].astype(F32) + their_b[i].astype(F32)).astype(BF)
    turn = [lane.go(their_b.at[peer["ctx"]], got.at[c], peer) for peer in cs]
    got[c] = their_b[c]
    while "a" not in ready:
        yield
    first_a = lane.go(part_a.at[1 - k], their_a, core)
    for copy in turn:
        copy.wait_recv()
    low = lax.broadcasted_iota(jnp.int32, (16, HALF), 0) < 8
    for i in range(N):
        rows = got[i, pl.ds(0, 16)].astype(F32)
        pair = got[i + 1 - 2 * (i % 2), pl.ds(0, 16)].astype(F32)
        blocks[i, pl.ds(96, 16)] = jnp.where(low, rows, rows + pair).astype(BF)
        blocks[i, pl.ds(112, 48)] = got[i, pl.ds(16, 48)]
    yield
    first_a.wait_recv()
    for i in range(N):
        blocks[i, pl.ds(0, 96)] = (part_a[k, i].astype(F32) + their_a[i].astype(F32)).astype(BF)
    yield from scatter_steps(lane_z, fsdp, blocks, CUT, ROWS, scratch[4:], take)


def turn_kernel(*refs):
    (low, *args), refs = refs[:13], refs[13:]
    (x, grad, vectors, out_parts, bias), refs = refs[:5], refs[5:]
    (outputs, grad_next, low_all, vecs, share), refs = refs[:5], refs[5:]
    (low_g, grad_b), refs = refs[:2], refs[2:]
    back, refs = refs[:BACKS], refs[BACKS:]
    buffers, refs = refs[:SCRATCHES], refs[SCRATCHES:]
    buffers_o, refs = refs[:SCRATCHES], refs[SCRATCHES:]
    scratch, rest = refs[:GRADS], refs[GRADS:]
    lane, lane_g, lane_w, lane_z, lane_o = (Lane(rest[2 * i : 2 * i + 2]) for i in range(5))
    keep_sem = rest[10]
    ctx, fsdp = Group("ctx"), Group("fsdp")
    cs = others("ctx", lax.axis_index("ctx"))
    core = {"dp": 1 - lax.axis_index("dp")}
    meet(cs + fsdp.neighbours() + [core])
    kept, ready = [], set()

    def tokens():
        def take(total):
            back_, grad_gain, grad_shift = norm_back(x[...], total, vectors[0:1])
            grad_next[...] = grad[...] + back_
            rounded = grad[...].astype(BF).astype(F32)
            vecs[pl.ds(0, 1)] = jnp.sum(rounded, axis=0, keepdims=True)
            vecs[pl.ds(1, 1)] = grad_gain
            vecs[pl.ds(2, 1)] = grad_shift
            vecs[pl.ds(3, 1)] = grad_b[...]
            vecs[pl.ds(4, 4)] = jnp.zeros((4, D), F32)

        while "normed" not in ready:
            yield
        yield from scatter_steps(lane, ctx, back[7], TOK // 2, TOK, buffers, take)
        low_g[...] = grad_next[...].astype(BF)
        keep = pltpu.make_async_copy(low_g, low_all.at[ctx.slot(0, 0)], keep_sem)
        keep.start()
        kept.append(keep)
        yield from gather_steps(lane_g, ctx, low_g, lambda slot: low_all.at[slot], TOK // 2, TOK)

    def weights():
        def take(total):
            share[...] = total.astype(BF)

        yield from grads_steps(ready, lane_w, lane_z, fsdp, cs, core, back[8], back[9], scratch, take)

    def ends():
        def take(total):
            outputs[...] = x[...] + (total + bias[2:3])

        yield from scatter_steps(lane_o, ctx, out_parts, TOK // 2, TOK, buffers_o, take)

    run(ends(), backward_steps(ready, low, *args, grad_b, *back), tokens(), weights())
    for each in (lane, lane_g, lane_w, lane_z, lane_o):
        each.finish()
    for copy in kept:
        copy.wait()


def turn(args, x, grad, vectors, out_parts, collective_id):
    tokens = jax.ShapeDtypeStruct((TOK, D), F32)
    return pl.pallas_call(
        turn_kernel,
        out_shape=(
            tokens,
            tokens,
            jax.ShapeDtypeStruct((N, TOK, D), BF),
            jax.ShapeDtypeStruct((8, D), F32),
            jax.ShapeDtypeStruct((ROWS, HALF), BF),
        ),
        in_specs=[VMEM] * 18,
        out_specs=(VMEM, VMEM, ANY, VMEM, VMEM),
        scratch_shapes=[pltpu.VMEM((TOK, D), BF), pltpu.VMEM((1, D), F32)]
        + backward_scratch()
        + scatter_scratch(TOK, TOK // 2, D)
        + scatter_scratch(TOK, TOK // 2, D)
        + grads_scratch()
        + sems(SCATTERS)
        + sems(GATHERS)
        + sems(2 + N - 1)
        + sems(SCATTERS)
        + sems(SCATTERS)
        + [pltpu.SemaphoreType.DMA],
        compiler_params=params(collective_id),
    )(*args, x, grad, vectors, out_parts, vectors)


FIRST_ROWS = ROWS + 16


def last_kernel(*refs):
    (low, *args), refs = refs[:13], refs[13:]
    (x, grad, vectors, vecs, share), refs = refs[:5], refs[5:]
    (grad_next, out_first, out_last), refs = refs[:3], refs[3:]
    (both, v_mine, v_their, v_all, grad_b), refs = refs[:5], refs[5:]
    back, refs = refs[:BACKS], refs[BACKS:]
    buffers, refs = refs[:SCRATCHES], refs[SCRATCHES:]
    scratch, rest = refs[:GRADS], refs[GRADS:]
    lane, lane_w, lane_z, lane_v, lane_x, lane_s = (Lane(rest[2 * i : 2 * i + 2]) for i in range(6))
    keeps = rest[12]
    c, f, k = lax.axis_index("ctx"), lax.axis_index("fsdp"), lax.axis_index("dp")
    ctx, fsdp = Group("ctx"), Group("fsdp")
    cs, fs = others("ctx", c), others("fsdp", f)
    core = {"dp": 1 - k}
    meet(cs + fs + [core])
    ready = set()

    def tokens():
        def take(total):
            back_, grad_gain, grad_shift = norm_back(x[...], total, vectors[0:1])
            grad_next[...] = grad[...] + back_
            rounded = grad[...].astype(BF).astype(F32)
            branch = jnp.sum(rounded, axis=0, keepdims=True)
            mine = [vecs[...], branch, grad_gain, grad_shift, grad_b[...], jnp.zeros((4, D), F32)]
            mine = jnp.concatenate(mine, axis=0)
            v_mine[0] = mine[:, :HALF].astype(BF)
            v_mine[1] = mine[:, HALF:].astype(BF)

        while "normed" not in ready:
            yield
        yield from scatter_steps(lane, ctx, back[7], TOK // 2, TOK, buffers, take)
        cross = lane_v.go(v_mine.at[1 - k], v_their, core)
        yield
        cross.wait_recv()
        v_all[f] = (v_mine[k].astype(F32) + v_their[...].astype(F32)).astype(BF)
        copies = [lane_v.go(v_all.at[f], v_all.at[f], peer) for peer in fs]
        yield
        for copy in copies:
            copy.wait_recv()
        total = v_all[0].astype(F32)
        for i in range(1, N):
            total = total + v_all[i].astype(F32)
        both[pl.ds(ROWS, 16)] = total.astype(BF)

    def weights():
        def take(total):
            both[pl.ds(0, ROWS)] = total.astype(BF)

        yield from grads_steps(ready, lane_w, lane_z, fsdp, cs, core, back[8], back[9], scratch, take)

    kept = []

    def older():
        keep = pltpu.make_async_copy(share, out_last.at[k, c], keeps.at[0])
        keep.start()
        kept.append(keep)
        yield from gather_steps(lane_s, ctx, share, lambda slot: out_last.at[k, slot], CUT, ROWS)
        keep.wait()
        copy = lane_s.go(out_last.at[k], out_last.at[k], core)
        yield
        copy.wait_recv()

    run(older(), backward_steps(ready, low, *args, grad_b, *back), tokens(), weights())
    keep = pltpu.make_async_copy(both, out_first.at[k, c], keeps.at[1])
    keep.start()
    run(gather_steps(lane_x, ctx, both, lambda slot: out_first.at[k, slot], W_CUT, FIRST_ROWS))
    keep.wait()
    lane_x.go(out_first.at[k], out_first.at[k], core).wait_recv()
    for each in (lane, lane_w, lane_z, lane_v, lane_x, lane_s):
        each.finish()


def last(args, x, grad, vectors, vecs, share, collective_id):
    return pl.pallas_call(
        last_kernel,
        out_shape=(
            jax.ShapeDtypeStruct((TOK, D), F32),
            jax.ShapeDtypeStruct((2, N, FIRST_ROWS, HALF), BF),
            jax.ShapeDtypeStruct((2, N, ROWS, HALF), BF),
        ),
        in_specs=[VMEM] * 18,
        out_specs=(VMEM, ANY, ANY),
        scratch_shapes=[
            pltpu.VMEM((FIRST_ROWS, HALF), BF),
            pltpu.VMEM((2, 16, HALF), BF),
            pltpu.VMEM((16, HALF), BF),
            pltpu.VMEM((N, 16, HALF), BF),
            pltpu.VMEM((1, D), F32),
        ]
        + backward_scratch()
        + scatter_scratch(TOK, TOK // 2, D)
        + grads_scratch()
        + sems(SCATTERS)
        + sems(2 + N - 1)
        + sems(SCATTERS)
        + sems(N)
        + sems(GATHERS + 1)
        + sems(GATHERS + 1)
        + [pltpu.SemaphoreType.DMA((2,))],
        compiler_params=params(collective_id),
    )(*args, x, grad, vectors, vecs, share)


def spread_kernel(got_first, got_last, g_qkv, g_out, g_up, g_down):
    odd = lax.axis_index("fsdp") % 2
    for layer in range(LAYERS):
        got, base = (got_first, got_last)[layer], 0

        def heads(i, got=got, base=base):
            return got[0, i, pl.ds(base, 96)].astype(F32)

        chunks = []
        for p in range(4):
            one, two = heads(2 * p), heads(2 * p + 1)
            both = one + two
            for values, lane in ((one, 0), (both, HEAD_DIM), (two, 0)):
                chunks += [values[:, 128 * i + lane : 128 * i + lane + HEAD_DIM] for i in range(3)]
        for i in range(len(chunks) // 2):
            g_qkv[layer, :, pl.ds(128 * i, 128)] = jnp.concatenate(chunks[2 * i : 2 * i + 2], axis=1)
        for i in range(N):
            g_up[layer, :, pl.ds(HALF * i, HALF)] = got[1, i, pl.ds(base, 96)].astype(F32)
            for h in range(2):
                cols = pl.ds(HALF * h, HALF)
                g_down[layer, pl.ds(48 * i, 48), cols] = got[h, i, pl.ds(base + 112, 48)].astype(F32)
        for h in range(2):
            cols = pl.ds(HALF * h, HALF)
            rows = [got[h, i, pl.ds(base + 96, 16)].astype(F32) for i in range(N)]
            first = [r[:8] for r in rows]
            even = jnp.concatenate(first + [r[8:] for r in rows[:4]], axis=0)
            uneven = jnp.concatenate([r[8:] for r in rows[4:]] + first, axis=0)
            g_out[layer, :, cols] = jnp.where(odd == 0, even, uneven)


def spread(got_first, got_last):
    shape = jax.ShapeDtypeStruct
    return pl.pallas_call(
        spread_kernel,
        out_shape=(
            shape((LAYERS, 96, 3 * D), F32),
            shape((LAYERS, 96, D), F32),
            shape((LAYERS, 96, FF), F32),
            shape((LAYERS, HALF, D), F32),
        ),
        in_specs=[VMEM] * 2,
        out_specs=[VMEM] * 4,
        compiler_params=local_params(),
    )(got_first, got_last)


def body(
    inputs, positions, cotangent, w_qkv, b_qkv, w_out, b_out, w_up, b_up, w_down, b_down, ln_gain, ln_bias
):
    c = lax.axis_index("ctx")
    p, s = c // 2, lax.rem(c, 2)
    head_a, head_b = 3 * p + 2 * s, 3 * p + 1

    def heads_cols(w):
        grouped = w.reshape(w.shape[:-1] + (12, 3, HEAD_DIM))
        axis = grouped.ndim - 3
        both = jnp.concatenate(
            [
                lax.dynamic_slice_in_dim(grouped, head_a, 1, axis=axis),
                lax.dynamic_slice_in_dim(grouped, head_b, 1, axis=axis),
            ],
            axis=axis,
        )
        return jnp.swapaxes(both, axis, axis + 1).reshape(w.shape[:-1] + (HALF,))

    def hidden_cols(w):
        return lax.dynamic_slice_in_dim(w, c * HALF, HALF, axis=w.ndim - 1)

    f = lax.axis_index("fsdp")
    f_s = lax.rem(f, 2)

    def piece(w, start, count):
        return lax.dynamic_slice_in_dim(w, start, count, axis=1)

    cols = jnp.concatenate([heads_cols(w_qkv), hidden_cols(w_up)], axis=-1)
    first_rows = piece(w_out, jnp.where(f_s == 0, 0, 32) + 8 * c, 8)
    shared_rows = piece(w_out, jnp.where(f_s == 0, 64, -32) + 8 * jnp.where(f_s == 0, c % 4, c), 8)
    down_rows = piece(w_down, 48 * c, 48)
    by_layer = jnp.concatenate([cols, first_rows, shared_rows, down_rows], axis=1)
    def wide(vector):
        return jnp.pad(vector, ((0, 0), (0, HALF - vector.shape[1])))

    vec = jnp.stack([wide(v) for v in (b_qkv, b_up, ln_gain, ln_bias, b_out, b_down)], axis=1)
    vec = jnp.pad(vec, ((0, 0), (0, 10), (0, 0)))
    src = [jnp.stack([one[:, :HALF], one[:, HALF:]]) for one in (by_layer[0], by_layer[1])]
    src[0] = jnp.concatenate([src[0], vec], axis=1)
    stream, cot = inputs[0], cotangent[0]
    cols, pieces, vec_all, marks, unit = gather_weights(src[0], marks_of(positions), stream, 1)
    tables, col, vectors = prepare(marks, vec_all)
    row = marks[:, 16].reshape(BLOCKS, BLOCK)
    w_first = cols.reshape(2, D, HALF)
    branch, *kept_first, x_last, unit, low_last, cols, pieces_last = forward_between(
        (unit.reshape(SEQ, D), vectors[0], w_first, pieces, col, row, tables), stream, cot, src[1], 2
    )
    w_last = cols.reshape(2, D, HALF)
    branch, *kept_last = forward(
        unit.reshape(SEQ, D), vectors[1], w_last, pieces_last, col, row, tables
    )
    outputs, grad, low, vecs, share = turn(
        (low_last.reshape(SEQ, D), w_last, *kept_last, col, row, tables), x_last, cot, vectors[1], branch, 3
    )
    grad, got_first, got_last = last(
        (low.reshape(SEQ, D), w_first, *kept_first, col, row, tables), stream, grad, vectors[0], vecs, share, 4
    )
    g_qkv, g_out, g_up, g_down = spread(got_first, got_last)

    rows = jnp.concatenate([got_first[0, :, ROWS:], got_first[1, :, ROWS:]], axis=-1).astype(F32)
    summed = jnp.sum(rows, axis=0)

    def cut(vector, width):
        return lax.dynamic_slice_in_dim(vector, f * width, width, axis=vector.ndim - 1)

    def own_vectors(biases):
        qkv = biases[:, :HALF].reshape(4, 2, 3, 2, HEAD_DIM)
        shared = qkv[:, 0, :, 1] + qkv[:, 1, :, 1]
        qkv = jnp.stack([qkv[:, 0, :, 0], shared, qkv[:, 1, :, 0]], axis=1).reshape(3 * D)
        up = lax.dynamic_index_in_dim(biases[:, HALF:], f, axis=0, keepdims=False)
        return cut(qkv, 288), up

    pairs = [own_vectors(rows[:, 11]), own_vectors(rows[:, 3])]
    g_b_qkv = jnp.stack([pair[0] for pair in pairs])
    g_b_up = jnp.stack([pair[1] for pair in pairs])
    g_branch, g_gain, g_shift = (cut(jnp.stack([summed[8 + i], summed[i]]), 96) for i in range(3))
    return (
        outputs[None], grad[None], g_qkv, g_b_qkv, g_out, g_branch, g_up, g_b_up, g_down, g_branch, g_gain, g_shift,
    )


def solution(mesh):
    seqs = ("dp", "fsdp")
    whole = P(None, "fsdp", None)
    row = P(None, "fsdp")
    in_specs = (
        P(seqs, "ctx", None), P(seqs, "ctx"), P(seqs, "ctx", None),
        whole, row, whole, row, whole, row, whole, row, row, row,
    )
    out_specs = (
        P(seqs, "ctx", None), P(seqs, "ctx", None),
        whole, row, whole, row, whole, row, whole, row, row, row,
    )
    return jax.shard_map(body, mesh=mesh, in_specs=in_specs, out_specs=out_specs, check_vma=False)
```

```python
import functools

import jax
import jax.numpy as jnp
from jax import lax
from jax.experimental import pallas as pl
from jax.experimental.pallas import tpu as pltpu
from jax.sharding import PartitionSpec as P

MESH = pl.DeviceIdType.MESH
HEAD_DIM = 64
ROT = 16
LAYERS = 2
D = 768
FF = 3072
N = 8
TOK = 128
SEQ = 1024
HALF = 384
epsilon = 1e-05
BF = jnp.bfloat16
F32 = jnp.float32
ANY = pl.BlockSpec(memory_space=pl.ANY)


def dot(a, b, dims):
    return lax.dot_general(a, b, (dims, ((), ())), preferred_element_type=F32)


def meet(devices):
    barrier = pltpu.get_barrier_semaphore()
    for device in devices:
        pl.semaphore_signal(barrier, inc=1, device_id=device, device_id_type=MESH)
    pl.semaphore_wait(barrier, len(devices))


def push(src, dst, send, recv, device):
    copy = pltpu.make_async_remote_copy(
        src_ref=src, dst_ref=dst, send_sem=send, recv_sem=recv, device_id=device, device_id_type=MESH
    )
    copy.start()
    return copy


def others(axis, index):
    return [{axis: lax.rem(index + d, N)} for d in range(1, N)]


class Group:
    def __init__(self, axis):
        self.axis = axis
        index = lax.axis_index(axis)
        self.r, self.h = (index % 4, index // 4) if axis == "ctx" else (index // 2, index % 2)
        self.right = {axis: self.slot(1, 0)}
        self.left = {axis: self.slot(3, 0)}
        self.pair = {axis: self.slot(0, 1)}

    def slot(self, dr, dh):
        r, h = lax.rem(self.r + dr, 4), lax.rem(self.h + dh, 2)
        return h * 4 + r if self.axis == "ctx" else r * 2 + h

    def neighbours(self):
        return [self.right, self.left, self.pair]


class Lane:
    def __init__(self, sems):
        self.send, self.recv = sems
        self.copies = []

    def go(self, src, dst, device):
        i = len(self.copies)
        self.copies.append(push(src, dst, self.send.at[i], self.recv.at[i], device))
        return self.copies[-1]

    def finish(self):
        for copy in self.copies:
            copy.wait_send()


def run(*steps):
    live = list(steps)
    while live:
        for one in list(live):
            try:
                next(one)
            except StopIteration:
                live.remove(one)


GATHERS = 8


def gather_steps(lane, group, own, at, cut, rows):
    head, tail = pl.ds(0, cut), pl.ds(cut, rows - cut)
    go = lane.go
    me, twin, far = group.slot(0, 0), group.slot(0, 1), group.slot(2, 0)
    c0 = go(own, at(me), group.right)
    c1 = go(own, at(me), group.left)
    c2 = go(own, at(me), group.pair)
    yield
    c0.wait_recv()
    behind = at(group.slot(3, 0)).at[head]
    c3 = go(behind, behind, group.right)
    yield
    c1.wait_recv()
    ahead = at(group.slot(1, 0)).at[tail]
    c4 = go(ahead, ahead, group.left)
    yield
    c2.wait_recv()
    c5 = go(at(twin), at(twin), group.right)
    c6 = go(at(twin), at(twin), group.left)
    yield
    c3.wait_recv()
    yield
    c4.wait_recv()
    c7 = go(at(far), at(far), group.pair)
    for copy in (c5, c6, c7):
        yield
        copy.wait_recv()


SCATTERS = 11


def scatter_scratch(rows, cut, width):
    return [
        pltpu.VMEM((rows, width), BF),
        pltpu.VMEM((rows, width), BF),
        pltpu.VMEM((cut, width), BF),
        pltpu.VMEM((rows - cut, width), BF),
        pltpu.VMEM((cut, width), BF),
        pltpu.VMEM((rows - cut, width), BF),
        pltpu.VMEM((2, rows, width), BF),
        pltpu.VMEM((2, rows, width), BF),
        pltpu.VMEM((rows, width), BF),
        pltpu.VMEM((rows, width), BF),
    ]


SCRATCHES = 10


def scatter_steps(lane, group, src, cut, rows, buffers, take):
    in_far, st_far, in_right, in_left, st_left, st_right, from_right, from_left, st_pair, from_pair = buffers
    head, tail = pl.ds(0, cut), pl.ds(cut, rows - cut)
    go = lane.go
    opposite = go(src.at[group.slot(2, 1)], in_far, group.pair)
    beside = [
        go(src.at[group.slot(3, 1)], from_right.at[0], group.left),
        go(src.at[group.slot(1, 1)], from_left.at[0], group.right),
    ]
    near = [
        go(src.at[group.slot(3, 0)].at[tail], from_right.at[1].at[tail], group.left),
        go(src.at[group.slot(1, 0)].at[head], from_left.at[1].at[head], group.right),
    ]
    yield
    opposite.wait_recv()
    st_far[...] = (src[group.slot(2, 0)].astype(F32) + in_far[...].astype(F32)).astype(BF)
    far_left = go(st_far.at[head], in_right, group.left)
    far_right = go(st_far.at[tail], in_left, group.right)
    for copy in beside:
        yield
        copy.wait_recv()
    total = src[group.slot(0, 1)].astype(F32) + from_right[0].astype(F32) + from_left[0].astype(F32)
    st_pair[...] = total.astype(BF)
    last = go(st_pair, from_pair, group.pair)
    yield
    far_left.wait_recv()
    st_left[...] = (src[group.slot(3, 0), head].astype(F32) + in_right[...].astype(F32)).astype(BF)
    near.append(go(st_left, from_right.at[1].at[head], group.left))
    yield
    far_right.wait_recv()
    st_right[...] = (src[group.slot(1, 0), tail].astype(F32) + in_left[...].astype(F32)).astype(BF)
    near.append(go(st_right, from_left.at[1].at[tail], group.right))
    for copy in near + [last]:
        yield
        copy.wait_recv()
    total = src[group.slot(0, 0)].astype(F32) + from_right[1].astype(F32) + from_left[1].astype(F32)
    take(total + from_pair[...].astype(F32))


def sems(count):
    return [pltpu.SemaphoreType.DMA((count,)), pltpu.SemaphoreType.DMA((count,))]


def params(collective_id):
    return pltpu.CompilerParams(
        collective_id=collective_id, has_side_effects=True, vmem_limit_bytes=36 * 1024 * 1024
    )


def normalize(stream):
    mean = jnp.mean(stream, axis=-1, keepdims=True)
    centred = stream - mean
    scale = lax.rsqrt(jnp.mean(centred * centred, axis=-1, keepdims=True) + epsilon)
    return centred * scale, scale


def norm_back(stream, grad_normed, gain):
    unit, scale = normalize(stream)
    grad_unit = grad_normed * gain
    first = jnp.mean(grad_unit, axis=-1, keepdims=True)
    second = jnp.mean(grad_unit * unit, axis=-1, keepdims=True)
    grad_gain = jnp.sum(grad_normed * unit, axis=0, keepdims=True)
    grad_shift = jnp.sum(grad_normed, axis=0, keepdims=True)
    return scale * (grad_unit - first - unit * second), grad_gain, grad_shift


PIECE = 64
ROWS = 96 + PIECE
CUT = 80
W_FIRST = ROWS + 16
W_CUT = 96
VMEM = pl.BlockSpec(memory_space=pltpu.VMEM)


def shard_scratch(rows):
    return [
        pltpu.VMEM((N, rows, HALF), BF),
        pltpu.VMEM((N, PIECE, HALF), BF),
        pltpu.VMEM((N, PIECE, HALF), BF),
    ]


SHARD_LANE = N - 1 + 3


def shard_steps(lane, lane_z, fsdp, cs, core, src, cut, rows, scratch, outs, own, kept):
    held, mixed, got = scratch
    c, k = lax.axis_index("ctx"), lax.axis_index("dp")
    first = pltpu.make_async_copy(src.at[k], held.at[fsdp.slot(0, 0)], own.at[0])
    first.start()
    yield from gather_steps(lane_z, fsdp, src.at[k], lambda slot: held.at[slot], cut, rows)
    first.wait()
    low = lax.broadcasted_iota(jnp.int32, (16, HALF), 0) < 8
    for i in range(N):
        own_rows = held[i, pl.ds(96, 16)].astype(F32)
        shared = held[i // 2 * 2 + c // 4, pl.ds(96, 16)].astype(F32)
        mixed[i, pl.ds(0, 16)] = jnp.where(low, own_rows, shared).astype(BF)
        mixed[i, pl.ds(16, 48)] = held[i, pl.ds(112, 48)]
    turn = [lane.go(mixed.at[peer["ctx"]], got.at[c], peer) for peer in cs]
    got[c] = mixed[c]
    cross = []

    def share(part, out, sem):
        cross.append(lane.go(part, out.at[k], core))
        keep = pltpu.make_async_copy(part, out.at[k], sem)
        keep.start()
        kept.append(keep)

    share(held.at[:, pl.ds(0, 96)], outs[0], own.at[1])
    if len(outs) > 2:
        share(held.at[:, pl.ds(ROWS, 16)], outs[2], own.at[2])
    for copy in turn:
        yield
        copy.wait_recv()
    share(got, outs[1], own.at[3])
    for copy in cross:
        yield
        copy.wait_recv()


COLS_SHAPE = jax.ShapeDtypeStruct((2, N, 96, HALF), BF)
PIECES_SHAPE = jax.ShapeDtypeStruct((2, N, PIECE, HALF), BF)


def weights_kernel(
    src, places, x, cols_all, pieces_all, vec_all, places_all, unit_all, *rest
):
    scratch, unit, rest = rest[:3], rest[3], rest[4:]
    lane, lane_z, lane_m, lane_u = (Lane(rest[2 * i : 2 * i + 2]) for i in range(4))
    own, keeps = rest[8], rest[9]
    c = lax.axis_index("ctx")
    fsdp, ctx = Group("fsdp"), Group("ctx")
    cs = others("ctx", c)
    core = {"dp": 1 - lax.axis_index("dp")}
    mark = pltpu.make_async_copy(places, places_all.at[c], keeps.at[0])
    mark.start()
    meet(fsdp.neighbours() + cs + [core])
    kept = [mark]
    marks = [lane_m.go(places, places_all.at[c], peer) for peer in cs]

    def tokens():
        unit[...] = normalize(x[...])[0].astype(BF)
        keep = pltpu.make_async_copy(unit, unit_all.at[c], keeps.at[1])
        keep.start()
        kept.append(keep)
        yield from gather_steps(lane_u, ctx, unit, lambda slot: unit_all.at[slot], TOK // 2, TOK)

    outs = (cols_all, pieces_all, vec_all)
    run(
        shard_steps(lane, lane_z, fsdp, cs, core, src, W_CUT, W_FIRST, scratch, outs, own, kept),
        tokens(),
    )
    for copy in marks:
        copy.wait_recv()
    for each in (lane, lane_z, lane_m, lane_u):
        each.finish()
    for copy in kept:
        copy.wait()


def gather_weights(src, places, x, collective_id):
    tokens = jax.ShapeDtypeStruct((N, TOK, D), BF)
    return pl.pallas_call(
        weights_kernel,
        out_shape=(
            COLS_SHAPE,
            PIECES_SHAPE,
            jax.ShapeDtypeStruct((2, N, 16, HALF), BF),
            jax.ShapeDtypeStruct((N,) + places.shape, places.dtype),
            tokens,
        ),
        in_specs=[ANY] * 2 + [VMEM],
        out_specs=[ANY] * 5,
        scratch_shapes=shard_scratch(W_FIRST)
        + [pltpu.VMEM((TOK, D), BF)]
        + sems(SHARD_LANE)
        + sems(GATHERS)
        + sems(N - 1)
        + sems(GATHERS)
        + [pltpu.SemaphoreType.DMA((4,)), pltpu.SemaphoreType.DMA((2,))],
        compiler_params=params(collective_id),
    )(src, places, x)


def marks_of(places):
    frequency = 10000.0 ** (-2.0 * jnp.arange(ROT // 2, dtype=F32) / ROT)
    where = places.astype(F32).reshape(1, -1)
    angles = frequency[:, None] * where
    return jnp.concatenate([jnp.cos(angles), jnp.sin(angles), jnp.broadcast_to(where, angles.shape)], axis=0)


def prepare_kernel(marks, vectors, tables, col, rows_out):
    zero = jnp.zeros((8, TOK), F32)
    one = zero + 1.0
    for i in range(N):
        cosine, sine, where = marks[i, 0:8], marks[i, 8:16], marks[i, 16:24]
        rows = pl.ds(i * TOK, TOK)
        own = [cosine, cosine] + [one] * 6
        left = [zero, sine] + [zero] * 6
        right = [-sine, zero] + [zero] * 6
        for t, tiles in enumerate((own, left, right)):
            tables[t, rows] = jnp.concatenate(tiles + tiles, axis=0).T
        col[rows] = jnp.concatenate([where] * 16, axis=0).T

    c = lax.axis_index("ctx")
    head_a, head_b = 3 * (c // 2) + 2 * (c % 2), 3 * (c // 2) + 1

    def place(values, column, width, cut):
        shard = jnp.zeros((1, width), jnp.int32)
        for t in range(1, N):
            shard = shard + jnp.where(column >= cut * t, 1, 0)
        inner = column - cut * shard
        pick = lax.broadcasted_iota(jnp.int32, (HALF, width), 0) == inner
        spread_ = dot(values.astype(BF), jnp.where(pick, 1.0, 0.0).astype(BF), ((1,), (0,)))
        mine = lax.broadcasted_iota(jnp.int32, (N, width), 0) == shard
        return jnp.sum(jnp.where(mine, spread_, 0.0), axis=0, keepdims=True)

    lanes = lax.broadcasted_iota(jnp.int32, (1, D), 1)
    lane = lax.broadcasted_iota(jnp.int32, (1, HALF), 1)
    third = jnp.where(lane >= 128, 1, 0) + jnp.where(lane >= 256, 1, 0)
    within = lane - 128 * third
    second = jnp.where(within >= HEAD_DIM, 1, 0)
    head = jnp.where(second == 1, head_b, head_a)
    column = 192 * head + HEAD_DIM * third + (within - HEAD_DIM * second)
    for layer in range(LAYERS):
        shards = [vectors[layer, i].astype(F32) for i in range(N)]

        def row(r):
            return jnp.concatenate([one_shard[r : r + 1] for one_shard in shards], axis=0)

        rows_out[layer, 0:1] = place(row(2), lanes, D, 96)
        rows_out[layer, 1:2] = place(row(3), lanes, D, 96)
        rows_out[layer, 2:3] = place(row(4), lanes, D, 96) + place(row(5), lanes, D, 96)
        rows_out[layer, 3:4, pl.ds(0, HALF)] = place(row(0), column, HALF, 288)
        rows_out[layer, 3:4, pl.ds(HALF, HALF)] = vectors[layer, c].astype(F32)[1:2]
        rows_out[layer, 4:8] = jnp.zeros((4, D), F32)


def prepare(marks, vectors):
    return pl.pallas_call(
        prepare_kernel,
        out_shape=(
            jax.ShapeDtypeStruct((3, SEQ, 128), F32),
            jax.ShapeDtypeStruct((SEQ, 128), F32),
            jax.ShapeDtypeStruct((LAYERS, 8, D), F32),
        ),
        in_specs=[VMEM] * 2,
        out_specs=[VMEM] * 3,
        compiler_params=pltpu.CompilerParams(vmem_limit_bytes=48 * 1024 * 1024),
    )(marks, vectors)


BLOCK = 256
BLOCKS = SEQ // BLOCK


def unit_rows(b):
    s = lax.axis_index("ctx") % 2
    start = jnp.where(b < BLOCKS, b * BLOCK, s * (SEQ // 2) + (b - BLOCKS) * BLOCK)
    start = pl.multiple_of(start, BLOCK)
    lanes = lax.broadcasted_iota(jnp.int32, (BLOCK, 2 * HEAD_DIM), 1) // HEAD_DIM
    return start, lanes == jnp.where(b < BLOCKS, 0, 1)


def mix_rows(pieces, w_mix):
    for h in range(2):
        cols = pl.ds(HALF * h, HALF)
        rows = [pieces[h, j, pl.ds(0, 16)].astype(F32) for j in range(N)]
        heads = [r[:8] for r in rows] + [r[8:] for r in rows]
        w_mix[pl.ds(0, 128), cols] = jnp.concatenate(heads, axis=0).astype(BF)
        for j in range(N):
            w_mix[pl.ds(128 + 48 * j, 48), cols] = pieces[h, j, pl.ds(16, 48)]


def forward_steps(
    unit, vectors, w_cat, pieces, col, row, tables,
    branch, normed, query, key, value, slope, mixed, lse, w_mix, turned,
):
    mix_rows(pieces, w_mix)

    @pl.loop(0, BLOCKS)
    def _(i):
        rows = pl.ds(pl.multiple_of(i * BLOCK, BLOCK), BLOCK)
        low = (unit[rows].astype(F32) * vectors[0:1] + vectors[1:2]).astype(BF)
        normed[rows] = low
        heads = dot(low, w_cat[0], ((1,), (0,))) + vectors[3:4, :HALF]

        def rotate(values):
            return (
                values * tables[0, rows]
                + pltpu.roll(values, 8, axis=1) * tables[1, rows]
                + pltpu.roll(values, 120, axis=1) * tables[2, rows]
            )

        query[rows] = (rotate(heads[:, :128]) * HEAD_DIM ** (-0.5)).astype(BF)
        key[rows] = rotate(heads[:, 128:256]).astype(BF)
        value[rows] = heads[:, 256:].astype(BF)
        pre = dot(low, w_cat[1], ((1,), (0,))) + vectors[3:4, HALF:]
        cdf = 0.5 * (1.0 + lax.erf(pre * 0.5**0.5))
        mixed[rows, pl.ds(128, HALF)] = (pre * cdf).astype(BF)
        mixed[rows, pl.ds(0, 128)] = jnp.zeros((BLOCK, 128), BF)
        slope[rows] = cdf + pre * (jnp.exp(-0.5 * pre * pre) * 0.3989422804014327)

    turned[...] = value[...].astype(F32).T.astype(BF)
    yield
    for n in range(3):

        @pl.loop(2 * n, 2 * n + 2)
        def _(b):
            start, mask = unit_rows(b)
            rows = pl.ds(start, BLOCK)
            q = jnp.where(mask, query[rows].astype(F32), 0.0).astype(BF)
            scores = dot(key[...], q, ((1,), (1,)))
            seen = jnp.concatenate([col[...], col[...]], axis=1) <= row[pl.ds(start // BLOCK, 1)]
            scores = jnp.where(seen, scores, -jnp.inf)
            top = jnp.max(scores, axis=0, keepdims=True)
            expos = jnp.exp(scores - top)
            total = jnp.sum(expos, axis=0, keepdims=True)
            lse[pl.ds(b, 1)] = top + jnp.log(total)
            probs = (expos * (1.0 / total)).astype(BF)
            out = dot(turned[...], probs, ((1,), (0,))).T
            mixed[rows, pl.ds(0, 128)] = jnp.where(mask, out, mixed[rows, pl.ds(0, 128)].astype(F32)).astype(BF)

        yield
    for i in range(N):
        rows = pl.ds(i * TOK, TOK)
        branch[i] = dot(mixed[rows], w_mix[...], ((1,), (0,))).astype(BF)


def forward_shapes():
    shape = jax.ShapeDtypeStruct
    return (
        shape((N, TOK, D), BF),
        shape((SEQ, D), BF),
        shape((SEQ, 128), BF),
        shape((SEQ, 128), BF),
        shape((SEQ, 128), BF),
        shape((SEQ, HALF), F32),
        shape((SEQ, 512), BF),
        shape((8, BLOCK), F32),
        shape((512, D), BF),
    )


FORWARDS = 9


def local_params():
    return pltpu.CompilerParams(vmem_limit_bytes=36 * 1024 * 1024)


def forward_kernel(*refs):
    run(forward_steps(*refs))


def forward(*args):
    return pl.pallas_call(
        forward_kernel,
        out_shape=forward_shapes(),
        in_specs=[VMEM] * len(args),
        out_specs=[VMEM] * FORWARDS,
        scratch_shapes=[pltpu.VMEM((128, SEQ), BF)],
        compiler_params=local_params(),
    )(*args)


def forward_between_kernel(*refs):
    args, (x, cot, src), refs = refs[:7], refs[7:10], refs[10:]
    outs, refs = refs[:FORWARDS], refs[FORWARDS:]
    (x_next, unit_all, low_all, cols_all, pieces_all), refs = refs[:5], refs[5:]
    turned, unit, low_g, scratch, rest = refs[0], refs[1], refs[2], refs[3:6], refs[6:]
    buffers, rest = rest[:SCRATCHES], rest[SCRATCHES:]
    lane, lane_u, lane_g, lane_w, lane_z = (Lane(rest[2 * i : 2 * i + 2]) for i in range(5))
    own, keeps = rest[10], rest[11]
    ctx, fsdp = Group("ctx"), Group("fsdp")
    cs = others("ctx", lax.axis_index("ctx"))
    core = {"dp": 1 - lax.axis_index("dp")}
    meet(fsdp.neighbours() + cs + [core])
    kept = []
    branch, vectors = outs[0], args[1]

    def tokens():
        yield from forward_steps(*args, *outs, turned)

        def take(total):
            x_next[...] = x[...] + (total + vectors[2:3])

        yield from scatter_steps(lane, ctx, branch, TOK // 2, TOK, buffers, take)
        unit[...] = normalize(x_next[...])[0].astype(BF)
        keep = pltpu.make_async_copy(unit, unit_all.at[ctx.slot(0, 0)], keeps.at[0])
        keep.start()
        kept.append(keep)
        yield from gather_steps(lane_u, ctx, unit, lambda slot: unit_all.at[slot], TOK // 2, TOK)

    def later():
        low_g[...] = cot[...].astype(BF)
        keep = pltpu.make_async_copy(low_g, low_all.at[ctx.slot(0, 0)], keeps.at[1])
        keep.start()
        kept.append(keep)
        yield from gather_steps(lane_g, ctx, low_g, lambda slot: low_all.at[slot], TOK // 2, TOK)

    outs_w = (cols_all, pieces_all)
    run(
        shard_steps(lane_w, lane_z, fsdp, cs, core, src, CUT, ROWS, scratch, outs_w, own, kept),
        later(),
        tokens(),
    )
    for each in (lane, lane_u, lane_g, lane_w, lane_z):
        each.finish()
    for copy in kept:
        copy.wait()


def forward_between(args, x, cot, src, collective_id):
    tokens = jax.ShapeDtypeStruct((N, TOK, D), BF)
    return pl.pallas_call(
        forward_between_kernel,
        out_shape=forward_shapes()
        + (jax.ShapeDtypeStruct((TOK, D), F32), tokens, tokens, COLS_SHAPE, PIECES_SHAPE),
        in_specs=[VMEM] * 9 + [ANY],
        out_specs=[VMEM] * (FORWARDS + 1) + [ANY] * 4,
        scratch_shapes=[
            pltpu.VMEM((128, SEQ), BF),
            pltpu.VMEM((TOK, D), BF),
            pltpu.VMEM((TOK, D), BF),
        ]
        + shard_scratch(ROWS)
        + scatter_scratch(TOK, TOK // 2, D)
        + sems(SCATTERS)
        + sems(GATHERS)
        + sems(GATHERS)
        + sems(SHARD_LANE)
        + sems(GATHERS)
        + [pltpu.SemaphoreType.DMA((4,)), pltpu.SemaphoreType.DMA((2,))],
        compiler_params=params(collective_id),
    )(*args, x, cot, src)


BACK_ARGS = 12


def backward_scratch():
    return [
        pltpu.VMEM((SEQ, 128), BF),
        pltpu.VMEM((SEQ, D), BF),
        pltpu.VMEM((SEQ, 128), F32),
        pltpu.VMEM((SEQ, 128), F32),
        pltpu.VMEM((SEQ, 128), F32),
        pltpu.VMEM((128, SEQ), BF),
        pltpu.VMEM((D, D), F32),
        pltpu.VMEM((N, TOK, D), BF),
        pltpu.VMEM((2, N, 96, HALF), BF),
        pltpu.VMEM((2, N, PIECE, HALF), BF),
    ]


BACKS = 10


def backward_steps(
    ready, low, w_cat, normed, query, key, value, slope, mixed, lse, w_mix, col, row, tables, grad_b,
    grad_att, grad_pre, dq, dk, dv, turned, big, grad_normed, part_a, part_b,
):
    @pl.loop(0, 2)
    def _(i):
        cols = pl.ds(pl.multiple_of(i * BLOCK, BLOCK), BLOCK)
        big[cols] = dot(mixed[:, cols], low[...], ((0,), (0,)))

    for j in range(N):
        for h in range(2):
            at = slice(HALF * h, HALF * h + HALF)
            first = big[8 * j : 8 * j + 8, at]
            second = big[64 + 8 * j : 64 + 8 * j + 8, at]
            part_b[h, j, pl.ds(0, 16)] = jnp.concatenate([first, second], axis=0).astype(BF)
            part_b[h, j, pl.ds(16, 48)] = big[128 + 48 * j : 176 + 48 * j, at].astype(BF)
    ready.add("b")
    yield

    @pl.loop(0, BLOCKS)
    def _(i):
        rows = pl.ds(pl.multiple_of(i * BLOCK, BLOCK), BLOCK)
        back = dot(low[rows], w_mix[...], ((1,), (1,)))
        grad_att[rows] = back[:, :128].astype(BF)
        grad_pre[rows, pl.ds(HALF, HALF)] = (back[:, 128:] * slope[rows]).astype(BF)

    turned[...] = key[...].astype(F32).T.astype(BF)
    dq[...] = jnp.zeros((SEQ, 128), F32)
    dk[...] = jnp.zeros((SEQ, 128), F32)
    dv[...] = jnp.zeros((SEQ, 128), F32)
    yield
    for n in range(3):

        @pl.loop(2 * n, 2 * n + 2)
        def _(b):
            start, mask = unit_rows(b)
            rows = pl.ds(start, BLOCK)
            q = jnp.where(mask, query[rows].astype(F32), 0.0).astype(BF)
            g = jnp.where(mask, grad_att[rows].astype(F32), 0.0).astype(BF)
            scores = dot(key[...], q, ((1,), (1,)))
            seen = jnp.concatenate([col[...], col[...]], axis=1) <= row[pl.ds(start // BLOCK, 1)]
            probs = jnp.exp(jnp.where(seen, scores, -jnp.inf) - lse[pl.ds(b, 1)])
            grad_probs = dot(value[...], g, ((1,), (1,)))
            mean = jnp.sum(probs * grad_probs, axis=0, keepdims=True)
            grad_scores = (probs * (grad_probs - mean)).astype(BF)
            dq[rows] = jnp.where(mask, dot(turned[...], grad_scores, ((1,), (0,))).T, dq[rows])
            dk[...] += dot(grad_scores, q, ((1,), (0,)))
            dv[...] += dot(probs.astype(BF), g, ((1,), (0,)))

        yield
    grad_b[...] = jnp.zeros((1, D), F32)

    @pl.loop(0, N)
    def _(i):
        rows = pl.ds(pl.multiple_of(i * TOK, TOK), TOK)

        def rotate_back(grads):
            return (
                grads * tables[0, rows]
                + pltpu.roll(grads * tables[1, rows], 120, axis=1)
                + pltpu.roll(grads * tables[2, rows], 8, axis=1)
            )

        grad_pre[rows, pl.ds(0, 128)] = rotate_back(dq[rows] * HEAD_DIM ** (-0.5)).astype(BF)
        grad_pre[rows, pl.ds(128, 128)] = rotate_back(dk[rows]).astype(BF)
        grad_pre[rows, pl.ds(256, 128)] = dv[rows].astype(BF)
        block = grad_pre[rows]
        grad_b[...] += jnp.sum(block.astype(F32), axis=0, keepdims=True)
        grad_normed[i] = (
            dot(block[:, :HALF], w_cat[0], ((1,), (1,))) + dot(block[:, HALF:], w_cat[1], ((1,), (1,)))
        ).astype(BF)

    ready.add("normed")
    yield

    @pl.loop(0, D // BLOCK)
    def _(i):
        cols = pl.ds(pl.multiple_of(i * BLOCK, BLOCK), BLOCK)
        big[cols] = dot(normed[:, cols], grad_pre[...], ((0,), (0,)))

    for f in range(N):
        for h in range(2):
            part_a[h, f] = big[96 * f : 96 * f + 96, HALF * h : HALF * h + HALF].astype(BF)
    ready.add("a")


def grads_scratch():
    return [
        pltpu.VMEM((N, 96, HALF), BF),
        pltpu.VMEM((N, PIECE, HALF), BF),
        pltpu.VMEM((N, PIECE, HALF), BF),
        pltpu.VMEM((N, ROWS, HALF), BF),
    ] + scatter_scratch(ROWS, CUT, HALF)


GRADS = 4 + SCRATCHES


def grads_steps(ready, lane, lane_z, fsdp, cs, core, part_a, part_b, scratch, take):
    their_a, their_b, got, blocks = scratch[:4]
    c, k = lax.axis_index("ctx"), lax.axis_index("dp")
    while "b" not in ready:
        yield
    first_b = lane.go(part_b.at[1 - k], their_b, core)
    yield
    first_b.wait_recv()
    for i in range(N):
        their_b[i] = (part_b[k, i].astype(F32) + their_b[i].astype(F32)).astype(BF)
    turn = [lane.go(their_b.at[peer["ctx"]], got.at[c], peer) for peer in cs]
    got[c] = their_b[c]
    while "a" not in ready:
        yield
    first_a = lane.go(part_a.at[1 - k], their_a, core)
    for copy in turn:
        copy.wait_recv()
    low = lax.broadcasted_iota(jnp.int32, (16, HALF), 0) < 8
    for i in range(N):
        rows = got[i, pl.ds(0, 16)].astype(F32)
        pair = got[i + 1 - 2 * (i % 2), pl.ds(0, 16)].astype(F32)
        blocks[i, pl.ds(96, 16)] = jnp.where(low, rows, rows + pair).astype(BF)
        blocks[i, pl.ds(112, 48)] = got[i, pl.ds(16, 48)]
    yield
    first_a.wait_recv()
    for i in range(N):
        blocks[i, pl.ds(0, 96)] = (part_a[k, i].astype(F32) + their_a[i].astype(F32)).astype(BF)
    yield from scatter_steps(lane_z, fsdp, blocks, CUT, ROWS, scratch[4:], take)


def turn_kernel(*refs):
    (low, *args), refs = refs[:13], refs[13:]
    (x, grad, vectors, out_parts, bias), refs = refs[:5], refs[5:]
    (outputs, grad_next, low_all, vecs, share), refs = refs[:5], refs[5:]
    (low_g, grad_b), refs = refs[:2], refs[2:]
    back, refs = refs[:BACKS], refs[BACKS:]
    buffers, refs = refs[:SCRATCHES], refs[SCRATCHES:]
    buffers_o, refs = refs[:SCRATCHES], refs[SCRATCHES:]
    scratch, rest = refs[:GRADS], refs[GRADS:]
    lane, lane_g, lane_w, lane_z, lane_o = (Lane(rest[2 * i : 2 * i + 2]) for i in range(5))
    keep_sem = rest[10]
    ctx, fsdp = Group("ctx"), Group("fsdp")
    cs = others("ctx", lax.axis_index("ctx"))
    core = {"dp": 1 - lax.axis_index("dp")}
    meet(cs + fsdp.neighbours() + [core])
    kept, ready = [], set()

    def tokens():
        def take(total):
            back_, grad_gain, grad_shift = norm_back(x[...], total, vectors[0:1])
            grad_next[...] = grad[...] + back_
            rounded = grad[...].astype(BF).astype(F32)
            vecs[pl.ds(0, 1)] = jnp.sum(rounded, axis=0, keepdims=True)
            vecs[pl.ds(1, 1)] = grad_gain
            vecs[pl.ds(2, 1)] = grad_shift
            vecs[pl.ds(3, 1)] = grad_b[...]
            vecs[pl.ds(4, 4)] = jnp.zeros((4, D), F32)

        while "normed" not in ready:
            yield
        yield from scatter_steps(lane, ctx, back[7], TOK // 2, TOK, buffers, take)
        low_g[...] = grad_next[...].astype(BF)
        keep = pltpu.make_async_copy(low_g, low_all.at[ctx.slot(0, 0)], keep_sem)
        keep.start()
        kept.append(keep)
        yield from gather_steps(lane_g, ctx, low_g, lambda slot: low_all.at[slot], TOK // 2, TOK)

    def weights():
        def take(total):
            share[...] = total.astype(BF)

        yield from grads_steps(ready, lane_w, lane_z, fsdp, cs, core, back[8], back[9], scratch, take)

    def ends():
        def take(total):
            outputs[...] = x[...] + (total + bias[2:3])

        yield from scatter_steps(lane_o, ctx, out_parts, TOK // 2, TOK, buffers_o, take)

    run(ends(), backward_steps(ready, low, *args, grad_b, *back), tokens(), weights())
    for each in (lane, lane_g, lane_w, lane_z, lane_o):
        each.finish()
    for copy in kept:
        copy.wait()


def turn(args, x, grad, vectors, out_parts, collective_id):
    tokens = jax.ShapeDtypeStruct((TOK, D), F32)
    return pl.pallas_call(
        turn_kernel,
        out_shape=(
            tokens,
            tokens,
            jax.ShapeDtypeStruct((N, TOK, D), BF),
            jax.ShapeDtypeStruct((8, D), F32),
            jax.ShapeDtypeStruct((ROWS, HALF), BF),
        ),
        in_specs=[VMEM] * 18,
        out_specs=(VMEM, VMEM, ANY, VMEM, VMEM),
        scratch_shapes=[pltpu.VMEM((TOK, D), BF), pltpu.VMEM((1, D), F32)]
        + backward_scratch()
        + scatter_scratch(TOK, TOK // 2, D)
        + scatter_scratch(TOK, TOK // 2, D)
        + grads_scratch()
        + sems(SCATTERS)
        + sems(GATHERS)
        + sems(2 + N - 1)
        + sems(SCATTERS)
        + sems(SCATTERS)
        + [pltpu.SemaphoreType.DMA],
        compiler_params=params(collective_id),
    )(*args, x, grad, vectors, out_parts, vectors)


FIRST_ROWS = ROWS + 16


def last_kernel(*refs):
    (low, *args), refs = refs[:13], refs[13:]
    (x, grad, vectors, vecs, share), refs = refs[:5], refs[5:]
    (grad_next, out_first, out_last), refs = refs[:3], refs[3:]
    (both, v_mine, v_their, v_all, grad_b), refs = refs[:5], refs[5:]
    back, refs = refs[:BACKS], refs[BACKS:]
    buffers, refs = refs[:SCRATCHES], refs[SCRATCHES:]
    scratch, rest = refs[:GRADS], refs[GRADS:]
    lane, lane_w, lane_z, lane_v, lane_x, lane_s = (Lane(rest[2 * i : 2 * i + 2]) for i in range(6))
    keeps = rest[12]
    c, f, k = lax.axis_index("ctx"), lax.axis_index("fsdp"), lax.axis_index("dp")
    ctx, fsdp = Group("ctx"), Group("fsdp")
    cs, fs = others("ctx", c), others("fsdp", f)
    core = {"dp": 1 - k}
    meet(cs + fs + [core])
    ready = set()

    def tokens():
        def take(total):
            back_, grad_gain, grad_shift = norm_back(x[...], total, vectors[0:1])
            grad_next[...] = grad[...] + back_
            rounded = grad[...].astype(BF).astype(F32)
            branch = jnp.sum(rounded, axis=0, keepdims=True)
            mine = [vecs[...], branch, grad_gain, grad_shift, grad_b[...], jnp.zeros((4, D), F32)]
            mine = jnp.concatenate(mine, axis=0)
            v_mine[0] = mine[:, :HALF].astype(BF)
            v_mine[1] = mine[:, HALF:].astype(BF)

        while "normed" not in ready:
            yield
        yield from scatter_steps(lane, ctx, back[7], TOK // 2, TOK, buffers, take)
        cross = lane_v.go(v_mine.at[1 - k], v_their, core)
        yield
        cross.wait_recv()
        v_all[f] = (v_mine[k].astype(F32) + v_their[...].astype(F32)).astype(BF)
        copies = [lane_v.go(v_all.at[f], v_all.at[f], peer) for peer in fs]
        yield
        for copy in copies:
            copy.wait_recv()
        total = v_all[0].astype(F32)
        for i in range(1, N):
            total = total + v_all[i].astype(F32)
        both[pl.ds(ROWS, 16)] = total.astype(BF)

    def weights():
        def take(total):
            both[pl.ds(0, ROWS)] = total.astype(BF)

        yield from grads_steps(ready, lane_w, lane_z, fsdp, cs, core, back[8], back[9], scratch, take)

    kept = []

    def older():
        keep = pltpu.make_async_copy(share, out_last.at[k, c], keeps.at[0])
        keep.start()
        kept.append(keep)
        yield from gather_steps(lane_s, ctx, share, lambda slot: out_last.at[k, slot], CUT, ROWS)
        keep.wait()
        copy = lane_s.go(out_last.at[k], out_last.at[k], core)
        yield
        copy.wait_recv()

    run(older(), backward_steps(ready, low, *args, grad_b, *back), tokens(), weights())
    keep = pltpu.make_async_copy(both, out_first.at[k, c], keeps.at[1])
    keep.start()
    run(gather_steps(lane_x, ctx, both, lambda slot: out_first.at[k, slot], W_CUT, FIRST_ROWS))
    keep.wait()
    lane_x.go(out_first.at[k], out_first.at[k], core).wait_recv()
    for each in (lane, lane_w, lane_z, lane_v, lane_x, lane_s):
        each.finish()


def last(args, x, grad, vectors, vecs, share, collective_id):
    return pl.pallas_call(
        last_kernel,
        out_shape=(
            jax.ShapeDtypeStruct((TOK, D), F32),
            jax.ShapeDtypeStruct((2, N, FIRST_ROWS, HALF), BF),
            jax.ShapeDtypeStruct((2, N, ROWS, HALF), BF),
        ),
        in_specs=[VMEM] * 18,
        out_specs=(VMEM, ANY, ANY),
        scratch_shapes=[
            pltpu.VMEM((FIRST_ROWS, HALF), BF),
            pltpu.VMEM((2, 16, HALF), BF),
            pltpu.VMEM((16, HALF), BF),
            pltpu.VMEM((N, 16, HALF), BF),
            pltpu.VMEM((1, D), F32),
        ]
        + backward_scratch()
        + scatter_scratch(TOK, TOK // 2, D)
        + grads_scratch()
        + sems(SCATTERS)
        + sems(2 + N - 1)
        + sems(SCATTERS)
        + sems(N)
        + sems(GATHERS + 1)
        + sems(GATHERS + 1)
        + [pltpu.SemaphoreType.DMA((2,))],
        compiler_params=params(collective_id),
    )(*args, x, grad, vectors, vecs, share)


def spread_kernel(got_first, got_last, g_qkv, g_out, g_up, g_down):
    odd = lax.axis_index("fsdp") % 2
    for layer in range(LAYERS):
        got, base = (got_first, got_last)[layer], 0

        def heads(i, got=got, base=base):
            return got[0, i, pl.ds(base, 96)].astype(F32)

        chunks = []
        for p in range(4):
            one, two = heads(2 * p), heads(2 * p + 1)
            both = one + two
            for values, lane in ((one, 0), (both, HEAD_DIM), (two, 0)):
                chunks += [values[:, 128 * i + lane : 128 * i + lane + HEAD_DIM] for i in range(3)]
        for i in range(len(chunks) // 2):
            g_qkv[layer, :, pl.ds(128 * i, 128)] = jnp.concatenate(chunks[2 * i : 2 * i + 2], axis=1)
        for i in range(N):
            g_up[layer, :, pl.ds(HALF * i, HALF)] = got[1, i, pl.ds(base, 96)].astype(F32)
            for h in range(2):
                cols = pl.ds(HALF * h, HALF)
                g_down[layer, pl.ds(48 * i, 48), cols] = got[h, i, pl.ds(base + 112, 48)].astype(F32)
        for h in range(2):
            cols = pl.ds(HALF * h, HALF)
            rows = [got[h, i, pl.ds(base + 96, 16)].astype(F32) for i in range(N)]
            first = [r[:8] for r in rows]
            even = jnp.concatenate(first + [r[8:] for r in rows[:4]], axis=0)
            uneven = jnp.concatenate([r[8:] for r in rows[4:]] + first, axis=0)
            g_out[layer, :, cols] = jnp.where(odd == 0, even, uneven)


def spread(got_first, got_last):
    shape = jax.ShapeDtypeStruct
    return pl.pallas_call(
        spread_kernel,
        out_shape=(
            shape((LAYERS, 96, 3 * D), F32),
            shape((LAYERS, 96, D), F32),
            shape((LAYERS, 96, FF), F32),
            shape((LAYERS, HALF, D), F32),
        ),
        in_specs=[VMEM] * 2,
        out_specs=[VMEM] * 4,
        compiler_params=local_params(),
    )(got_first, got_last)


def body(
    inputs, positions, cotangent, w_qkv, b_qkv, w_out, b_out, w_up, b_up, w_down, b_down, ln_gain, ln_bias
):
    c = lax.axis_index("ctx")
    p, s = c // 2, lax.rem(c, 2)
    head_a, head_b = 3 * p + 2 * s, 3 * p + 1

    def heads_cols(w):
        grouped = w.reshape(w.shape[:-1] + (12, 3, HEAD_DIM))
        axis = grouped.ndim - 3
        both = jnp.concatenate(
            [
                lax.dynamic_slice_in_dim(grouped, head_a, 1, axis=axis),
                lax.dynamic_slice_in_dim(grouped, head_b, 1, axis=axis),
            ],
            axis=axis,
        )
        return jnp.swapaxes(both, axis, axis + 1).reshape(w.shape[:-1] + (HALF,))

    def hidden_cols(w):
        return lax.dynamic_slice_in_dim(w, c * HALF, HALF, axis=w.ndim - 1)

    f = lax.axis_index("fsdp")
    f_s = lax.rem(f, 2)

    def piece(w, start, count):
        return lax.dynamic_slice_in_dim(w, start, count, axis=1)

    cols = jnp.concatenate([heads_cols(w_qkv), hidden_cols(w_up)], axis=-1)
    first_rows = piece(w_out, jnp.where(f_s == 0, 0, 32) + 8 * c, 8)
    shared_rows = piece(w_out, jnp.where(f_s == 0, 64, -32) + 8 * jnp.where(f_s == 0, c % 4, c), 8)
    down_rows = piece(w_down, 48 * c, 48)
    by_layer = jnp.concatenate([cols, first_rows, shared_rows, down_rows], axis=1)
    def wide(vector):
        return jnp.pad(vector, ((0, 0), (0, HALF - vector.shape[1])))

    vec = jnp.stack([wide(v) for v in (b_qkv, b_up, ln_gain, ln_bias, b_out, b_down)], axis=1)
    vec = jnp.pad(vec, ((0, 0), (0, 10), (0, 0)))
    src = [jnp.stack([one[:, :HALF], one[:, HALF:]]) for one in (by_layer[0], by_layer[1])]
    src[0] = jnp.concatenate([src[0], vec], axis=1)
    stream, cot = inputs[0], cotangent[0]
    cols, pieces, vec_all, marks, unit = gather_weights(src[0], marks_of(positions), stream, 1)
    tables, col, vectors = prepare(marks, vec_all)
    row = marks[:, 16].reshape(BLOCKS, BLOCK)
    w_first = cols.reshape(2, D, HALF)
    branch, *kept_first, x_last, unit, low_last, cols, pieces_last = forward_between(
        (unit.reshape(SEQ, D), vectors[0], w_first, pieces, col, row, tables), stream, cot, src[1], 2
    )
    w_last = cols.reshape(2, D, HALF)
    branch, *kept_last = forward(
        unit.reshape(SEQ, D), vectors[1], w_last, pieces_last, col, row, tables
    )
    outputs, grad, low, vecs, share = turn(
        (low_last.reshape(SEQ, D), w_last, *kept_last, col, row, tables), x_last, cot, vectors[1], branch, 3
    )
    grad, got_first, got_last = last(
        (low.reshape(SEQ, D), w_first, *kept_first, col, row, tables), stream, grad, vectors[0], vecs, share, 4
    )
    g_qkv, g_out, g_up, g_down = spread(got_first, got_last)

    rows = jnp.concatenate([got_first[0, :, ROWS:], got_first[1, :, ROWS:]], axis=-1).astype(F32)
    summed = jnp.sum(rows, axis=0)

    def cut(vector, width):
        return lax.dynamic_slice_in_dim(vector, f * width, width, axis=vector.ndim - 1)

    def own_vectors(biases):
        qkv = biases[:, :HALF].reshape(4, 2, 3, 2, HEAD_DIM)
        shared = qkv[:, 0, :, 1] + qkv[:, 1, :, 1]
        qkv = jnp.stack([qkv[:, 0, :, 0], shared, qkv[:, 1, :, 0]], axis=1).reshape(3 * D)
        up = lax.dynamic_index_in_dim(biases[:, HALF:], f, axis=0, keepdims=False)
        return cut(qkv, 288), up

    pairs = [own_vectors(rows[:, 11]), own_vectors(rows[:, 3])]
    g_b_qkv = jnp.stack([pair[0] for pair in pairs])
    g_b_up = jnp.stack([pair[1] for pair in pairs])
    g_branch, g_gain, g_shift = (cut(jnp.stack([summed[8 + i], summed[i]]), 96) for i in range(3))
    return (
        outputs[None], grad[None], g_qkv, g_b_qkv, g_out, g_branch, g_up, g_b_up, g_down, g_branch, g_gain, g_shift,
    )


def solution(mesh):
    seqs = ("dp", "fsdp")
    whole = P(None, "fsdp", None)
    row = P(None, "fsdp")
    in_specs = (
        P(seqs, "ctx", None), P(seqs, "ctx"), P(seqs, "ctx", None),
        whole, row, whole, row, whole, row, whole, row, row, row,
    )
    out_specs = (
        P(seqs, "ctx", None), P(seqs, "ctx", None),
        whole, row, whole, row, whole, row, whole, row, row, row,
    )
    return jax.shard_map(body, mesh=mesh, in_specs=in_specs, out_specs=out_specs, check_vma=False)
```

```python
import functools

import jax
import jax.numpy as jnp
from jax import lax
from jax.experimental import pallas as pl
from jax.experimental.pallas import tpu as pltpu
from jax.sharding import PartitionSpec as P

MESH = pl.DeviceIdType.MESH
HEAD_DIM = 64
ROT = 16
LAYERS = 2
D = 768
FF = 3072
N = 8
TOK = 128
SEQ = 1024
HALF = 384
epsilon = 1e-05
BF = jnp.bfloat16
F32 = jnp.float32
ANY = pl.BlockSpec(memory_space=pl.ANY)


def dot(a, b, dims):
    return lax.dot_general(a, b, (dims, ((), ())), preferred_element_type=F32)


def meet(devices):
    barrier = pltpu.get_barrier_semaphore()
    for device in devices:
        pl.semaphore_signal(barrier, inc=1, device_id=device, device_id_type=MESH)
    pl.semaphore_wait(barrier, len(devices))


def push(src, dst, send, recv, device):
    copy = pltpu.make_async_remote_copy(
        src_ref=src, dst_ref=dst, send_sem=send, recv_sem=recv, device_id=device, device_id_type=MESH
    )
    copy.start()
    return copy


def others(axis, index):
    return [{axis: lax.rem(index + d, N)} for d in range(1, N)]


class Group:
    def __init__(self, axis):
        self.axis = axis
        index = lax.axis_index(axis)
        self.r, self.h = (index % 4, index // 4) if axis == "ctx" else (index // 2, index % 2)
        self.right = {axis: self.slot(1, 0)}
        self.left = {axis: self.slot(3, 0)}
        self.pair = {axis: self.slot(0, 1)}

    def slot(self, dr, dh):
        r, h = lax.rem(self.r + dr, 4), lax.rem(self.h + dh, 2)
        return h * 4 + r if self.axis == "ctx" else r * 2 + h

    def neighbours(self):
        return [self.right, self.left, self.pair]


class Lane:
    def __init__(self, sems):
        self.send, self.recv = sems
        self.copies = []

    def go(self, src, dst, device):
        i = len(self.copies)
        self.copies.append(push(src, dst, self.send.at[i], self.recv.at[i], device))
        return self.copies[-1]

    def finish(self):
        for copy in self.copies:
            copy.wait_send()


def run(*steps):
    live = list(steps)
    while live:
        for one in list(live):
            try:
                next(one)
            except StopIteration:
                live.remove(one)


GATHERS = 8


def gather_steps(lane, group, own, at, cut, rows):
    head, tail = pl.ds(0, cut), pl.ds(cut, rows - cut)
    go = lane.go
    me, twin, far = group.slot(0, 0), group.slot(0, 1), group.slot(2, 0)
    c0 = go(own, at(me), group.right)
    c1 = go(own, at(me), group.left)
    c2 = go(own, at(me), group.pair)
    yield
    c0.wait_recv()
    behind = at(group.slot(3, 0)).at[head]
    c3 = go(behind, behind, group.right)
    yield
    c1.wait_recv()
    ahead = at(group.slot(1, 0)).at[tail]
    c4 = go(ahead, ahead, group.left)
    yield
    c2.wait_recv()
    c5 = go(at(twin), at(twin), group.right)
    c6 = go(at(twin), at(twin), group.left)
    yield
    c3.wait_recv()
    yield
    c4.wait_recv()
    c7 = go(at(far), at(far), group.pair)
    for copy in (c5, c6, c7):
        yield
        copy.wait_recv()


def gather_few_steps(lane, group, own, at, cut, rows):
    head, tail = pl.ds(0, cut), pl.ds(cut, rows - cut)
    go = lane.go
    me, twin, far = group.slot(0, 0), group.slot(0, 1), group.slot(2, 0)
    c0 = go(own, at(me), group.right)
    c1 = go(own, at(me), group.left)
    c2 = go(own, at(me), group.pair)
    yield
    c0.wait_recv()
    behind = at(group.slot(3, 0)).at[head]
    c3 = go(behind, behind, group.right)
    c1.wait_recv()
    ahead = at(group.slot(1, 0)).at[tail]
    c4 = go(ahead, ahead, group.left)
    c2.wait_recv()
    c5 = go(at(twin), at(twin), group.right)
    c6 = go(at(twin), at(twin), group.left)
    yield
    c3.wait_recv()
    c4.wait_recv()
    c7 = go(at(far), at(far), group.pair)
    yield
    for copy in (c5, c6, c7):
        copy.wait_recv()


SCATTERS = 11


def scatter_scratch(rows, cut, width):
    return [
        pltpu.VMEM((rows, width), BF),
        pltpu.VMEM((rows, width), BF),
        pltpu.VMEM((cut, width), BF),
        pltpu.VMEM((rows - cut, width), BF),
        pltpu.VMEM((cut, width), BF),
        pltpu.VMEM((rows - cut, width), BF),
        pltpu.VMEM((2, rows, width), BF),
        pltpu.VMEM((2, rows, width), BF),
        pltpu.VMEM((rows, width), BF),
        pltpu.VMEM((rows, width), BF),
    ]


SCRATCHES = 10


def scatter_steps(lane, group, src, cut, rows, buffers, take):
    in_far, st_far, in_right, in_left, st_left, st_right, from_right, from_left, st_pair, from_pair = buffers
    head, tail = pl.ds(0, cut), pl.ds(cut, rows - cut)
    go = lane.go
    opposite = go(src.at[group.slot(2, 1)], in_far, group.pair)
    beside = [
        go(src.at[group.slot(3, 1)], from_right.at[0], group.left),
        go(src.at[group.slot(1, 1)], from_left.at[0], group.right),
    ]
    near = [
        go(src.at[group.slot(3, 0)].at[tail], from_right.at[1].at[tail], group.left),
        go(src.at[group.slot(1, 0)].at[head], from_left.at[1].at[head], group.right),
    ]
    yield
    opposite.wait_recv()
    st_far[...] = (src[group.slot(2, 0)].astype(F32) + in_far[...].astype(F32)).astype(BF)
    far_left = go(st_far.at[head], in_right, group.left)
    far_right = go(st_far.at[tail], in_left, group.right)
    for copy in beside:
        yield
        copy.wait_recv()
    total = src[group.slot(0, 1)].astype(F32) + from_right[0].astype(F32) + from_left[0].astype(F32)
    st_pair[...] = total.astype(BF)
    last = go(st_pair, from_pair, group.pair)
    yield
    far_left.wait_recv()
    st_left[...] = (src[group.slot(3, 0), head].astype(F32) + in_right[...].astype(F32)).astype(BF)
    near.append(go(st_left, from_right.at[1].at[head], group.left))
    yield
    far_right.wait_recv()
    st_right[...] = (src[group.slot(1, 0), tail].astype(F32) + in_left[...].astype(F32)).astype(BF)
    near.append(go(st_right, from_left.at[1].at[tail], group.right))
    for copy in near + [last]:
        yield
        copy.wait_recv()
    total = src[group.slot(0, 0)].astype(F32) + from_right[1].astype(F32) + from_left[1].astype(F32)
    take(total + from_pair[...].astype(F32))


def sems(count):
    return [pltpu.SemaphoreType.DMA((count,)), pltpu.SemaphoreType.DMA((count,))]


def params(collective_id):
    return pltpu.CompilerParams(
        collective_id=collective_id, has_side_effects=True, vmem_limit_bytes=36 * 1024 * 1024
    )


def normalize(stream):
    mean = jnp.mean(stream, axis=-1, keepdims=True)
    centred = stream - mean
    scale = lax.rsqrt(jnp.mean(centred * centred, axis=-1, keepdims=True) + epsilon)
    return centred * scale, scale


def norm_back(stream, grad_normed, gain):
    unit, scale = normalize(stream)
    grad_unit = grad_normed * gain
    first = jnp.mean(grad_unit, axis=-1, keepdims=True)
    second = jnp.mean(grad_unit * unit, axis=-1, keepdims=True)
    grad_gain = jnp.sum(grad_normed * unit, axis=0, keepdims=True)
    grad_shift = jnp.sum(grad_normed, axis=0, keepdims=True)
    return scale * (grad_unit - first - unit * second), grad_gain, grad_shift


PIECE = 64
ROWS = 96 + PIECE
CUT = 80
W_FIRST = ROWS + 16
W_CUT = 96
VMEM = pl.BlockSpec(memory_space=pltpu.VMEM)


def shard_scratch(rows):
    return [
        pltpu.VMEM((N, rows, HALF), BF),
        pltpu.VMEM((N, PIECE, HALF), BF),
        pltpu.VMEM((N, PIECE, HALF), BF),
    ]


SHARD_LANE = N - 1 + 3


def shard_steps(lane, lane_z, fsdp, cs, core, src, cut, rows, scratch, outs, own, kept, gather=gather_steps):
    held, mixed, got = scratch
    c, k = lax.axis_index("ctx"), lax.axis_index("dp")
    first = pltpu.make_async_copy(src.at[k], held.at[fsdp.slot(0, 0)], own.at[0])
    first.start()
    yield from gather(lane_z, fsdp, src.at[k], lambda slot: held.at[slot], cut, rows)
    first.wait()
    low = lax.broadcasted_iota(jnp.int32, (16, HALF), 0) < 8
    for i in range(N):
        own_rows = held[i, pl.ds(96, 16)].astype(F32)
        shared = held[i // 2 * 2 + c // 4, pl.ds(96, 16)].astype(F32)
        mixed[i, pl.ds(0, 16)] = jnp.where(low, own_rows, shared).astype(BF)
        mixed[i, pl.ds(16, 48)] = held[i, pl.ds(112, 48)]
    turn = [lane.go(mixed.at[peer["ctx"]], got.at[c], peer) for peer in cs]
    got[c] = mixed[c]
    cross = []

    def share(part, out, sem):
        cross.append(lane.go(part, out.at[k], core))
        keep = pltpu.make_async_copy(part, out.at[k], sem)
        keep.start()
        kept.append(keep)

    share(held.at[:, pl.ds(0, 96)], outs[0], own.at[1])
    if len(outs) > 2:
        share(held.at[:, pl.ds(ROWS, 16)], outs[2], own.at[2])
    for copy in turn:
        yield
        copy.wait_recv()
    share(got, outs[1], own.at[3])
    for copy in cross:
        yield
        copy.wait_recv()


COLS_SHAPE = jax.ShapeDtypeStruct((2, N, 96, HALF), BF)
PIECES_SHAPE = jax.ShapeDtypeStruct((2, N, PIECE, HALF), BF)


def weights_kernel(
    src, places, x, cols_all, pieces_all, vec_all, places_all, unit_all, *rest
):
    scratch, unit, rest = rest[:3], rest[3], rest[4:]
    lane, lane_z, lane_m, lane_u = (Lane(rest[2 * i : 2 * i + 2]) for i in range(4))
    own, keeps = rest[8], rest[9]
    c = lax.axis_index("ctx")
    fsdp, ctx = Group("fsdp"), Group("ctx")
    cs = others("ctx", c)
    core = {"dp": 1 - lax.axis_index("dp")}
    mark = pltpu.make_async_copy(places, places_all.at[c], keeps.at[0])
    mark.start()
    meet(fsdp.neighbours() + cs + [core])
    kept = [mark]
    marks = [lane_m.go(places, places_all.at[c], peer) for peer in cs]

    def tokens():
        unit[...] = normalize(x[...])[0].astype(BF)
        keep = pltpu.make_async_copy(unit, unit_all.at[c], keeps.at[1])
        keep.start()
        kept.append(keep)
        yield from gather_few_steps(lane_u, ctx, unit, lambda slot: unit_all.at[slot], TOK // 2, TOK)

    outs = (cols_all, pieces_all, vec_all)
    run(
        shard_steps(
            lane, lane_z, fsdp, cs, core, src, W_CUT, W_FIRST, scratch, outs, own, kept, gather_few_steps
        ),
        tokens(),
    )
    for copy in marks:
        copy.wait_recv()
    for each in (lane, lane_z, lane_m, lane_u):
        each.finish()
    for copy in kept:
        copy.wait()


def gather_weights(src, places, x, collective_id):
    tokens = jax.ShapeDtypeStruct((N, TOK, D), BF)
    return pl.pallas_call(
        weights_kernel,
        out_shape=(
            COLS_SHAPE,
            PIECES_SHAPE,
            jax.ShapeDtypeStruct((2, N, 16, HALF), BF),
            jax.ShapeDtypeStruct((N,) + places.shape, places.dtype),
            tokens,
        ),
        in_specs=[ANY] * 2 + [VMEM],
        out_specs=[ANY] * 5,
        scratch_shapes=shard_scratch(W_FIRST)
        + [pltpu.VMEM((TOK, D), BF)]
        + sems(SHARD_LANE)
        + sems(GATHERS)
        + sems(N - 1)
        + sems(GATHERS)
        + [pltpu.SemaphoreType.DMA((4,)), pltpu.SemaphoreType.DMA((2,))],
        compiler_params=params(collective_id),
    )(src, places, x)


def marks_of(places):
    frequency = 10000.0 ** (-2.0 * jnp.arange(ROT // 2, dtype=F32) / ROT)
    where = places.astype(F32).reshape(1, -1)
    angles = frequency[:, None] * where
    return jnp.concatenate([jnp.cos(angles), jnp.sin(angles), jnp.broadcast_to(where, angles.shape)], axis=0)


def prepare_kernel(marks, vectors, tables, col, rows_out):
    zero = jnp.zeros((8, TOK), F32)
    one = zero + 1.0
    for i in range(N):
        cosine, sine, where = marks[i, 0:8], marks[i, 8:16], marks[i, 16:24]
        rows = pl.ds(i * TOK, TOK)
        own = [cosine, cosine] + [one] * 6
        left = [zero, sine] + [zero] * 6
        right = [-sine, zero] + [zero] * 6
        for t, tiles in enumerate((own, left, right)):
            tables[t, rows] = jnp.concatenate(tiles + tiles, axis=0).T
        col[rows] = jnp.concatenate([where] * 16, axis=0).T

    c = lax.axis_index("ctx")
    head_a, head_b = 3 * (c // 2) + 2 * (c % 2), 3 * (c // 2) + 1

    def place(values, column, width, cut):
        shard = jnp.zeros((1, width), jnp.int32)
        for t in range(1, N):
            shard = shard + jnp.where(column >= cut * t, 1, 0)
        inner = column - cut * shard
        pick = lax.broadcasted_iota(jnp.int32, (HALF, width), 0) == inner
        spread_ = dot(values.astype(BF), jnp.where(pick, 1.0, 0.0).astype(BF), ((1,), (0,)))
        mine = lax.broadcasted_iota(jnp.int32, (N, width), 0) == shard
        return jnp.sum(jnp.where(mine, spread_, 0.0), axis=0, keepdims=True)

    lanes = lax.broadcasted_iota(jnp.int32, (1, D), 1)
    lane = lax.broadcasted_iota(jnp.int32, (1, HALF), 1)
    third = jnp.where(lane >= 128, 1, 0) + jnp.where(lane >= 256, 1, 0)
    within = lane - 128 * third
    second = jnp.where(within >= HEAD_DIM, 1, 0)
    head = jnp.where(second == 1, head_b, head_a)
    column = 192 * head + HEAD_DIM * third + (within - HEAD_DIM * second)
    for layer in range(LAYERS):
        shards = [vectors[layer, i].astype(F32) for i in range(N)]

        def row(r):
            return jnp.concatenate([one_shard[r : r + 1] for one_shard in shards], axis=0)

        rows_out[layer, 0:1] = place(row(2), lanes, D, 96)
        rows_out[layer, 1:2] = place(row(3), lanes, D, 96)
        rows_out[layer, 2:3] = place(row(4), lanes, D, 96) + place(row(5), lanes, D, 96)
        rows_out[layer, 3:4, pl.ds(0, HALF)] = place(row(0), column, HALF, 288)
        rows_out[layer, 3:4, pl.ds(HALF, HALF)] = vectors[layer, c].astype(F32)[1:2]
        rows_out[layer, 4:8] = jnp.zeros((4, D), F32)


def prepare(marks, vectors):
    return pl.pallas_call(
        prepare_kernel,
        out_shape=(
            jax.ShapeDtypeStruct((3, SEQ, 128), F32),
            jax.ShapeDtypeStruct((SEQ, 128), F32),
            jax.ShapeDtypeStruct((LAYERS, 8, D), F32),
        ),
        in_specs=[VMEM] * 2,
        out_specs=[VMEM] * 3,
        compiler_params=pltpu.CompilerParams(vmem_limit_bytes=48 * 1024 * 1024),
    )(marks, vectors)


BLOCK = 256
BLOCKS = SEQ // BLOCK


def unit_rows(b):
    s = lax.axis_index("ctx") % 2
    start = jnp.where(b < BLOCKS, b * BLOCK, s * (SEQ // 2) + (b - BLOCKS) * BLOCK)
    start = pl.multiple_of(start, BLOCK)
    lanes = lax.broadcasted_iota(jnp.int32, (BLOCK, 2 * HEAD_DIM), 1) // HEAD_DIM
    return start, lanes == jnp.where(b < BLOCKS, 0, 1)


def mix_rows(pieces, w_mix):
    for h in range(2):
        cols = pl.ds(HALF * h, HALF)
        rows = [pieces[h, j, pl.ds(0, 16)].astype(F32) for j in range(N)]
        heads = [r[:8] for r in rows] + [r[8:] for r in rows]
        w_mix[pl.ds(0, 128), cols] = jnp.concatenate(heads, axis=0).astype(BF)
        for j in range(N):
            w_mix[pl.ds(128 + 48 * j, 48), cols] = pieces[h, j, pl.ds(16, 48)]


def forward_steps(
    unit, vectors, w_cat, pieces, col, row, tables,
    branch, normed, query, key, value, slope, mixed, lse, w_mix, turned,
):
    mix_rows(pieces, w_mix)

    @pl.loop(0, BLOCKS)
    def _(i):
        rows = pl.ds(pl.multiple_of(i * BLOCK, BLOCK), BLOCK)
        low = (unit[rows].astype(F32) * vectors[0:1] + vectors[1:2]).astype(BF)
        normed[rows] = low
        heads = dot(low, w_cat[0], ((1,), (0,))) + vectors[3:4, :HALF]

        def rotate(values):
            return (
                values * tables[0, rows]
                + pltpu.roll(values, 8, axis=1) * tables[1, rows]
                + pltpu.roll(values, 120, axis=1) * tables[2, rows]
            )

        query[rows] = (rotate(heads[:, :128]) * HEAD_DIM ** (-0.5)).astype(BF)
        key[rows] = rotate(heads[:, 128:256]).astype(BF)
        value[rows] = heads[:, 256:].astype(BF)
        pre = dot(low, w_cat[1], ((1,), (0,))) + vectors[3:4, HALF:]
        cdf = 0.5 * (1.0 + lax.erf(pre * 0.5**0.5))
        mixed[rows, pl.ds(128, HALF)] = (pre * cdf).astype(BF)
        mixed[rows, pl.ds(0, 128)] = jnp.zeros((BLOCK, 128), BF)
        slope[rows] = cdf + pre * (jnp.exp(-0.5 * pre * pre) * 0.3989422804014327)

    turned[...] = value[...].astype(F32).T.astype(BF)
    yield
    for n in range(3):

        @pl.loop(2 * n, 2 * n + 2)
        def _(b):
            start, mask = unit_rows(b)
            rows = pl.ds(start, BLOCK)
            q = jnp.where(mask, query[rows].astype(F32), 0.0).astype(BF)
            scores = dot(key[...], q, ((1,), (1,)))
            seen = jnp.concatenate([col[...], col[...]], axis=1) <= row[pl.ds(start // BLOCK, 1)]
            scores = jnp.where(seen, scores, -jnp.inf)
            top = jnp.max(scores, axis=0, keepdims=True)
            expos = jnp.exp(scores - top)
            total = jnp.sum(expos, axis=0, keepdims=True)
            lse[pl.ds(b, 1)] = top + jnp.log(total)
            probs = (expos * (1.0 / total)).astype(BF)
            out = dot(turned[...], probs, ((1,), (0,))).T
            mixed[rows, pl.ds(0, 128)] = jnp.where(mask, out, mixed[rows, pl.ds(0, 128)].astype(F32)).astype(BF)

        yield
    for i in range(N):
        rows = pl.ds(i * TOK, TOK)
        branch[i] = dot(mixed[rows], w_mix[...], ((1,), (0,))).astype(BF)


def unit_rows_of(b):
    s = lax.axis_index("ctx") % 2
    lanes = lax.broadcasted_iota(jnp.int32, (BLOCK, 2 * HEAD_DIM), 1)
    if b < BLOCKS:
        return b * BLOCK, lanes < HEAD_DIM
    return pl.multiple_of(s * (SEQ // 2) + (b - BLOCKS) * BLOCK, BLOCK), lanes >= HEAD_DIM


def forward_unrolled(
    unit, vectors, w_cat, pieces, col, row, tables,
    branch, normed, query, key, value, slope, mixed, lse, w_mix, turned,
):
    mix_rows(pieces, w_mix)
    for i in range(BLOCKS):
        rows = pl.ds(i * BLOCK, BLOCK)
        low = (unit[rows].astype(F32) * vectors[0:1] + vectors[1:2]).astype(BF)
        normed[rows] = low
        heads = dot(low, w_cat[0], ((1,), (0,))) + vectors[3:4, :HALF]

        def rotate(values, rows=rows):
            return (
                values * tables[0, rows]
                + pltpu.roll(values, 8, axis=1) * tables[1, rows]
                + pltpu.roll(values, 120, axis=1) * tables[2, rows]
            )

        query[rows] = (rotate(heads[:, :128]) * HEAD_DIM ** (-0.5)).astype(BF)
        key[rows] = rotate(heads[:, 128:256]).astype(BF)
        value[rows] = heads[:, 256:].astype(BF)
        pre = dot(low, w_cat[1], ((1,), (0,))) + vectors[3:4, HALF:]
        cdf = 0.5 * (1.0 + lax.erf(pre * 0.5**0.5))
        mixed[rows, pl.ds(128, HALF)] = (pre * cdf).astype(BF)
        mixed[rows, pl.ds(0, 128)] = jnp.zeros((BLOCK, 128), BF)
        slope[rows] = cdf + pre * (jnp.exp(-0.5 * pre * pre) * 0.3989422804014327)
        yield

    turned[...] = value[...].astype(F32).T.astype(BF)
    for b in range(BLOCKS + 2):
        start, mask = unit_rows_of(b)
        rows = pl.ds(start, BLOCK)
        q = jnp.where(mask, query[rows].astype(F32), 0.0).astype(BF)
        scores = dot(key[...], q, ((1,), (1,)))
        seen = jnp.concatenate([col[...], col[...]], axis=1) <= row[pl.ds(start // BLOCK, 1)]
        scores = jnp.where(seen, scores, -jnp.inf)
        top = jnp.max(scores, axis=0, keepdims=True)
        expos = jnp.exp(scores - top)
        total = jnp.sum(expos, axis=0, keepdims=True)
        lse[pl.ds(b, 1)] = top + jnp.log(total)
        probs = (expos * (1.0 / total)).astype(BF)
        out = dot(turned[...], probs, ((1,), (0,))).T
        mixed[rows, pl.ds(0, 128)] = jnp.where(mask, out, mixed[rows, pl.ds(0, 128)].astype(F32)).astype(BF)
        yield
    for i in range(BLOCKS):
        rows = pl.ds(i * BLOCK, BLOCK)
        out = dot(mixed[rows], w_mix[...], ((1,), (0,))).astype(BF)
        branch[2 * i] = out[:TOK]
        branch[2 * i + 1] = out[TOK:]
        yield


def forward_shapes():
    shape = jax.ShapeDtypeStruct
    return (
        shape((N, TOK, D), BF),
        shape((SEQ, D), BF),
        shape((SEQ, 128), BF),
        shape((SEQ, 128), BF),
        shape((SEQ, 128), BF),
        shape((SEQ, HALF), F32),
        shape((SEQ, 512), BF),
        shape((8, BLOCK), F32),
        shape((512, D), BF),
    )


FORWARDS = 9


def local_params():
    return pltpu.CompilerParams(vmem_limit_bytes=36 * 1024 * 1024)


def forward_kernel(*refs):
    run(forward_unrolled(*refs))


def forward(*args):
    return pl.pallas_call(
        forward_kernel,
        out_shape=forward_shapes(),
        in_specs=[VMEM] * len(args),
        out_specs=[VMEM] * FORWARDS,
        scratch_shapes=[pltpu.VMEM((128, SEQ), BF)],
        compiler_params=local_params(),
    )(*args)


def forward_between_kernel(*refs):
    args, (x, cot, src), refs = refs[:7], refs[7:10], refs[10:]
    outs, refs = refs[:FORWARDS], refs[FORWARDS:]
    (x_next, unit_all, low_all, cols_all, pieces_all), refs = refs[:5], refs[5:]
    turned, unit, low_g, scratch, rest = refs[0], refs[1], refs[2], refs[3:6], refs[6:]
    buffers, rest = rest[:SCRATCHES], rest[SCRATCHES:]
    lane, lane_u, lane_g, lane_w, lane_z = (Lane(rest[2 * i : 2 * i + 2]) for i in range(5))
    own, keeps = rest[10], rest[11]
    ctx, fsdp = Group("ctx"), Group("fsdp")
    cs = others("ctx", lax.axis_index("ctx"))
    core = {"dp": 1 - lax.axis_index("dp")}
    meet(fsdp.neighbours() + cs + [core])
    kept = []
    branch, vectors = outs[0], args[1]

    def tokens():
        yield from forward_steps(*args, *outs, turned)

        def take(total):
            x_next[...] = x[...] + (total + vectors[2:3])

        yield from scatter_steps(lane, ctx, branch, TOK // 2, TOK, buffers, take)
        unit[...] = normalize(x_next[...])[0].astype(BF)
        keep = pltpu.make_async_copy(unit, unit_all.at[ctx.slot(0, 0)], keeps.at[0])
        keep.start()
        kept.append(keep)
        yield from gather_steps(lane_u, ctx, unit, lambda slot: unit_all.at[slot], TOK // 2, TOK)

    def later():
        low_g[...] = cot[...].astype(BF)
        keep = pltpu.make_async_copy(low_g, low_all.at[ctx.slot(0, 0)], keeps.at[1])
        keep.start()
        kept.append(keep)
        yield from gather_steps(lane_g, ctx, low_g, lambda slot: low_all.at[slot], TOK // 2, TOK)

    outs_w = (cols_all, pieces_all)
    run(
        shard_steps(lane_w, lane_z, fsdp, cs, core, src, CUT, ROWS, scratch, outs_w, own, kept),
        later(),
        tokens(),
    )
    for each in (lane, lane_u, lane_g, lane_w, lane_z):
        each.finish()
    for copy in kept:
        copy.wait()


def forward_between(args, x, cot, src, collective_id):
    tokens = jax.ShapeDtypeStruct((N, TOK, D), BF)
    return pl.pallas_call(
        forward_between_kernel,
        out_shape=forward_shapes()
        + (jax.ShapeDtypeStruct((TOK, D), F32), tokens, tokens, COLS_SHAPE, PIECES_SHAPE),
        in_specs=[VMEM] * 9 + [ANY],
        out_specs=[VMEM] * (FORWARDS + 1) + [ANY] * 4,
        scratch_shapes=[
            pltpu.VMEM((128, SEQ), BF),
            pltpu.VMEM((TOK, D), BF),
            pltpu.VMEM((TOK, D), BF),
        ]
        + shard_scratch(ROWS)
        + scatter_scratch(TOK, TOK // 2, D)
        + sems(SCATTERS)
        + sems(GATHERS)
        + sems(GATHERS)
        + sems(SHARD_LANE)
        + sems(GATHERS)
        + [pltpu.SemaphoreType.DMA((4,)), pltpu.SemaphoreType.DMA((2,))],
        compiler_params=params(collective_id),
    )(*args, x, cot, src)


BACK_ARGS = 12


def backward_scratch():
    return [
        pltpu.VMEM((SEQ, 128), BF),
        pltpu.VMEM((SEQ, D), BF),
        pltpu.VMEM((SEQ, 128), F32),
        pltpu.VMEM((SEQ, 128), F32),
        pltpu.VMEM((SEQ, 128), F32),
        pltpu.VMEM((128, SEQ), BF),
        pltpu.VMEM((D, D), F32),
        pltpu.VMEM((N, TOK, D), BF),
        pltpu.VMEM((2, N, 96, HALF), BF),
        pltpu.VMEM((2, N, PIECE, HALF), BF),
    ]


BACKS = 10


def backward_steps(
    ready, low, w_cat, normed, query, key, value, slope, mixed, lse, w_mix, col, row, tables, grad_b,
    grad_att, grad_pre, dq, dk, dv, turned, big, grad_normed, part_a, part_b,
):
    @pl.loop(0, 2)
    def _(i):
        cols = pl.ds(pl.multiple_of(i * BLOCK, BLOCK), BLOCK)
        big[cols] = dot(mixed[:, cols], low[...], ((0,), (0,)))

    for j in range(N):
        for h in range(2):
            at = slice(HALF * h, HALF * h + HALF)
            first = big[8 * j : 8 * j + 8, at]
            second = big[64 + 8 * j : 64 + 8 * j + 8, at]
            part_b[h, j, pl.ds(0, 16)] = jnp.concatenate([first, second], axis=0).astype(BF)
            part_b[h, j, pl.ds(16, 48)] = big[128 + 48 * j : 176 + 48 * j, at].astype(BF)
    ready.add("b")
    yield

    @pl.loop(0, BLOCKS)
    def _(i):
        rows = pl.ds(pl.multiple_of(i * BLOCK, BLOCK), BLOCK)
        back = dot(low[rows], w_mix[...], ((1,), (1,)))
        grad_att[rows] = back[:, :128].astype(BF)
        grad_pre[rows, pl.ds(HALF, HALF)] = (back[:, 128:] * slope[rows]).astype(BF)

    turned[...] = key[...].astype(F32).T.astype(BF)
    dq[...] = jnp.zeros((SEQ, 128), F32)
    dk[...] = jnp.zeros((SEQ, 128), F32)
    dv[...] = jnp.zeros((SEQ, 128), F32)
    yield
    for n in range(3):

        @pl.loop(2 * n, 2 * n + 2)
        def _(b):
            start, mask = unit_rows(b)
            rows = pl.ds(start, BLOCK)
            q = jnp.where(mask, query[rows].astype(F32), 0.0).astype(BF)
            g = jnp.where(mask, grad_att[rows].astype(F32), 0.0).astype(BF)
            scores = dot(key[...], q, ((1,), (1,)))
            seen = jnp.concatenate([col[...], col[...]], axis=1) <= row[pl.ds(start // BLOCK, 1)]
            probs = jnp.exp(jnp.where(seen, scores, -jnp.inf) - lse[pl.ds(b, 1)])
            grad_probs = dot(value[...], g, ((1,), (1,)))
            mean = jnp.sum(probs * grad_probs, axis=0, keepdims=True)
            grad_scores = (probs * (grad_probs - mean)).astype(BF)
            dq[rows] = jnp.where(mask, dot(turned[...], grad_scores, ((1,), (0,))).T, dq[rows])
            dk[...] += dot(grad_scores, q, ((1,), (0,)))
            dv[...] += dot(probs.astype(BF), g, ((1,), (0,)))

        yield
    grad_b[...] = jnp.zeros((1, D), F32)

    @pl.loop(0, N)
    def _(i):
        rows = pl.ds(pl.multiple_of(i * TOK, TOK), TOK)

        def rotate_back(grads):
            return (
                grads * tables[0, rows]
                + pltpu.roll(grads * tables[1, rows], 120, axis=1)
                + pltpu.roll(grads * tables[2, rows], 8, axis=1)
            )

        grad_pre[rows, pl.ds(0, 128)] = rotate_back(dq[rows] * HEAD_DIM ** (-0.5)).astype(BF)
        grad_pre[rows, pl.ds(128, 128)] = rotate_back(dk[rows]).astype(BF)
        grad_pre[rows, pl.ds(256, 128)] = dv[rows].astype(BF)
        block = grad_pre[rows]
        grad_b[...] += jnp.sum(block.astype(F32), axis=0, keepdims=True)
        grad_normed[i] = (
            dot(block[:, :HALF], w_cat[0], ((1,), (1,))) + dot(block[:, HALF:], w_cat[1], ((1,), (1,)))
        ).astype(BF)

    ready.add("normed")
    yield

    @pl.loop(0, D // BLOCK)
    def _(i):
        cols = pl.ds(pl.multiple_of(i * BLOCK, BLOCK), BLOCK)
        big[cols] = dot(normed[:, cols], grad_pre[...], ((0,), (0,)))

    for f in range(N):
        for h in range(2):
            part_a[h, f] = big[96 * f : 96 * f + 96, HALF * h : HALF * h + HALF].astype(BF)
    ready.add("a")


def grads_scratch():
    return [
        pltpu.VMEM((N, 96, HALF), BF),
        pltpu.VMEM((N, PIECE, HALF), BF),
        pltpu.VMEM((N, PIECE, HALF), BF),
        pltpu.VMEM((N, ROWS, HALF), BF),
    ] + scatter_scratch(ROWS, CUT, HALF)


GRADS = 4 + SCRATCHES


def grads_steps(ready, lane, lane_z, fsdp, cs, core, part_a, part_b, scratch, take):
    their_a, their_b, got, blocks = scratch[:4]
    c, k = lax.axis_index("ctx"), lax.axis_index("dp")
    while "b" not in ready:
        yield
    first_b = lane.go(part_b.at[1 - k], their_b, core)
    yield
    first_b.wait_recv()
    for i in range(N):
        their_b[i] = (part_b[k, i].astype(F32) + their_b[i].astype(F32)).astype(BF)
    turn = [lane.go(their_b.at[peer["ctx"]], got.at[c], peer) for peer in cs]
    got[c] = their_b[c]
    while "a" not in ready:
        yield
    first_a = lane.go(part_a.at[1 - k], their_a, core)
    for copy in turn:
        copy.wait_recv()
    low = lax.broadcasted_iota(jnp.int32, (16, HALF), 0) < 8
    for i in range(N):
        rows = got[i, pl.ds(0, 16)].astype(F32)
        pair = got[i + 1 - 2 * (i % 2), pl.ds(0, 16)].astype(F32)
        blocks[i, pl.ds(96, 16)] = jnp.where(low, rows, rows + pair).astype(BF)
        blocks[i, pl.ds(112, 48)] = got[i, pl.ds(16, 48)]
    yield
    first_a.wait_recv()
    for i in range(N):
        blocks[i, pl.ds(0, 96)] = (part_a[k, i].astype(F32) + their_a[i].astype(F32)).astype(BF)
    yield from scatter_steps(lane_z, fsdp, blocks, CUT, ROWS, scratch[4:], take)


def turn_kernel(*refs):
    (low, *args), refs = refs[:13], refs[13:]
    (x, grad, vectors, out_parts, bias), refs = refs[:5], refs[5:]
    (outputs, grad_next, low_all, vecs, share), refs = refs[:5], refs[5:]
    (low_g, grad_b), refs = refs[:2], refs[2:]
    back, refs = refs[:BACKS], refs[BACKS:]
    buffers, refs = refs[:SCRATCHES], refs[SCRATCHES:]
    buffers_o, refs = refs[:SCRATCHES], refs[SCRATCHES:]
    scratch, rest = refs[:GRADS], refs[GRADS:]
    lane, lane_g, lane_w, lane_z, lane_o = (Lane(rest[2 * i : 2 * i + 2]) for i in range(5))
    keep_sem = rest[10]
    ctx, fsdp = Group("ctx"), Group("fsdp")
    cs = others("ctx", lax.axis_index("ctx"))
    core = {"dp": 1 - lax.axis_index("dp")}
    meet(cs + fsdp.neighbours() + [core])
    kept, ready = [], set()

    def tokens():
        def take(total):
            back_, grad_gain, grad_shift = norm_back(x[...], total, vectors[0:1])
            grad_next[...] = grad[...] + back_
            rounded = grad[...].astype(BF).astype(F32)
            vecs[pl.ds(0, 1)] = jnp.sum(rounded, axis=0, keepdims=True)
            vecs[pl.ds(1, 1)] = grad_gain
            vecs[pl.ds(2, 1)] = grad_shift
            vecs[pl.ds(3, 1)] = grad_b[...]
            vecs[pl.ds(4, 4)] = jnp.zeros((4, D), F32)

        while "normed" not in ready:
            yield
        yield from scatter_steps(lane, ctx, back[7], TOK // 2, TOK, buffers, take)
        low_g[...] = grad_next[...].astype(BF)
        keep = pltpu.make_async_copy(low_g, low_all.at[ctx.slot(0, 0)], keep_sem)
        keep.start()
        kept.append(keep)
        yield from gather_steps(lane_g, ctx, low_g, lambda slot: low_all.at[slot], TOK // 2, TOK)

    def weights():
        def take(total):
            share[...] = total.astype(BF)

        yield from grads_steps(ready, lane_w, lane_z, fsdp, cs, core, back[8], back[9], scratch, take)

    def ends():
        def take(total):
            outputs[...] = x[...] + (total + bias[2:3])

        yield from scatter_steps(lane_o, ctx, out_parts, TOK // 2, TOK, buffers_o, take)

    run(ends(), backward_steps(ready, low, *args, grad_b, *back), tokens(), weights())
    for each in (lane, lane_g, lane_w, lane_z, lane_o):
        each.finish()
    for copy in kept:
        copy.wait()


def turn(args, x, grad, vectors, out_parts, collective_id):
    tokens = jax.ShapeDtypeStruct((TOK, D), F32)
    return pl.pallas_call(
        turn_kernel,
        out_shape=(
            tokens,
            tokens,
            jax.ShapeDtypeStruct((N, TOK, D), BF),
            jax.ShapeDtypeStruct((8, D), F32),
            jax.ShapeDtypeStruct((ROWS, HALF), BF),
        ),
        in_specs=[VMEM] * 18,
        out_specs=(VMEM, VMEM, ANY, VMEM, VMEM),
        scratch_shapes=[pltpu.VMEM((TOK, D), BF), pltpu.VMEM((1, D), F32)]
        + backward_scratch()
        + scatter_scratch(TOK, TOK // 2, D)
        + scatter_scratch(TOK, TOK // 2, D)
        + grads_scratch()
        + sems(SCATTERS)
        + sems(GATHERS)
        + sems(2 + N - 1)
        + sems(SCATTERS)
        + sems(SCATTERS)
        + [pltpu.SemaphoreType.DMA],
        compiler_params=params(collective_id),
    )(*args, x, grad, vectors, out_parts, vectors)


FIRST_ROWS = ROWS + 16


def last_kernel(*refs):
    (low, *args), refs = refs[:13], refs[13:]
    (x, grad, vectors, vecs, share), refs = refs[:5], refs[5:]
    (grad_next, out_first, out_last), refs = refs[:3], refs[3:]
    (both, v_mine, v_their, v_all, grad_b), refs = refs[:5], refs[5:]
    back, refs = refs[:BACKS], refs[BACKS:]
    buffers, refs = refs[:SCRATCHES], refs[SCRATCHES:]
    scratch, rest = refs[:GRADS], refs[GRADS:]
    lane, lane_w, lane_z, lane_v, lane_x, lane_s = (Lane(rest[2 * i : 2 * i + 2]) for i in range(6))
    keeps = rest[12]
    c, f, k = lax.axis_index("ctx"), lax.axis_index("fsdp"), lax.axis_index("dp")
    ctx, fsdp = Group("ctx"), Group("fsdp")
    cs, fs = others("ctx", c), others("fsdp", f)
    core = {"dp": 1 - k}
    meet(cs + fs + [core])
    ready = set()

    def tokens():
        def take(total):
            back_, grad_gain, grad_shift = norm_back(x[...], total, vectors[0:1])
            grad_next[...] = grad[...] + back_
            rounded = grad[...].astype(BF).astype(F32)
            branch = jnp.sum(rounded, axis=0, keepdims=True)
            mine = [vecs[...], branch, grad_gain, grad_shift, grad_b[...], jnp.zeros((4, D), F32)]
            mine = jnp.concatenate(mine, axis=0)
            v_mine[0] = mine[:, :HALF].astype(BF)
            v_mine[1] = mine[:, HALF:].astype(BF)

        while "normed" not in ready:
            yield
        yield from scatter_steps(lane, ctx, back[7], TOK // 2, TOK, buffers, take)
        cross = lane_v.go(v_mine.at[1 - k], v_their, core)
        yield
        cross.wait_recv()
        v_all[f] = (v_mine[k].astype(F32) + v_their[...].astype(F32)).astype(BF)
        copies = [lane_v.go(v_all.at[f], v_all.at[f], peer) for peer in fs]
        yield
        for copy in copies:
            copy.wait_recv()
        total = v_all[0].astype(F32)
        for i in range(1, N):
            total = total + v_all[i].astype(F32)
        both[pl.ds(ROWS, 16)] = total.astype(BF)

    def weights():
        def take(total):
            both[pl.ds(0, ROWS)] = total.astype(BF)

        yield from grads_steps(ready, lane_w, lane_z, fsdp, cs, core, back[8], back[9], scratch, take)

    kept = []

    def older():
        keep = pltpu.make_async_copy(share, out_last.at[k, c], keeps.at[0])
        keep.start()
        kept.append(keep)
        yield from gather_steps(lane_s, ctx, share, lambda slot: out_last.at[k, slot], CUT, ROWS)
        keep.wait()
        copy = lane_s.go(out_last.at[k], out_last.at[k], core)
        yield
        copy.wait_recv()

    run(older(), backward_steps(ready, low, *args, grad_b, *back), tokens(), weights())
    keep = pltpu.make_async_copy(both, out_first.at[k, c], keeps.at[1])
    keep.start()
    run(gather_steps(lane_x, ctx, both, lambda slot: out_first.at[k, slot], W_CUT, FIRST_ROWS))
    keep.wait()
    lane_x.go(out_first.at[k], out_first.at[k], core).wait_recv()
    for each in (lane, lane_w, lane_z, lane_v, lane_x, lane_s):
        each.finish()


def last(args, x, grad, vectors, vecs, share, collective_id):
    return pl.pallas_call(
        last_kernel,
        out_shape=(
            jax.ShapeDtypeStruct((TOK, D), F32),
            jax.ShapeDtypeStruct((2, N, FIRST_ROWS, HALF), BF),
            jax.ShapeDtypeStruct((2, N, ROWS, HALF), BF),
        ),
        in_specs=[VMEM] * 18,
        out_specs=(VMEM, ANY, ANY),
        scratch_shapes=[
            pltpu.VMEM((FIRST_ROWS, HALF), BF),
            pltpu.VMEM((2, 16, HALF), BF),
            pltpu.VMEM((16, HALF), BF),
            pltpu.VMEM((N, 16, HALF), BF),
            pltpu.VMEM((1, D), F32),
        ]
        + backward_scratch()
        + scatter_scratch(TOK, TOK // 2, D)
        + grads_scratch()
        + sems(SCATTERS)
        + sems(2 + N - 1)
        + sems(SCATTERS)
        + sems(N)
        + sems(GATHERS + 1)
        + sems(GATHERS + 1)
        + [pltpu.SemaphoreType.DMA((2,))],
        compiler_params=params(collective_id),
    )(*args, x, grad, vectors, vecs, share)


def spread_kernel(got_first, got_last, g_qkv, g_out, g_up, g_down):
    odd = lax.axis_index("fsdp") % 2
    for layer in range(LAYERS):
        got, base = (got_first, got_last)[layer], 0

        def heads(i, got=got, base=base):
            return got[0, i, pl.ds(base, 96)].astype(F32)

        chunks = []
        for p in range(4):
            one, two = heads(2 * p), heads(2 * p + 1)
            both = one + two
            for values, lane in ((one, 0), (both, HEAD_DIM), (two, 0)):
                chunks += [values[:, 128 * i + lane : 128 * i + lane + HEAD_DIM] for i in range(3)]
        for i in range(len(chunks) // 2):
            g_qkv[layer, :, pl.ds(128 * i, 128)] = jnp.concatenate(chunks[2 * i : 2 * i + 2], axis=1)
        for i in range(N):
            g_up[layer, :, pl.ds(HALF * i, HALF)] = got[1, i, pl.ds(base, 96)].astype(F32)
            for h in range(2):
                cols = pl.ds(HALF * h, HALF)
                g_down[layer, pl.ds(48 * i, 48), cols] = got[h, i, pl.ds(base + 112, 48)].astype(F32)
        for h in range(2):
            cols = pl.ds(HALF * h, HALF)
            rows = [got[h, i, pl.ds(base + 96, 16)].astype(F32) for i in range(N)]
            first = [r[:8] for r in rows]
            even = jnp.concatenate(first + [r[8:] for r in rows[:4]], axis=0)
            uneven = jnp.concatenate([r[8:] for r in rows[4:]] + first, axis=0)
            g_out[layer, :, cols] = jnp.where(odd == 0, even, uneven)


def spread(got_first, got_last):
    shape = jax.ShapeDtypeStruct
    return pl.pallas_call(
        spread_kernel,
        out_shape=(
            shape((LAYERS, 96, 3 * D), F32),
            shape((LAYERS, 96, D), F32),
            shape((LAYERS, 96, FF), F32),
            shape((LAYERS, HALF, D), F32),
        ),
        in_specs=[VMEM] * 2,
        out_specs=[VMEM] * 4,
        compiler_params=local_params(),
    )(got_first, got_last)


def body(
    inputs, positions, cotangent, w_qkv, b_qkv, w_out, b_out, w_up, b_up, w_down, b_down, ln_gain, ln_bias
):
    c = lax.axis_index("ctx")
    p, s = c // 2, lax.rem(c, 2)
    head_a, head_b = 3 * p + 2 * s, 3 * p + 1

    def heads_cols(w):
        grouped = w.reshape(w.shape[:-1] + (12, 3, HEAD_DIM))
        axis = grouped.ndim - 3
        both = jnp.concatenate(
            [
                lax.dynamic_slice_in_dim(grouped, head_a, 1, axis=axis),
                lax.dynamic_slice_in_dim(grouped, head_b, 1, axis=axis),
            ],
            axis=axis,
        )
        return jnp.swapaxes(both, axis, axis + 1).reshape(w.shape[:-1] + (HALF,))

    def hidden_cols(w):
        return lax.dynamic_slice_in_dim(w, c * HALF, HALF, axis=w.ndim - 1)

    f = lax.axis_index("fsdp")
    f_s = lax.rem(f, 2)

    def piece(w, start, count):
        return lax.dynamic_slice_in_dim(w, start, count, axis=1)

    cols = jnp.concatenate([heads_cols(w_qkv), hidden_cols(w_up)], axis=-1)
    first_rows = piece(w_out, jnp.where(f_s == 0, 0, 32) + 8 * c, 8)
    shared_rows = piece(w_out, jnp.where(f_s == 0, 64, -32) + 8 * jnp.where(f_s == 0, c % 4, c), 8)
    down_rows = piece(w_down, 48 * c, 48)
    by_layer = jnp.concatenate([cols, first_rows, shared_rows, down_rows], axis=1)
    def wide(vector):
        return jnp.pad(vector, ((0, 0), (0, HALF - vector.shape[1])))

    vec = jnp.stack([wide(v) for v in (b_qkv, b_up, ln_gain, ln_bias, b_out, b_down)], axis=1)
    vec = jnp.pad(vec, ((0, 0), (0, 10), (0, 0)))
    src = [jnp.stack([one[:, :HALF], one[:, HALF:]]) for one in (by_layer[0], by_layer[1])]
    src[0] = jnp.concatenate([src[0], vec], axis=1)
    stream, cot = inputs[0], cotangent[0]
    cols, pieces, vec_all, marks, unit = gather_weights(src[0], marks_of(positions), stream, 1)
    tables, col, vectors = prepare(marks, vec_all)
    row = marks[:, 16].reshape(BLOCKS, BLOCK)
    w_first = cols.reshape(2, D, HALF)
    branch, *kept_first, x_last, unit, low_last, cols, pieces_last = forward_between(
        (unit.reshape(SEQ, D), vectors[0], w_first, pieces, col, row, tables), stream, cot, src[1], 2
    )
    w_last = cols.reshape(2, D, HALF)
    branch, *kept_last = forward(
        unit.reshape(SEQ, D), vectors[1], w_last, pieces_last, col, row, tables
    )
    outputs, grad, low, vecs, share = turn(
        (low_last.reshape(SEQ, D), w_last, *kept_last, col, row, tables), x_last, cot, vectors[1], branch, 3
    )
    grad, got_first, got_last = last(
        (low.reshape(SEQ, D), w_first, *kept_first, col, row, tables), stream, grad, vectors[0], vecs, share, 4
    )
    g_qkv, g_out, g_up, g_down = spread(got_first, got_last)

    rows = jnp.concatenate([got_first[0, :, ROWS:], got_first[1, :, ROWS:]], axis=-1).astype(F32)
    summed = jnp.sum(rows, axis=0)

    def cut(vector, width):
        return lax.dynamic_slice_in_dim(vector, f * width, width, axis=vector.ndim - 1)

    def own_vectors(biases):
        qkv = biases[:, :HALF].reshape(4, 2, 3, 2, HEAD_DIM)
        shared = qkv[:, 0, :, 1] + qkv[:, 1, :, 1]
        qkv = jnp.stack([qkv[:, 0, :, 0], shared, qkv[:, 1, :, 0]], axis=1).reshape(3 * D)
        up = lax.dynamic_index_in_dim(biases[:, HALF:], f, axis=0, keepdims=False)
        return cut(qkv, 288), up

    pairs = [own_vectors(rows[:, 11]), own_vectors(rows[:, 3])]
    g_b_qkv = jnp.stack([pair[0] for pair in pairs])
    g_b_up = jnp.stack([pair[1] for pair in pairs])
    g_branch, g_gain, g_shift = (cut(jnp.stack([summed[8 + i], summed[i]]), 96) for i in range(3))
    return (
        outputs[None], grad[None], g_qkv, g_b_qkv, g_out, g_branch, g_up, g_b_up, g_down, g_branch, g_gain, g_shift,
    )


def solution(mesh):
    seqs = ("dp", "fsdp")
    whole = P(None, "fsdp", None)
    row = P(None, "fsdp")
    in_specs = (
        P(seqs, "ctx", None), P(seqs, "ctx"), P(seqs, "ctx", None),
        whole, row, whole, row, whole, row, whole, row, row, row,
    )
    out_specs = (
        P(seqs, "ctx", None), P(seqs, "ctx", None),
        whole, row, whole, row, whole, row, whole, row, row, row,
    )
    return jax.shard_map(body, mesh=mesh, in_specs=in_specs, out_specs=out_specs, check_vma=False)
```

```python
import functools

import jax
import jax.numpy as jnp
from jax import lax
from jax.experimental import pallas as pl
from jax.experimental.pallas import tpu as pltpu
from jax.sharding import PartitionSpec as P

MESH = pl.DeviceIdType.MESH
HEAD_DIM = 64
ROT = 16
LAYERS = 2
D = 768
FF = 3072
N = 8
TOK = 128
SEQ = 1024
HALF = 384
epsilon = 1e-05
BF = jnp.bfloat16
F32 = jnp.float32
ANY = pl.BlockSpec(memory_space=pl.ANY)


def dot(a, b, dims):
    return lax.dot_general(a, b, (dims, ((), ())), preferred_element_type=F32)


def meet(devices):
    barrier = pltpu.get_barrier_semaphore()
    for device in devices:
        pl.semaphore_signal(barrier, inc=1, device_id=device, device_id_type=MESH)
    pl.semaphore_wait(barrier, len(devices))


def push(src, dst, send, recv, device):
    copy = pltpu.make_async_remote_copy(
        src_ref=src, dst_ref=dst, send_sem=send, recv_sem=recv, device_id=device, device_id_type=MESH
    )
    copy.start()
    return copy


def others(axis, index):
    return [{axis: lax.rem(index + d, N)} for d in range(1, N)]


class Group:
    def __init__(self, axis):
        self.axis = axis
        index = lax.axis_index(axis)
        self.r, self.h = (index % 4, index // 4) if axis == "ctx" else (index // 2, index % 2)
        self.right = {axis: self.slot(1, 0)}
        self.left = {axis: self.slot(3, 0)}
        self.pair = {axis: self.slot(0, 1)}

    def slot(self, dr, dh):
        r, h = lax.rem(self.r + dr, 4), lax.rem(self.h + dh, 2)
        return h * 4 + r if self.axis == "ctx" else r * 2 + h

    def neighbours(self):
        return [self.right, self.left, self.pair]


class Lane:
    def __init__(self, sems):
        self.send, self.recv = sems
        self.copies = []

    def go(self, src, dst, device):
        i = len(self.copies)
        self.copies.append(push(src, dst, self.send.at[i], self.recv.at[i], device))
        return self.copies[-1]

    def finish(self):
        for copy in self.copies:
            copy.wait_send()


def run(*steps):
    live = list(steps)
    while live:
        for one in list(live):
            try:
                next(one)
            except StopIteration:
                live.remove(one)


GATHERS = 8


def gather_steps(lane, group, own, at, cut, rows):
    head, tail = pl.ds(0, cut), pl.ds(cut, rows - cut)
    go = lane.go
    me, twin, far = group.slot(0, 0), group.slot(0, 1), group.slot(2, 0)
    c0 = go(own, at(me), group.right)
    c1 = go(own, at(me), group.left)
    c2 = go(own, at(me), group.pair)
    yield
    c0.wait_recv()
    behind = at(group.slot(3, 0)).at[head]
    c3 = go(behind, behind, group.right)
    yield
    c1.wait_recv()
    ahead = at(group.slot(1, 0)).at[tail]
    c4 = go(ahead, ahead, group.left)
    yield
    c2.wait_recv()
    c5 = go(at(twin), at(twin), group.right)
    c6 = go(at(twin), at(twin), group.left)
    yield
    c3.wait_recv()
    yield
    c4.wait_recv()
    c7 = go(at(far), at(far), group.pair)
    for copy in (c5, c6, c7):
        yield
        copy.wait_recv()


def gather_few_steps(lane, group, own, at, cut, rows):
    head, tail = pl.ds(0, cut), pl.ds(cut, rows - cut)
    go = lane.go
    me, twin, far = group.slot(0, 0), group.slot(0, 1), group.slot(2, 0)
    c0 = go(own, at(me), group.right)
    c1 = go(own, at(me), group.left)
    c2 = go(own, at(me), group.pair)
    yield
    c0.wait_recv()
    behind = at(group.slot(3, 0)).at[head]
    c3 = go(behind, behind, group.right)
    c1.wait_recv()
    ahead = at(group.slot(1, 0)).at[tail]
    c4 = go(ahead, ahead, group.left)
    c2.wait_recv()
    c5 = go(at(twin), at(twin), group.right)
    c6 = go(at(twin), at(twin), group.left)
    yield
    c3.wait_recv()
    c4.wait_recv()
    c7 = go(at(far), at(far), group.pair)
    yield
    for copy in (c5, c6, c7):
        copy.wait_recv()


SCATTERS = 11


def scatter_scratch(rows, cut, width):
    return [
        pltpu.VMEM((rows, width), BF),
        pltpu.VMEM((rows, width), BF),
        pltpu.VMEM((cut, width), BF),
        pltpu.VMEM((rows - cut, width), BF),
        pltpu.VMEM((cut, width), BF),
        pltpu.VMEM((rows - cut, width), BF),
        pltpu.VMEM((2, rows, width), BF),
        pltpu.VMEM((2, rows, width), BF),
        pltpu.VMEM((rows, width), BF),
        pltpu.VMEM((rows, width), BF),
    ]


SCRATCHES = 10


def scatter_steps(lane, group, src, cut, rows, buffers, take):
    in_far, st_far, in_right, in_left, st_left, st_right, from_right, from_left, st_pair, from_pair = buffers
    head, tail = pl.ds(0, cut), pl.ds(cut, rows - cut)
    go = lane.go
    opposite = go(src.at[group.slot(2, 1)], in_far, group.pair)
    beside = [
        go(src.at[group.slot(3, 1)], from_right.at[0], group.left),
        go(src.at[group.slot(1, 1)], from_left.at[0], group.right),
    ]
    near = [
        go(src.at[group.slot(3, 0)].at[tail], from_right.at[1].at[tail], group.left),
        go(src.at[group.slot(1, 0)].at[head], from_left.at[1].at[head], group.right),
    ]
    yield
    opposite.wait_recv()
    st_far[...] = (src[group.slot(2, 0)].astype(F32) + in_far[...].astype(F32)).astype(BF)
    far_left = go(st_far.at[head], in_right, group.left)
    far_right = go(st_far.at[tail], in_left, group.right)
    for copy in beside:
        yield
        copy.wait_recv()
    total = src[group.slot(0, 1)].astype(F32) + from_right[0].astype(F32) + from_left[0].astype(F32)
    st_pair[...] = total.astype(BF)
    last = go(st_pair, from_pair, group.pair)
    yield
    far_left.wait_recv()
    st_left[...] = (src[group.slot(3, 0), head].astype(F32) + in_right[...].astype(F32)).astype(BF)
    near.append(go(st_left, from_right.at[1].at[head], group.left))
    yield
    far_right.wait_recv()
    st_right[...] = (src[group.slot(1, 0), tail].astype(F32) + in_left[...].astype(F32)).astype(BF)
    near.append(go(st_right, from_left.at[1].at[tail], group.right))
    for copy in near + [last]:
        yield
        copy.wait_recv()
    total = src[group.slot(0, 0)].astype(F32) + from_right[1].astype(F32) + from_left[1].astype(F32)
    take(total + from_pair[...].astype(F32))


def sems(count):
    return [pltpu.SemaphoreType.DMA((count,)), pltpu.SemaphoreType.DMA((count,))]


def params(collective_id):
    return pltpu.CompilerParams(
        collective_id=collective_id, has_side_effects=True, vmem_limit_bytes=36 * 1024 * 1024
    )


def normalize(stream):
    mean = jnp.mean(stream, axis=-1, keepdims=True)
    centred = stream - mean
    scale = lax.rsqrt(jnp.mean(centred * centred, axis=-1, keepdims=True) + epsilon)
    return centred * scale, scale


def norm_back(stream, grad_normed, gain):
    unit, scale = normalize(stream)
    grad_unit = grad_normed * gain
    first = jnp.mean(grad_unit, axis=-1, keepdims=True)
    second = jnp.mean(grad_unit * unit, axis=-1, keepdims=True)
    grad_gain = jnp.sum(grad_normed * unit, axis=0, keepdims=True)
    grad_shift = jnp.sum(grad_normed, axis=0, keepdims=True)
    return scale * (grad_unit - first - unit * second), grad_gain, grad_shift


PIECE = 64
ROWS = 96 + PIECE
CUT = 80
W_FIRST = ROWS + 16
W_CUT = 96
VMEM = pl.BlockSpec(memory_space=pltpu.VMEM)


def shard_scratch(rows):
    return [
        pltpu.VMEM((N, rows, HALF), BF),
        pltpu.VMEM((N, PIECE, HALF), BF),
        pltpu.VMEM((N, PIECE, HALF), BF),
    ]


SHARD_LANE = N - 1 + 3


def shard_steps(lane, lane_z, fsdp, cs, core, src, cut, rows, scratch, outs, own, kept, gather=gather_steps):
    held, mixed, got = scratch
    c, k = lax.axis_index("ctx"), lax.axis_index("dp")
    first = pltpu.make_async_copy(src.at[k], held.at[fsdp.slot(0, 0)], own.at[0])
    first.start()
    yield from gather(lane_z, fsdp, src.at[k], lambda slot: held.at[slot], cut, rows)
    first.wait()
    low = lax.broadcasted_iota(jnp.int32, (16, HALF), 0) < 8
    for i in range(N):
        own_rows = held[i, pl.ds(96, 16)].astype(F32)
        shared = held[i // 2 * 2 + c // 4, pl.ds(96, 16)].astype(F32)
        mixed[i, pl.ds(0, 16)] = jnp.where(low, own_rows, shared).astype(BF)
        mixed[i, pl.ds(16, 48)] = held[i, pl.ds(112, 48)]
    turn = [lane.go(mixed.at[peer["ctx"]], got.at[c], peer) for peer in cs]
    got[c] = mixed[c]
    cross = []

    def share(part, out, sem):
        cross.append(lane.go(part, out.at[k], core))
        keep = pltpu.make_async_copy(part, out.at[k], sem)
        keep.start()
        kept.append(keep)

    share(held.at[:, pl.ds(0, 96)], outs[0], own.at[1])
    if len(outs) > 2:
        share(held.at[:, pl.ds(ROWS, 16)], outs[2], own.at[2])
    for copy in turn:
        yield
        copy.wait_recv()
    share(got, outs[1], own.at[3])
    for copy in cross:
        yield
        copy.wait_recv()


COLS_SHAPE = jax.ShapeDtypeStruct((2, N, 96, HALF), BF)
PIECES_SHAPE = jax.ShapeDtypeStruct((2, N, PIECE, HALF), BF)


def weights_kernel(
    src, places, x, cols_all, pieces_all, vec_all, places_all, unit_all, *rest
):
    scratch, unit, rest = rest[:3], rest[3], rest[4:]
    lane, lane_z, lane_m, lane_u = (Lane(rest[2 * i : 2 * i + 2]) for i in range(4))
    own, keeps = rest[8], rest[9]
    c = lax.axis_index("ctx")
    fsdp, ctx = Group("fsdp"), Group("ctx")
    cs = others("ctx", c)
    core = {"dp": 1 - lax.axis_index("dp")}
    mark = pltpu.make_async_copy(places, places_all.at[c], keeps.at[0])
    mark.start()
    meet(fsdp.neighbours() + cs + [core])
    kept = [mark]
    marks = [lane_m.go(places, places_all.at[c], peer) for peer in cs]

    def tokens():
        unit[...] = normalize(x[...])[0].astype(BF)
        keep = pltpu.make_async_copy(unit, unit_all.at[c], keeps.at[1])
        keep.start()
        kept.append(keep)
        yield from gather_few_steps(lane_u, ctx, unit, lambda slot: unit_all.at[slot], TOK // 2, TOK)

    outs = (cols_all, pieces_all, vec_all)
    run(
        shard_steps(
            lane, lane_z, fsdp, cs, core, src, W_CUT, W_FIRST, scratch, outs, own, kept, gather_few_steps
        ),
        tokens(),
    )
    for copy in marks:
        copy.wait_recv()
    for each in (lane, lane_z, lane_m, lane_u):
        each.finish()
    for copy in kept:
        copy.wait()


def gather_weights(src, places, x, collective_id):
    tokens = jax.ShapeDtypeStruct((N, TOK, D), BF)
    return pl.pallas_call(
        weights_kernel,
        out_shape=(
            COLS_SHAPE,
            PIECES_SHAPE,
            jax.ShapeDtypeStruct((2, N, 16, HALF), BF),
            jax.ShapeDtypeStruct((N,) + places.shape, places.dtype),
            tokens,
        ),
        in_specs=[ANY] * 2 + [VMEM],
        out_specs=[ANY] * 5,
        scratch_shapes=shard_scratch(W_FIRST)
        + [pltpu.VMEM((TOK, D), BF)]
        + sems(SHARD_LANE)
        + sems(GATHERS)
        + sems(N - 1)
        + sems(GATHERS)
        + [pltpu.SemaphoreType.DMA((4,)), pltpu.SemaphoreType.DMA((2,))],
        compiler_params=params(collective_id),
    )(src, places, x)


def marks_of(places):
    frequency = 10000.0 ** (-2.0 * jnp.arange(ROT // 2, dtype=F32) / ROT)
    where = places.astype(F32).reshape(1, -1)
    angles = frequency[:, None] * where
    return jnp.concatenate([jnp.cos(angles), jnp.sin(angles), jnp.broadcast_to(where, angles.shape)], axis=0)


def prepare_kernel(marks, vectors, tables, col, rows_out):
    zero = jnp.zeros((8, TOK), F32)
    one = zero + 1.0
    for i in range(N):
        cosine, sine, where = marks[i, 0:8], marks[i, 8:16], marks[i, 16:24]
        rows = pl.ds(i * TOK, TOK)
        own = [cosine, cosine] + [one] * 6
        left = [zero, sine] + [zero] * 6
        right = [-sine, zero] + [zero] * 6
        for t, tiles in enumerate((own, left, right)):
            tables[t, rows] = jnp.concatenate(tiles + tiles, axis=0).T
        col[rows] = jnp.concatenate([where] * 16, axis=0).T

    c = lax.axis_index("ctx")
    head_a, head_b = 3 * (c // 2) + 2 * (c % 2), 3 * (c // 2) + 1

    def place(values, column, width, cut):
        shard = jnp.zeros((1, width), jnp.int32)
        for t in range(1, N):
            shard = shard + jnp.where(column >= cut * t, 1, 0)
        inner = column - cut * shard
        pick = lax.broadcasted_iota(jnp.int32, (HALF, width), 0) == inner
        spread_ = dot(values.astype(BF), jnp.where(pick, 1.0, 0.0).astype(BF), ((1,), (0,)))
        mine = lax.broadcasted_iota(jnp.int32, (N, width), 0) == shard
        return jnp.sum(jnp.where(mine, spread_, 0.0), axis=0, keepdims=True)

    lanes = lax.broadcasted_iota(jnp.int32, (1, D), 1)
    lane = lax.broadcasted_iota(jnp.int32, (1, HALF), 1)
    third = jnp.where(lane >= 128, 1, 0) + jnp.where(lane >= 256, 1, 0)
    within = lane - 128 * third
    second = jnp.where(within >= HEAD_DIM, 1, 0)
    head = jnp.where(second == 1, head_b, head_a)
    column = 192 * head + HEAD_DIM * third + (within - HEAD_DIM * second)
    for layer in range(LAYERS):
        shards = [vectors[layer, i].astype(F32) for i in range(N)]

        def row(r):
            return jnp.concatenate([one_shard[r : r + 1] for one_shard in shards], axis=0)

        rows_out[layer, 0:1] = place(row(2), lanes, D, 96)
        rows_out[layer, 1:2] = place(row(3), lanes, D, 96)
        rows_out[layer, 2:3] = place(row(4), lanes, D, 96) + place(row(5), lanes, D, 96)
        rows_out[layer, 3:4, pl.ds(0, HALF)] = place(row(0), column, HALF, 288)
        rows_out[layer, 3:4, pl.ds(HALF, HALF)] = vectors[layer, c].astype(F32)[1:2]
        rows_out[layer, 4:8] = jnp.zeros((4, D), F32)


def prepare(marks, vectors):
    return pl.pallas_call(
        prepare_kernel,
        out_shape=(
            jax.ShapeDtypeStruct((3, SEQ, 128), F32),
            jax.ShapeDtypeStruct((SEQ, 128), F32),
            jax.ShapeDtypeStruct((LAYERS, 8, D), F32),
        ),
        in_specs=[VMEM] * 2,
        out_specs=[VMEM] * 3,
        compiler_params=pltpu.CompilerParams(vmem_limit_bytes=48 * 1024 * 1024),
    )(marks, vectors)


BLOCK = 256
BLOCKS = SEQ // BLOCK


def unit_rows(b):
    s = lax.axis_index("ctx") % 2
    start = jnp.where(b < BLOCKS, b * BLOCK, s * (SEQ // 2) + (b - BLOCKS) * BLOCK)
    start = pl.multiple_of(start, BLOCK)
    lanes = lax.broadcasted_iota(jnp.int32, (BLOCK, 2 * HEAD_DIM), 1) // HEAD_DIM
    return start, lanes == jnp.where(b < BLOCKS, 0, 1)


def mix_rows(pieces, w_mix):
    for h in range(2):
        cols = pl.ds(HALF * h, HALF)
        rows = [pieces[h, j, pl.ds(0, 16)].astype(F32) for j in range(N)]
        heads = [r[:8] for r in rows] + [r[8:] for r in rows]
        w_mix[pl.ds(0, 128), cols] = jnp.concatenate(heads, axis=0).astype(BF)
        for j in range(N):
            w_mix[pl.ds(128 + 48 * j, 48), cols] = pieces[h, j, pl.ds(16, 48)]


def forward_steps(
    unit, vectors, w_cat, pieces, col, row, tables,
    branch, normed, query, key, value, slope, mixed, lse, w_mix, turned,
):
    mix_rows(pieces, w_mix)

    @pl.loop(0, BLOCKS)
    def _(i):
        rows = pl.ds(pl.multiple_of(i * BLOCK, BLOCK), BLOCK)
        low = (unit[rows].astype(F32) * vectors[0:1] + vectors[1:2]).astype(BF)
        normed[rows] = low
        heads = dot(low, w_cat[0], ((1,), (0,))) + vectors[3:4, :HALF]

        def rotate(values):
            return (
                values * tables[0, rows]
                + pltpu.roll(values, 8, axis=1) * tables[1, rows]
                + pltpu.roll(values, 120, axis=1) * tables[2, rows]
            )

        query[rows] = (rotate(heads[:, :128]) * HEAD_DIM ** (-0.5)).astype(BF)
        key[rows] = rotate(heads[:, 128:256]).astype(BF)
        value[rows] = heads[:, 256:].astype(BF)
        pre = dot(low, w_cat[1], ((1,), (0,))) + vectors[3:4, HALF:]
        cdf = 0.5 * (1.0 + lax.erf(pre * 0.5**0.5))
        mixed[rows, pl.ds(128, HALF)] = (pre * cdf).astype(BF)
        mixed[rows, pl.ds(0, 128)] = jnp.zeros((BLOCK, 128), BF)
        slope[rows] = cdf + pre * (jnp.exp(-0.5 * pre * pre) * 0.3989422804014327)

    turned[...] = value[...].astype(F32).T.astype(BF)
    yield
    for n in range(3):

        @pl.loop(2 * n, 2 * n + 2)
        def _(b):
            start, mask = unit_rows(b)
            rows = pl.ds(start, BLOCK)
            q = jnp.where(mask, query[rows].astype(F32), 0.0).astype(BF)
            scores = dot(key[...], q, ((1,), (1,)))
            seen = jnp.concatenate([col[...], col[...]], axis=1) <= row[pl.ds(start // BLOCK, 1)]
            scores = jnp.where(seen, scores, -jnp.inf)
            top = jnp.max(scores, axis=0, keepdims=True)
            expos = jnp.exp(scores - top)
            total = jnp.sum(expos, axis=0, keepdims=True)
            lse[pl.ds(b, 1)] = top + jnp.log(total)
            probs = (expos * (1.0 / total)).astype(BF)
            out = dot(turned[...], probs, ((1,), (0,))).T
            mixed[rows, pl.ds(0, 128)] = jnp.where(mask, out, mixed[rows, pl.ds(0, 128)].astype(F32)).astype(BF)

        yield
    for i in range(N):
        rows = pl.ds(i * TOK, TOK)
        branch[i] = dot(mixed[rows], w_mix[...], ((1,), (0,))).astype(BF)


def unit_rows_of(b):
    s = lax.axis_index("ctx") % 2
    lanes = lax.broadcasted_iota(jnp.int32, (BLOCK, 2 * HEAD_DIM), 1)
    if b < BLOCKS:
        return b * BLOCK, lanes < HEAD_DIM
    return pl.multiple_of(s * (SEQ // 2) + (b - BLOCKS) * BLOCK, BLOCK), lanes >= HEAD_DIM


def forward_unrolled(
    unit, vectors, w_cat, pieces, col, row, tables,
    branch, normed, query, key, value, slope, mixed, lse, w_mix, turned,
):
    mix_rows(pieces, w_mix)
    for i in range(BLOCKS):
        rows = pl.ds(i * BLOCK, BLOCK)
        low = (unit[rows].astype(F32) * vectors[0:1] + vectors[1:2]).astype(BF)
        normed[rows] = low
        heads = dot(low, w_cat[0], ((1,), (0,))) + vectors[3:4, :HALF]

        def rotate(values, rows=rows):
            return (
                values * tables[0, rows]
                + pltpu.roll(values, 8, axis=1) * tables[1, rows]
                + pltpu.roll(values, 120, axis=1) * tables[2, rows]
            )

        query[rows] = (rotate(heads[:, :128]) * HEAD_DIM ** (-0.5)).astype(BF)
        key[rows] = rotate(heads[:, 128:256]).astype(BF)
        value[rows] = heads[:, 256:].astype(BF)
        pre = dot(low, w_cat[1], ((1,), (0,))) + vectors[3:4, HALF:]
        cdf = 0.5 * (1.0 + lax.erf(pre * 0.5**0.5))
        mixed[rows, pl.ds(128, HALF)] = (pre * cdf).astype(BF)
        mixed[rows, pl.ds(0, 128)] = jnp.zeros((BLOCK, 128), BF)
        slope[rows] = cdf + pre * (jnp.exp(-0.5 * pre * pre) * 0.3989422804014327)
        yield

    turned[...] = value[...].astype(F32).T.astype(BF)
    for b in range(BLOCKS + 2):
        start, mask = unit_rows_of(b)
        rows = pl.ds(start, BLOCK)
        q = jnp.where(mask, query[rows].astype(F32), 0.0).astype(BF)
        scores = dot(key[...], q, ((1,), (1,)))
        seen = jnp.concatenate([col[...], col[...]], axis=1) <= row[pl.ds(start // BLOCK, 1)]
        scores = jnp.where(seen, scores, -jnp.inf)
        top = jnp.max(scores, axis=0, keepdims=True)
        expos = jnp.exp(scores - top)
        total = jnp.sum(expos, axis=0, keepdims=True)
        lse[pl.ds(b, 1)] = top + jnp.log(total)
        probs = (expos * (1.0 / total)).astype(BF)
        out = dot(turned[...], probs, ((1,), (0,))).T
        mixed[rows, pl.ds(0, 128)] = jnp.where(mask, out, mixed[rows, pl.ds(0, 128)].astype(F32)).astype(BF)
        yield
    for i in range(BLOCKS):
        rows = pl.ds(i * BLOCK, BLOCK)
        out = dot(mixed[rows], w_mix[...], ((1,), (0,))).astype(BF)
        branch[2 * i] = out[:TOK]
        branch[2 * i + 1] = out[TOK:]
        yield


def forward_shapes():
    shape = jax.ShapeDtypeStruct
    return (
        shape((N, TOK, D), BF),
        shape((SEQ, D), BF),
        shape((SEQ, 128), BF),
        shape((SEQ, 128), BF),
        shape((SEQ, 128), BF),
        shape((SEQ, HALF), F32),
        shape((SEQ, 512), BF),
        shape((8, BLOCK), F32),
        shape((512, D), BF),
    )


FORWARDS = 9


def local_params():
    return pltpu.CompilerParams(vmem_limit_bytes=36 * 1024 * 1024)


def forward_kernel(*refs):
    run(forward_unrolled(*refs))


def forward(*args):
    return pl.pallas_call(
        forward_kernel,
        out_shape=forward_shapes(),
        in_specs=[VMEM] * len(args),
        out_specs=[VMEM] * FORWARDS,
        scratch_shapes=[pltpu.VMEM((128, SEQ), BF)],
        compiler_params=local_params(),
    )(*args)


def forward_between_kernel(*refs):
    args, (x, cot, src), refs = refs[:7], refs[7:10], refs[10:]
    outs, refs = refs[:FORWARDS], refs[FORWARDS:]
    (x_next, unit_all, low_all, cols_all, pieces_all), refs = refs[:5], refs[5:]
    turned, unit, low_g, scratch, rest = refs[0], refs[1], refs[2], refs[3:6], refs[6:]
    buffers, rest = rest[:SCRATCHES], rest[SCRATCHES:]
    lane, lane_u, lane_g, lane_w, lane_z = (Lane(rest[2 * i : 2 * i + 2]) for i in range(5))
    own, keeps = rest[10], rest[11]
    ctx, fsdp = Group("ctx"), Group("fsdp")
    cs = others("ctx", lax.axis_index("ctx"))
    core = {"dp": 1 - lax.axis_index("dp")}
    meet(fsdp.neighbours() + cs + [core])
    kept = []
    branch, vectors = outs[0], args[1]

    def tokens():
        yield from forward_steps(*args, *outs, turned)

        def take(total):
            x_next[...] = x[...] + (total + vectors[2:3])

        yield from scatter_steps(lane, ctx, branch, TOK // 2, TOK, buffers, take)
        unit[...] = normalize(x_next[...])[0].astype(BF)
        keep = pltpu.make_async_copy(unit, unit_all.at[ctx.slot(0, 0)], keeps.at[0])
        keep.start()
        kept.append(keep)
        yield from gather_few_steps(lane_u, ctx, unit, lambda slot: unit_all.at[slot], TOK // 2, TOK)

    def later():
        low_g[...] = cot[...].astype(BF)
        keep = pltpu.make_async_copy(low_g, low_all.at[ctx.slot(0, 0)], keeps.at[1])
        keep.start()
        kept.append(keep)
        yield from gather_few_steps(lane_g, ctx, low_g, lambda slot: low_all.at[slot], TOK // 2, TOK)

    outs_w = (cols_all, pieces_all)
    run(
        shard_steps(lane_w, lane_z, fsdp, cs, core, src, CUT, ROWS, scratch, outs_w, own, kept, gather_few_steps),
        later(),
        tokens(),
    )
    for each in (lane, lane_u, lane_g, lane_w, lane_z):
        each.finish()
    for copy in kept:
        copy.wait()


def forward_between(args, x, cot, src, collective_id):
    tokens = jax.ShapeDtypeStruct((N, TOK, D), BF)
    return pl.pallas_call(
        forward_between_kernel,
        out_shape=forward_shapes()
        + (jax.ShapeDtypeStruct((TOK, D), F32), tokens, tokens, COLS_SHAPE, PIECES_SHAPE),
        in_specs=[VMEM] * 9 + [ANY],
        out_specs=[VMEM] * (FORWARDS + 1) + [ANY] * 4,
        scratch_shapes=[
            pltpu.VMEM((128, SEQ), BF),
            pltpu.VMEM((TOK, D), BF),
            pltpu.VMEM((TOK, D), BF),
        ]
        + shard_scratch(ROWS)
        + scatter_scratch(TOK, TOK // 2, D)
        + sems(SCATTERS)
        + sems(GATHERS)
        + sems(GATHERS)
        + sems(SHARD_LANE)
        + sems(GATHERS)
        + [pltpu.SemaphoreType.DMA((4,)), pltpu.SemaphoreType.DMA((2,))],
        compiler_params=params(collective_id),
    )(*args, x, cot, src)


BACK_ARGS = 12


def backward_scratch():
    return [
        pltpu.VMEM((SEQ, 128), BF),
        pltpu.VMEM((SEQ, D), BF),
        pltpu.VMEM((SEQ, 128), F32),
        pltpu.VMEM((SEQ, 128), F32),
        pltpu.VMEM((SEQ, 128), F32),
        pltpu.VMEM((128, SEQ), BF),
        pltpu.VMEM((D, D), F32),
        pltpu.VMEM((N, TOK, D), BF),
        pltpu.VMEM((2, N, 96, HALF), BF),
        pltpu.VMEM((2, N, PIECE, HALF), BF),
    ]


BACKS = 10


def backward_steps(
    ready, low, w_cat, normed, query, key, value, slope, mixed, lse, w_mix, col, row, tables, grad_b,
    grad_att, grad_pre, dq, dk, dv, turned, big, grad_normed, part_a, part_b,
):
    @pl.loop(0, 2)
    def _(i):
        cols = pl.ds(pl.multiple_of(i * BLOCK, BLOCK), BLOCK)
        big[cols] = dot(mixed[:, cols], low[...], ((0,), (0,)))

    for j in range(N):
        for h in range(2):
            at = slice(HALF * h, HALF * h + HALF)
            first = big[8 * j : 8 * j + 8, at]
            second = big[64 + 8 * j : 64 + 8 * j + 8, at]
            part_b[h, j, pl.ds(0, 16)] = jnp.concatenate([first, second], axis=0).astype(BF)
            part_b[h, j, pl.ds(16, 48)] = big[128 + 48 * j : 176 + 48 * j, at].astype(BF)
    ready.add("b")
    yield

    @pl.loop(0, BLOCKS)
    def _(i):
        rows = pl.ds(pl.multiple_of(i * BLOCK, BLOCK), BLOCK)
        back = dot(low[rows], w_mix[...], ((1,), (1,)))
        grad_att[rows] = back[:, :128].astype(BF)
        grad_pre[rows, pl.ds(HALF, HALF)] = (back[:, 128:] * slope[rows]).astype(BF)

    turned[...] = key[...].astype(F32).T.astype(BF)
    dq[...] = jnp.zeros((SEQ, 128), F32)
    dk[...] = jnp.zeros((SEQ, 128), F32)
    dv[...] = jnp.zeros((SEQ, 128), F32)
    yield
    for n in range(3):

        @pl.loop(2 * n, 2 * n + 2)
        def _(b):
            start, mask = unit_rows(b)
            rows = pl.ds(start, BLOCK)
            q = jnp.where(mask, query[rows].astype(F32), 0.0).astype(BF)
            g = jnp.where(mask, grad_att[rows].astype(F32), 0.0).astype(BF)
            scores = dot(key[...], q, ((1,), (1,)))
            seen = jnp.concatenate([col[...], col[...]], axis=1) <= row[pl.ds(start // BLOCK, 1)]
            probs = jnp.exp(jnp.where(seen, scores, -jnp.inf) - lse[pl.ds(b, 1)])
            grad_probs = dot(value[...], g, ((1,), (1,)))
            mean = jnp.sum(probs * grad_probs, axis=0, keepdims=True)
            grad_scores = (probs * (grad_probs - mean)).astype(BF)
            dq[rows] = jnp.where(mask, dot(turned[...], grad_scores, ((1,), (0,))).T, dq[rows])
            dk[...] += dot(grad_scores, q, ((1,), (0,)))
            dv[...] += dot(probs.astype(BF), g, ((1,), (0,)))

        yield
    grad_b[...] = jnp.zeros((1, D), F32)

    @pl.loop(0, N)
    def _(i):
        rows = pl.ds(pl.multiple_of(i * TOK, TOK), TOK)

        def rotate_back(grads):
            return (
                grads * tables[0, rows]
                + pltpu.roll(grads * tables[1, rows], 120, axis=1)
                + pltpu.roll(grads * tables[2, rows], 8, axis=1)
            )

        grad_pre[rows, pl.ds(0, 128)] = rotate_back(dq[rows] * HEAD_DIM ** (-0.5)).astype(BF)
        grad_pre[rows, pl.ds(128, 128)] = rotate_back(dk[rows]).astype(BF)
        grad_pre[rows, pl.ds(256, 128)] = dv[rows].astype(BF)
        block = grad_pre[rows]
        grad_b[...] += jnp.sum(block.astype(F32), axis=0, keepdims=True)
        grad_normed[i] = (
            dot(block[:, :HALF], w_cat[0], ((1,), (1,))) + dot(block[:, HALF:], w_cat[1], ((1,), (1,)))
        ).astype(BF)

    ready.add("normed")
    yield

    @pl.loop(0, D // BLOCK)
    def _(i):
        cols = pl.ds(pl.multiple_of(i * BLOCK, BLOCK), BLOCK)
        big[cols] = dot(normed[:, cols], grad_pre[...], ((0,), (0,)))

    for f in range(N):
        for h in range(2):
            part_a[h, f] = big[96 * f : 96 * f + 96, HALF * h : HALF * h + HALF].astype(BF)
    ready.add("a")


def grads_scratch():
    return [
        pltpu.VMEM((N, 96, HALF), BF),
        pltpu.VMEM((N, PIECE, HALF), BF),
        pltpu.VMEM((N, PIECE, HALF), BF),
        pltpu.VMEM((N, ROWS, HALF), BF),
    ] + scatter_scratch(ROWS, CUT, HALF)


GRADS = 4 + SCRATCHES


def grads_steps(ready, lane, lane_z, fsdp, cs, core, part_a, part_b, scratch, take):
    their_a, their_b, got, blocks = scratch[:4]
    c, k = lax.axis_index("ctx"), lax.axis_index("dp")
    while "b" not in ready:
        yield
    first_b = lane.go(part_b.at[1 - k], their_b, core)
    yield
    first_b.wait_recv()
    for i in range(N):
        their_b[i] = (part_b[k, i].astype(F32) + their_b[i].astype(F32)).astype(BF)
    turn = [lane.go(their_b.at[peer["ctx"]], got.at[c], peer) for peer in cs]
    got[c] = their_b[c]
    while "a" not in ready:
        yield
    first_a = lane.go(part_a.at[1 - k], their_a, core)
    for copy in turn:
        copy.wait_recv()
    low = lax.broadcasted_iota(jnp.int32, (16, HALF), 0) < 8
    for i in range(N):
        rows = got[i, pl.ds(0, 16)].astype(F32)
        pair = got[i + 1 - 2 * (i % 2), pl.ds(0, 16)].astype(F32)
        blocks[i, pl.ds(96, 16)] = jnp.where(low, rows, rows + pair).astype(BF)
        blocks[i, pl.ds(112, 48)] = got[i, pl.ds(16, 48)]
    yield
    first_a.wait_recv()
    for i in range(N):
        blocks[i, pl.ds(0, 96)] = (part_a[k, i].astype(F32) + their_a[i].astype(F32)).astype(BF)
    yield from scatter_steps(lane_z, fsdp, blocks, CUT, ROWS, scratch[4:], take)


def turn_kernel(*refs):
    (low, *args), refs = refs[:13], refs[13:]
    (x, grad, vectors, out_parts, bias), refs = refs[:5], refs[5:]
    (outputs, grad_next, low_all, vecs, share), refs = refs[:5], refs[5:]
    (low_g, grad_b), refs = refs[:2], refs[2:]
    back, refs = refs[:BACKS], refs[BACKS:]
    buffers, refs = refs[:SCRATCHES], refs[SCRATCHES:]
    buffers_o, refs = refs[:SCRATCHES], refs[SCRATCHES:]
    scratch, rest = refs[:GRADS], refs[GRADS:]
    lane, lane_g, lane_w, lane_z, lane_o = (Lane(rest[2 * i : 2 * i + 2]) for i in range(5))
    keep_sem = rest[10]
    ctx, fsdp = Group("ctx"), Group("fsdp")
    cs = others("ctx", lax.axis_index("ctx"))
    core = {"dp": 1 - lax.axis_index("dp")}
    meet(cs + fsdp.neighbours() + [core])
    kept, ready = [], set()

    def tokens():
        def take(total):
            back_, grad_gain, grad_shift = norm_back(x[...], total, vectors[0:1])
            grad_next[...] = grad[...] + back_
            rounded = grad[...].astype(BF).astype(F32)
            vecs[pl.ds(0, 1)] = jnp.sum(rounded, axis=0, keepdims=True)
            vecs[pl.ds(1, 1)] = grad_gain
            vecs[pl.ds(2, 1)] = grad_shift
            vecs[pl.ds(3, 1)] = grad_b[...]
            vecs[pl.ds(4, 4)] = jnp.zeros((4, D), F32)

        while "normed" not in ready:
            yield
        yield from scatter_steps(lane, ctx, back[7], TOK // 2, TOK, buffers, take)
        low_g[...] = grad_next[...].astype(BF)
        keep = pltpu.make_async_copy(low_g, low_all.at[ctx.slot(0, 0)], keep_sem)
        keep.start()
        kept.append(keep)
        yield from gather_few_steps(lane_g, ctx, low_g, lambda slot: low_all.at[slot], TOK // 2, TOK)

    def weights():
        def take(total):
            share[...] = total.astype(BF)

        yield from grads_steps(ready, lane_w, lane_z, fsdp, cs, core, back[8], back[9], scratch, take)

    def ends():
        def take(total):
            outputs[...] = x[...] + (total + bias[2:3])

        yield from scatter_steps(lane_o, ctx, out_parts, TOK // 2, TOK, buffers_o, take)

    run(ends(), backward_steps(ready, low, *args, grad_b, *back), tokens(), weights())
    for each in (lane, lane_g, lane_w, lane_z, lane_o):
        each.finish()
    for copy in kept:
        copy.wait()


def turn(args, x, grad, vectors, out_parts, collective_id):
    tokens = jax.ShapeDtypeStruct((TOK, D), F32)
    return pl.pallas_call(
        turn_kernel,
        out_shape=(
            tokens,
            tokens,
            jax.ShapeDtypeStruct((N, TOK, D), BF),
            jax.ShapeDtypeStruct((8, D), F32),
            jax.ShapeDtypeStruct((ROWS, HALF), BF),
        ),
        in_specs=[VMEM] * 18,
        out_specs=(VMEM, VMEM, ANY, VMEM, VMEM),
        scratch_shapes=[pltpu.VMEM((TOK, D), BF), pltpu.VMEM((1, D), F32)]
        + backward_scratch()
        + scatter_scratch(TOK, TOK // 2, D)
        + scatter_scratch(TOK, TOK // 2, D)
        + grads_scratch()
        + sems(SCATTERS)
        + sems(GATHERS)
        + sems(2 + N - 1)
        + sems(SCATTERS)
        + sems(SCATTERS)
        + [pltpu.SemaphoreType.DMA],
        compiler_params=params(collective_id),
    )(*args, x, grad, vectors, out_parts, vectors)


FIRST_ROWS = ROWS + 16


def last_kernel(*refs):
    (low, *args), refs = refs[:13], refs[13:]
    (x, grad, vectors, vecs, share), refs = refs[:5], refs[5:]
    (grad_next, out_first, out_last), refs = refs[:3], refs[3:]
    (both, v_mine, v_their, v_all, grad_b), refs = refs[:5], refs[5:]
    back, refs = refs[:BACKS], refs[BACKS:]
    buffers, refs = refs[:SCRATCHES], refs[SCRATCHES:]
    scratch, rest = refs[:GRADS], refs[GRADS:]
    lane, lane_w, lane_z, lane_v, lane_x, lane_s = (Lane(rest[2 * i : 2 * i + 2]) for i in range(6))
    keeps = rest[12]
    c, f, k = lax.axis_index("ctx"), lax.axis_index("fsdp"), lax.axis_index("dp")
    ctx, fsdp = Group("ctx"), Group("fsdp")
    cs, fs = others("ctx", c), others("fsdp", f)
    core = {"dp": 1 - k}
    meet(cs + fs + [core])
    ready = set()

    def tokens():
        def take(total):
            back_, grad_gain, grad_shift = norm_back(x[...], total, vectors[0:1])
            grad_next[...] = grad[...] + back_
            rounded = grad[...].astype(BF).astype(F32)
            branch = jnp.sum(rounded, axis=0, keepdims=True)
            mine = [vecs[...], branch, grad_gain, grad_shift, grad_b[...], jnp.zeros((4, D), F32)]
            mine = jnp.concatenate(mine, axis=0)
            v_mine[0] = mine[:, :HALF].astype(BF)
            v_mine[1] = mine[:, HALF:].astype(BF)

        while "normed" not in ready:
            yield
        yield from scatter_steps(lane, ctx, back[7], TOK // 2, TOK, buffers, take)
        cross = lane_v.go(v_mine.at[1 - k], v_their, core)
        yield
        cross.wait_recv()
        v_all[f] = (v_mine[k].astype(F32) + v_their[...].astype(F32)).astype(BF)
        copies = [lane_v.go(v_all.at[f], v_all.at[f], peer) for peer in fs]
        yield
        for copy in copies:
            copy.wait_recv()
        total = v_all[0].astype(F32)
        for i in range(1, N):
            total = total + v_all[i].astype(F32)
        both[pl.ds(ROWS, 16)] = total.astype(BF)

    def weights():
        def take(total):
            both[pl.ds(0, ROWS)] = total.astype(BF)

        yield from grads_steps(ready, lane_w, lane_z, fsdp, cs, core, back[8], back[9], scratch, take)

    kept = []

    def older():
        keep = pltpu.make_async_copy(share, out_last.at[k, c], keeps.at[0])
        keep.start()
        kept.append(keep)
        yield from gather_steps(lane_s, ctx, share, lambda slot: out_last.at[k, slot], CUT, ROWS)
        keep.wait()
        copy = lane_s.go(out_last.at[k], out_last.at[k], core)
        yield
        copy.wait_recv()

    run(older(), backward_steps(ready, low, *args, grad_b, *back), tokens(), weights())
    keep = pltpu.make_async_copy(both, out_first.at[k, c], keeps.at[1])
    keep.start()
    run(gather_steps(lane_x, ctx, both, lambda slot: out_first.at[k, slot], W_CUT, FIRST_ROWS))
    keep.wait()
    lane_x.go(out_first.at[k], out_first.at[k], core).wait_recv()
    for each in (lane, lane_w, lane_z, lane_v, lane_x, lane_s):
        each.finish()


def last(args, x, grad, vectors, vecs, share, collective_id):
    return pl.pallas_call(
        last_kernel,
        out_shape=(
            jax.ShapeDtypeStruct((TOK, D), F32),
            jax.ShapeDtypeStruct((2, N, FIRST_ROWS, HALF), BF),
            jax.ShapeDtypeStruct((2, N, ROWS, HALF), BF),
        ),
        in_specs=[VMEM] * 18,
        out_specs=(VMEM, ANY, ANY),
        scratch_shapes=[
            pltpu.VMEM((FIRST_ROWS, HALF), BF),
            pltpu.VMEM((2, 16, HALF), BF),
            pltpu.VMEM((16, HALF), BF),
            pltpu.VMEM((N, 16, HALF), BF),
            pltpu.VMEM((1, D), F32),
        ]
        + backward_scratch()
        + scatter_scratch(TOK, TOK // 2, D)
        + grads_scratch()
        + sems(SCATTERS)
        + sems(2 + N - 1)
        + sems(SCATTERS)
        + sems(N)
        + sems(GATHERS + 1)
        + sems(GATHERS + 1)
        + [pltpu.SemaphoreType.DMA((2,))],
        compiler_params=params(collective_id),
    )(*args, x, grad, vectors, vecs, share)


def spread_kernel(got_first, got_last, g_qkv, g_out, g_up, g_down):
    odd = lax.axis_index("fsdp") % 2
    for layer in range(LAYERS):
        got, base = (got_first, got_last)[layer], 0

        def heads(i, got=got, base=base):
            return got[0, i, pl.ds(base, 96)].astype(F32)

        chunks = []
        for p in range(4):
            one, two = heads(2 * p), heads(2 * p + 1)
            both = one + two
            for values, lane in ((one, 0), (both, HEAD_DIM), (two, 0)):
                chunks += [values[:, 128 * i + lane : 128 * i + lane + HEAD_DIM] for i in range(3)]
        for i in range(len(chunks) // 2):
            g_qkv[layer, :, pl.ds(128 * i, 128)] = jnp.concatenate(chunks[2 * i : 2 * i + 2], axis=1)
        for i in range(N):
            g_up[layer, :, pl.ds(HALF * i, HALF)] = got[1, i, pl.ds(base, 96)].astype(F32)
            for h in range(2):
                cols = pl.ds(HALF * h, HALF)
                g_down[layer, pl.ds(48 * i, 48), cols] = got[h, i, pl.ds(base + 112, 48)].astype(F32)
        for h in range(2):
            cols = pl.ds(HALF * h, HALF)
            rows = [got[h, i, pl.ds(base + 96, 16)].astype(F32) for i in range(N)]
            first = [r[:8] for r in rows]
            even = jnp.concatenate(first + [r[8:] for r in rows[:4]], axis=0)
            uneven = jnp.concatenate([r[8:] for r in rows[4:]] + first, axis=0)
            g_out[layer, :, cols] = jnp.where(odd == 0, even, uneven)


def spread(got_first, got_last):
    shape = jax.ShapeDtypeStruct
    return pl.pallas_call(
        spread_kernel,
        out_shape=(
            shape((LAYERS, 96, 3 * D), F32),
            shape((LAYERS, 96, D), F32),
            shape((LAYERS, 96, FF), F32),
            shape((LAYERS, HALF, D), F32),
        ),
        in_specs=[VMEM] * 2,
        out_specs=[VMEM] * 4,
        compiler_params=local_params(),
    )(got_first, got_last)


def body(
    inputs, positions, cotangent, w_qkv, b_qkv, w_out, b_out, w_up, b_up, w_down, b_down, ln_gain, ln_bias
):
    c = lax.axis_index("ctx")
    p, s = c // 2, lax.rem(c, 2)
    head_a, head_b = 3 * p + 2 * s, 3 * p + 1

    def heads_cols(w):
        grouped = w.reshape(w.shape[:-1] + (12, 3, HEAD_DIM))
        axis = grouped.ndim - 3
        both = jnp.concatenate(
            [
                lax.dynamic_slice_in_dim(grouped, head_a, 1, axis=axis),
                lax.dynamic_slice_in_dim(grouped, head_b, 1, axis=axis),
            ],
            axis=axis,
        )
        return jnp.swapaxes(both, axis, axis + 1).reshape(w.shape[:-1] + (HALF,))

    def hidden_cols(w):
        return lax.dynamic_slice_in_dim(w, c * HALF, HALF, axis=w.ndim - 1)

    f = lax.axis_index("fsdp")
    f_s = lax.rem(f, 2)

    def piece(w, start, count):
        return lax.dynamic_slice_in_dim(w, start, count, axis=1)

    cols = jnp.concatenate([heads_cols(w_qkv), hidden_cols(w_up)], axis=-1)
    first_rows = piece(w_out, jnp.where(f_s == 0, 0, 32) + 8 * c, 8)
    shared_rows = piece(w_out, jnp.where(f_s == 0, 64, -32) + 8 * jnp.where(f_s == 0, c % 4, c), 8)
    down_rows = piece(w_down, 48 * c, 48)
    by_layer = jnp.concatenate([cols, first_rows, shared_rows, down_rows], axis=1)
    def wide(vector):
        return jnp.pad(vector, ((0, 0), (0, HALF - vector.shape[1])))

    vec = jnp.stack([wide(v) for v in (b_qkv, b_up, ln_gain, ln_bias, b_out, b_down)], axis=1)
    vec = jnp.pad(vec, ((0, 0), (0, 10), (0, 0)))
    src = [jnp.stack([one[:, :HALF], one[:, HALF:]]) for one in (by_layer[0], by_layer[1])]
    src[0] = jnp.concatenate([src[0], vec], axis=1)
    stream, cot = inputs[0], cotangent[0]
    cols, pieces, vec_all, marks, unit = gather_weights(src[0], marks_of(positions), stream, 1)
    tables, col, vectors = prepare(marks, vec_all)
    row = marks[:, 16].reshape(BLOCKS, BLOCK)
    w_first = cols.reshape(2, D, HALF)
    branch, *kept_first, x_last, unit, low_last, cols, pieces_last = forward_between(
        (unit.reshape(SEQ, D), vectors[0], w_first, pieces, col, row, tables), stream, cot, src[1], 2
    )
    w_last = cols.reshape(2, D, HALF)
    branch, *kept_last = forward(
        unit.reshape(SEQ, D), vectors[1], w_last, pieces_last, col, row, tables
    )
    outputs, grad, low, vecs, share = turn(
        (low_last.reshape(SEQ, D), w_last, *kept_last, col, row, tables), x_last, cot, vectors[1], branch, 3
    )
    grad, got_first, got_last = last(
        (low.reshape(SEQ, D), w_first, *kept_first, col, row, tables), stream, grad, vectors[0], vecs, share, 4
    )
    g_qkv, g_out, g_up, g_down = spread(got_first, got_last)

    rows = jnp.concatenate([got_first[0, :, ROWS:], got_first[1, :, ROWS:]], axis=-1).astype(F32)
    summed = jnp.sum(rows, axis=0)

    def cut(vector, width):
        return lax.dynamic_slice_in_dim(vector, f * width, width, axis=vector.ndim - 1)

    def own_vectors(biases):
        qkv = biases[:, :HALF].reshape(4, 2, 3, 2, HEAD_DIM)
        shared = qkv[:, 0, :, 1] + qkv[:, 1, :, 1]
        qkv = jnp.stack([qkv[:, 0, :, 0], shared, qkv[:, 1, :, 0]], axis=1).reshape(3 * D)
        up = lax.dynamic_index_in_dim(biases[:, HALF:], f, axis=0, keepdims=False)
        return cut(qkv, 288), up

    pairs = [own_vectors(rows[:, 11]), own_vectors(rows[:, 3])]
    g_b_qkv = jnp.stack([pair[0] for pair in pairs])
    g_b_up = jnp.stack([pair[1] for pair in pairs])
    g_branch, g_gain, g_shift = (cut(jnp.stack([summed[8 + i], summed[i]]), 96) for i in range(3))
    return (
        outputs[None], grad[None], g_qkv, g_b_qkv, g_out, g_branch, g_up, g_b_up, g_down, g_branch, g_gain, g_shift,
    )


def solution(mesh):
    seqs = ("dp", "fsdp")
    whole = P(None, "fsdp", None)
    row = P(None, "fsdp")
    in_specs = (
        P(seqs, "ctx", None), P(seqs, "ctx"), P(seqs, "ctx", None),
        whole, row, whole, row, whole, row, whole, row, row, row,
    )
    out_specs = (
        P(seqs, "ctx", None), P(seqs, "ctx", None),
        whole, row, whole, row, whole, row, whole, row, row, row,
    )
    return jax.shard_map(body, mesh=mesh, in_specs=in_specs, out_specs=out_specs, check_vma=False)
```
